32 devices in a mesh: ctx: 8 (over y, x, core), exp: 4 (over z).
Axes of the slice: x: 2, y: 2, z: 4, core: 2. Of those that a mesh axis runs over, the one named last changes fastest.
Arguments:
- queries: bfloat16 [512, 8192], P('ctx', 'exp'), may hold values from -52 to 52
- cache_keys: bfloat16 [1024, 512], P('ctx'), may hold values from -6 to 6
- cache_values: bfloat16 [1024, 512], P('ctx'), may hold values from -6 to 6
- block_keys: bfloat16 [512, 512], P('ctx'), may hold values from -6 to 6
- block_values: bfloat16 [512, 512], P('ctx'), may hold values from -6 to 6
- seg_starts: int32 [10], replicated, may hold values from 0 to 1408, as said below
- out_weight: bfloat16 [8192, 4096], P('exp', 'ctx'), may hold values from -0.5 to 0.5
- residual: bfloat16 [512, 4096], P('exp', 'ctx'), may hold values from -45 to 45
- norm_gain: float32 [4096], P('ctx'), may hold values from 0.1 to 1.9
- routes: int32 [512, 8], P('exp'), may hold values from 0 to 127, as said below
- gate_values: float32 [512, 8], P('exp'), may hold values from 0.05 to 0.5
- expert_in: bfloat16 [8, 4096, 3072], P('exp', 'ctx'), may hold values from -0.09375 to 0.09375
- expert_out: bfloat16 [8, 1536, 4096], P('exp', None, 'ctx'), may hold values from -0.15625 to 0.15625
Outputs:
- mixed: bfloat16 [512, 4096], P('exp', 'ctx')
- expert_sum: bfloat16 [512, 4096], P('exp', 'ctx')
The draws below stay inside these ranges and needn't reach their ends.
Inputs may be any that keep to these rules, and one draw needn't show every extreme that they name: `routes`: 8 different experts in each row; within the rows of one index of exp (aligned blocks of 128 rows) no expert is named by more than 16 rows, and one expert numbered below 8 is named by exactly 16 rows in every block. `seg_starts`: strictly rising, the first 0; the last segment (the aggregator's part) starts inside the prefilled block.
All inputs are finite; a program needn't handle non-finite values.
Results may differ from the reference program's by a relative error of at most 0.029.
Values may be sent and summed in bfloat16 or wider, within the bound.
No kernel may reach another device: no remote copies, remote signals or barrier semaphores. Data moves between devices by JAX's collectives and lax.ppermute only.
A program may use at most 64 MiB of HBM per device.

```python
import math
import jax
import jax.numpy as jnp
from jax import lax

D = 4096
QHEADS = 64
KVH = 4
HEAD = 128
EXPERTS = 128
FFE = 1536
TOPK = 8
NSEG = 10
CAP = 16
SPAN = 512
CACHE = 1024
SEQ = 1536
TOK_EXP = 128
FLIGHT = 8
N_CTX = 8
N_EXP = 4


def shared_keys(key):
    base_key = jax.random.fold_in(key, 101)
    drawn_keys = jnp.clip(jax.random.normal(base_key, (CACHE, KVH * HEAD), jnp.float32), -6.0, 6.0)
    return drawn_keys


def draw_cache_keys(key, part):
    return shared_keys(key).astype(jnp.bfloat16)


def draw_queries(key, part):
    own_key = jax.random.fold_in(key, 202)
    drawn_rows = jnp.clip(2.0 * jax.random.normal(own_key, (SPAN, QHEADS * HEAD), jnp.float32), -16.0, 16.0)
    return drawn_rows.astype(jnp.bfloat16)


def draw_residual(key, part):
    key_row, key_col, key_noise = jax.random.split(jax.random.fold_in(key, 303), 3)
    row_scale = jnp.exp(jax.random.uniform(key_row, (SPAN, 1), jnp.float32, math.log(0.25), math.log(2.5)))
    col_ramp = 0.5 + jnp.arange(D, dtype=jnp.float32)[None, :] / D
    col_scale = jnp.exp(jax.random.uniform(key_col, (1, D), jnp.float32, math.log(0.2), math.log(2.0))) * col_ramp
    noise_part = jnp.clip(jax.random.normal(key_noise, (SPAN, D), jnp.float32), -6.0, 6.0)
    return (noise_part * row_scale * col_scale).astype(jnp.bfloat16)


def draw_routes(key, part):
    key_hot, key_blocks = jax.random.split(jax.random.fold_in(key, 404), 2)
    hot_expert = jax.random.randint(key_hot, (), 0, FLIGHT)
    others_count = EXPERTS - 1
    block_count = SPAN // TOK_EXP

    def one_block(block_key):
        key_perm, key_shift, key_rows = jax.random.split(block_key, 3)
        shuffled = jax.random.permutation(key_perm, others_count)
        others = jnp.where(shuffled >= hot_expert, shuffled + 1, shuffled)
        cyc_shift = jax.random.randint(key_shift, (), 0, others_count)
        cycle_pos = (jnp.arange(TOK_EXP)[:, None] * TOPK + jnp.arange(TOPK)[None, :] + cyc_shift) % others_count
        chosen_ids = others[cycle_pos]
        hot_rows = jax.random.permutation(key_rows, TOK_EXP)[:CAP]
        hot_flag = jnp.zeros((TOK_EXP,), jnp.int32).at[hot_rows].set(1)
        last_slot = jnp.where(hot_flag == 1, hot_expert, chosen_ids[:, TOPK - 1])
        return chosen_ids.at[:, TOPK - 1].set(last_slot)
    block_keys = jax.random.split(key_blocks, block_count)
    return jax.vmap(one_block)(block_keys).reshape(SPAN, TOPK).astype(jnp.int32)


def draw_seg_starts(key, part):
    key_prefix, key_agg, key_shares = jax.random.split(jax.random.fold_in(key, 505), 3)
    low_end = max(SEQ // 16, 8)
    high_end = max(SEQ // 8, low_end + 1)
    prefix = jax.random.randint(key_prefix, (), low_end, high_end)
    agg_start = jax.random.randint(key_agg, (), CACHE + SPAN // 2, CACHE + 3 * SPAN // 4 + 1)
    shares = jax.random.randint(key_shares, (NSEG - 2,), 1, 9)
    before = jnp.cumsum(shares) - shares
    share_sum = jnp.sum(shares)
    proposer = prefix + (agg_start - prefix - (NSEG - 2)) * before // share_sum + jnp.arange(NSEG - 2)
    return jnp.concatenate([jnp.zeros((1,), jnp.int32), proposer.astype(jnp.int32), agg_start.reshape(1).astype(jnp.int32)])


def shard_levels(key, shape, cuts, smallest, high):
    factor_of, own = 1.0, jax.random.fold_in(key, 6)
    for axis_at, shards_of in cuts:
        steps = jnp.exp(jax.random.uniform(jax.random.fold_in(own, axis_at), (shards_of,), jnp.float32, smallest / len(cuts), high / len(cuts)))
        factor_of = factor_of * jnp.repeat(steps, shape[axis_at] // shards_of).reshape([-1 if axis == axis_at else 1 for axis in range(len(shape))])
    return factor_of


def scatter_about(key, dims, scale, reach, cuts=(), held_as=jnp.bfloat16):
    factor_of = shard_levels(key, dims, cuts, -0.22, 0.18) if cuts else 1.0
    values = jax.random.normal(key, dims, jnp.float32) * scale * factor_of
    return jnp.minimum(jnp.maximum(values, -reach), reach).astype(held_as)


def setup_inputs(seed: int = 0) -> dict:
    keys = jax.random.split(jax.random.key(seed), 14)
    queries = draw_queries(jax.random.fold_in(keys[13], 71), 0)
    cache_keys = draw_cache_keys(jax.random.fold_in(keys[13], 71), 0)
    cache_values = scatter_about(keys[2], (CACHE, KVH * HEAD), 1.0, 6.0, ((0, 8),))
    block_keys = scatter_about(keys[3], (SPAN, KVH * HEAD), 1.0, 6.0, ((0, 8),))
    block_values = scatter_about(keys[4], (SPAN, KVH * HEAD), 1.0, 6.0, ((0, 8),))
    seg_starts = draw_seg_starts(jax.random.fold_in(keys[13], 71), 0)
    out_weight = scatter_about(keys[6], (QHEADS * HEAD, D), HEAD ** -0.5, 0.5, ((0, 4), (1, 8)))
    residual = draw_residual(jax.random.fold_in(keys[13], 71), 0)
    norm_gain = jnp.clip(1.0 + 0.18 * jax.random.normal(keys[8], (D,), jnp.float32), 0.1, 1.9)
    routes = draw_routes(jax.random.fold_in(keys[13], 71), 0)
    gate_values = jnp.clip(jnp.exp(math.log(0.5) - 2.3025851 * jax.random.uniform(keys[10], (SPAN, TOPK), jnp.float32) ** shard_levels(keys[10], (SPAN, TOPK), ((0, 4),), -0.2, 0.2)), 0.05, 0.5)
    expert_in = scatter_about(keys[11], (FLIGHT, D, 2 * FFE), D ** -0.5, 0.09375, ((0, 4), (1, 8)))
    expert_out = scatter_about(keys[12], (FLIGHT, FFE, D), FFE ** -0.5, 0.15625, ((0, 4), (2, 8)))
    return dict(queries=queries, cache_keys=cache_keys, cache_values=cache_values, block_keys=block_keys, block_values=block_values, seg_starts=seg_starts, out_weight=out_weight, residual=residual, norm_gain=norm_gain, routes=routes, gate_values=gate_values, expert_in=expert_in, expert_out=expert_out)


neg_large = -1e+30
eps_norm = 1e-06

def segment_of(positions, seg_starts):
    passed = (seg_starts[None, :] <= positions[:, None]).astype(jnp.int32)
    return lax.optimization_barrier(jnp.sum(passed, axis=1)) - 1

def reference(queries, cache_keys, cache_values, block_keys, block_values, seg_starts, out_weight, residual, norm_gain, routes, gate_values, expert_in, expert_out):
    all_keys = jnp.concatenate([cache_keys, block_keys], axis=0)
    all_values = jnp.concatenate([cache_values, block_values], axis=0)
    key_pos = jnp.arange(SEQ, dtype=jnp.int32)
    query_pos = CACHE + jnp.arange(SPAN, dtype=jnp.int32)
    key_seg = segment_of(key_pos, seg_starts)
    query_seg = segment_of(query_pos, seg_starts)
    allowed = (key_pos[None, :] <= query_pos[:, None]) & ((key_seg[None, :] == query_seg[:, None]) | (key_seg[None, :] == 0) | (query_seg[:, None] == NSEG - 1))
    score_scale = 1.0 / math.sqrt(HEAD)

    def one_head(head_index):
        kv_index = head_index // (QHEADS // KVH)
        head_q = lax.dynamic_slice_in_dim(queries, head_index * HEAD, HEAD, 1)
        head_k = lax.dynamic_slice_in_dim(all_keys, kv_index * HEAD, HEAD, 1)
        head_v = lax.dynamic_slice_in_dim(all_values, kv_index * HEAD, HEAD, 1)
        scores = lax.dot_general(head_q, head_k, (((1,), (1,)), ((), ())), preferred_element_type=jnp.float32) * score_scale
        scores = jnp.where(allowed, scores, neg_large)
        row_max = lax.optimization_barrier(jnp.max(scores, axis=1, keepdims=True))
        weights_now = jnp.where(allowed, jnp.exp(scores - row_max), 0.0)
        row_sum = lax.optimization_barrier(jnp.sum(weights_now, axis=1, keepdims=True))
        gathered = jnp.dot(weights_now.astype(jnp.bfloat16), head_v, preferred_element_type=jnp.float32)
        return (gathered / row_sum).astype(jnp.bfloat16)
    heads_out = lax.map(one_head, jnp.arange(QHEADS, dtype=jnp.int32))
    heads_out = jnp.transpose(heads_out, (1, 0, 2)).reshape(SPAN, QHEADS * HEAD)
    mixed = (residual.astype(jnp.float32) + jnp.dot(heads_out, out_weight, preferred_element_type=jnp.float32)).astype(jnp.bfloat16)
    mixed_wide = mixed.astype(jnp.float32)
    mean_square = lax.optimization_barrier(jnp.mean(mixed_wide * mixed_wide, axis=1))
    normed = (mixed_wide * lax.rsqrt(mean_square + eps_norm)[:, None] * norm_gain[None, :]).astype(jnp.bfloat16)
    block_width = D // N_CTX
    most_rows = N_EXP * CAP

    def one_expert(carried, expert_id):
        matched = routes == expert_id
        member = jnp.any(matched, axis=1)
        pair_gate = lax.optimization_barrier(jnp.sum(jnp.where(matched, gate_values, 0.0), axis=1))
        picked_rows = jnp.nonzero(member, size=most_rows, fill_value=0)[0].astype(jnp.int32)
        live_rows = (jnp.arange(most_rows, dtype=jnp.int32) < jnp.sum(member.astype(jnp.int32))).astype(jnp.float32)
        picked = normed[picked_rows].astype(jnp.float32).reshape(most_rows, N_CTX, block_width)
        weight_in = expert_in[expert_id].astype(jnp.float32).reshape(N_CTX, block_width, 2 * FFE)
        blocks = jnp.einsum('mcd,cdf->cmf', picked, weight_in)
        rounded = lax.optimization_barrier(blocks.astype(jnp.bfloat16)).astype(jnp.float32)
        gate_up = lax.optimization_barrier(jnp.sum(rounded, axis=0))
        active = (jax.nn.silu(gate_up[:, :FFE]) * gate_up[:, FFE:]).astype(jnp.bfloat16)
        produced = jnp.dot(active, expert_out[expert_id], preferred_element_type=jnp.float32).astype(jnp.bfloat16)
        scaled = produced.astype(jnp.float32) * (pair_gate[picked_rows] * live_rows)[:, None]
        return (carried.at[picked_rows].add(scaled), None)
    scanned = lax.scan(one_expert, jnp.zeros((SPAN, D), jnp.float32), jnp.arange(FLIGHT, dtype=jnp.int32))
    return (mixed, scanned[0].astype(jnp.bfloat16))
```

```python
import functools
import math

import jax
import jax.numpy as jnp
from jax import lax
from jax.experimental import pallas as pl
from jax.experimental.pallas import tpu as pltpu
from jax.sharding import PartitionSpec as P

QHEADS = 64
KVH = 4
HEAD = 128
CAP = 16
LANES = 128

neg_large = -1e30
eps_norm = 1e-06
bf16 = jnp.bfloat16
f32 = jnp.float32
MIB = 1024 * 1024

VMEM = pl.BlockSpec(memory_space=pltpu.VMEM)
SMEM = pl.BlockSpec(memory_space=pltpu.SMEM)
ANY = pl.BlockSpec(memory_space=pl.ANY)


def call(kernel, out_shape, in_specs, scratch=(), vmem=16, flops=0, nbytes=0):
    many = isinstance(out_shape, (list, tuple))
    return pl.pallas_call(
        kernel,
        out_shape=out_shape,
        in_specs=in_specs,
        out_specs=[VMEM] * len(out_shape) if many else VMEM,
        scratch_shapes=list(scratch),
        compiler_params=pltpu.CompilerParams(vmem_limit_bytes=vmem * MIB),
        cost_estimate=pl.CostEstimate(flops=flops, bytes_accessed=nbytes, transcendentals=0),
    )


def shape(dims, dtype):
    return jax.ShapeDtypeStruct(dims, dtype)


def dot(a, b):
    return lax.dot_general(a, b, (((1,), (0,)), ((), ())), preferred_element_type=f32)


def dot_t(a, b):
    return lax.dot_general(a, b, (((1,), (1,)), ((), ())), preferred_element_type=f32)


def rows_at(start, size, step):
    return pl.ds(pl.multiple_of(start, step), size)


def pick_kv(local_heads, ck, cv, bk, bv, out, sems):
    kv = lax.axis_index("exp") * local_heads // (QHEADS // KVH)
    cols = rows_at(kv * HEAD, HEAD, HEAD)
    cache, span = ck.shape[0], bk.shape[0]
    copies = []
    for n, (src, row, size, col) in enumerate(
        ((ck, 0, cache, 0), (cv, 0, cache, HEAD), (bk, cache, span, 0), (bv, cache, span, HEAD))
    ):
        copies.append(
            pltpu.make_async_copy(
                src.at[:, cols], out.at[pl.ds(row, size), pl.ds(col, HEAD)], sems.at[n]
            )
        )
    for copy in copies:
        copy.start()
    for copy in copies:
        copy.wait()


def rank_kernel(routes, gates, rank, gate):
    flight, tokens = rank.shape
    expert = lax.broadcasted_iota(jnp.int32, (flight, tokens), 0)
    member = jnp.zeros((flight, tokens), f32)
    weight = jnp.zeros((flight, tokens), f32)
    for k in range(routes.shape[0]):
        hit = routes[k : k + 1, :] == expert
        member = jnp.where(hit, 1.0, member)
        weight = weight + jnp.where(hit, gates[k : k + 1, :], 0.0)
    before = lax.broadcasted_iota(jnp.int32, (tokens, tokens), 0) < lax.broadcasted_iota(
        jnp.int32, (tokens, tokens), 1
    )
    count = dot(member.astype(bf16), jnp.where(before, 1.0, 0.0).astype(bf16))
    rank[...] = jnp.where(member > 0.5, count, -1.0)
    gate[...] = weight


def segment_of(position, seg_starts):
    passed = jnp.full(position.shape, -1, jnp.int32)
    for n in range(seg_starts.shape[0]):
        passed = passed + jnp.where(seg_starts[n] <= position, 1, 0)
    return passed


def visible(seg_starts, other, span, cache, pieces):
    ctx = lax.axis_index("ctx")
    cache_total = cache * lax.axis_size("ctx")
    piece_rows = cache + span
    keys = pieces * piece_rows
    index = lax.broadcasted_iota(jnp.int32, (1, keys), 1)
    key_pos = jnp.zeros((1, keys), jnp.int32)
    for k in range(pieces):
        owner = jnp.bitwise_xor(ctx, 2 * k + other)
        off = index - k * piece_rows
        pos = jnp.where(off < cache, owner * cache + off, cache_total + owner * span + off - cache)
        key_pos = pos if k == 0 else jnp.where(off >= 0, pos, key_pos)
    key_seg = segment_of(key_pos, seg_starts)
    query_pos = cache_total + ctx * span + lax.broadcasted_iota(jnp.int32, (span, 1), 0)
    query_seg = segment_of(query_pos, seg_starts)
    last = seg_starts.shape[0] - 1
    return (key_pos <= query_pos) & (
        (key_seg == query_seg) | (key_seg == 0) | (query_seg == last)
    )


GROUP = 4


def attend(seg_starts, q, kv, other, span, cache, heads, finish):
    pieces = kv.shape[0] // (cache + span)
    seen = visible(seg_starts, other, span, cache, pieces)
    scale = math.log2(math.e) / math.sqrt(HEAD)
    group = min(GROUP, heads)
    rows = group * span
    keys = kv[:, :HEAD]
    values = kv[:, HEAD:]
    for g in range(heads // group):
        stacked = jnp.concatenate(
            [q[:, (g * group + h) * HEAD : (g * group + h + 1) * HEAD] for h in range(group)], axis=0
        )
        scores = dot_t(stacked, keys)
        scores = jnp.where(
            seen[None], scores.reshape(group, span, kv.shape[0]), neg_large
        ).reshape(rows, kv.shape[0])
        top = jnp.max(scores, axis=1, keepdims=True)
        probs = jnp.exp2((scores - top) * scale)
        total = jnp.sum(probs, axis=1, keepdims=True)
        out = dot(probs.astype(bf16), values)
        finish(g, rows, group, out, top, total)


def attend_first(span, cache, heads, seg_starts, q, kv, o_out, m_out, l_out):
    def finish(g, rows, group, out, top, total):
        at = pl.ds(g * rows, rows)
        o_out[at, :] = out
        m_out[at, :] = jnp.broadcast_to(top, (rows, LANES))
        l_out[at, :] = jnp.broadcast_to(total, (rows, LANES))

    attend(seg_starts, q, kv, 0, span, cache, heads, finish)


def attend_second(span, cache, heads, seg_starts, q, kv, o_in, m_in, l_in, result):
    scale = math.log2(math.e) / math.sqrt(HEAD)

    def finish(g, rows, group, out, top, total):
        at = pl.ds(g * rows, rows)
        first = m_in[at, :]
        both = jnp.maximum(first, top)
        w_first = jnp.exp2((first - both) * scale)
        w_second = jnp.exp2((top - both) * scale)
        norm = l_in[at, :] * w_first + total * w_second
        merged = ((o_in[at, :] * w_first + out * w_second) / norm).astype(bf16)
        for h in range(group):
            col = (g * group + h) * HEAD
            result[:, col : col + HEAD] = merged[h * span : (h + 1) * span, :]

    attend(seg_starts, q, kv, 1, span, cache, heads, finish)


def project_first(heads_out, weight, out):
    out[...] = dot(heads_out[...], weight[...])


def project_second(n_exp, span, heads_out, weight, first, residual, *refs):
    ranks = refs[:n_exp]
    own_out = refs[n_exp]
    part_outs = refs[n_exp + 1 : 2 * n_exp]
    pick_outs = refs[2 * n_exp : 3 * n_exp]
    whole, picked = refs[3 * n_exp :]
    ctx, exp = lax.axis_index("ctx"), lax.axis_index("exp")
    second = dot(heads_out[...], weight[...])
    for k in range(heads_out.shape[0] // span):
        here = slice(k * span, (k + 1) * span)
        whole[rows_at(jnp.bitwise_xor(ctx, 2 * k) * span, span, span), :] = first[here, :]
        whole[rows_at(jnp.bitwise_xor(ctx, 2 * k + 1) * span, span, span), :] = second[here, :]
    tokens = residual.shape[0]
    flight = ranks[0].shape[0]
    local = flight // n_exp
    slot = lax.broadcasted_iota(jnp.int32, (CAP, tokens), 0).astype(f32)
    for k in range(n_exp):
        block = jnp.bitwise_xor(exp, k)
        part = whole[rows_at(block * tokens, tokens, tokens), :]
        if k == 0:
            part = part + residual[...].astype(f32)
            own_out[...] = part
        narrow = part.astype(bf16)
        if k > 0:
            part_outs[k - 1][...] = narrow
        rank = ranks[k][...]
        table = jnp.concatenate(
            [jnp.where(rank[e : e + 1, :] == slot, 1.0, 0.0) for e in range(flight)], axis=0
        ).astype(bf16)
        rows = dot(table, narrow).astype(bf16)
        for e in range(flight):
            at = (e % local) * n_exp * CAP + block * CAP
            picked[e // local, rows_at(at, CAP, CAP), :] = rows[e * CAP : (e + 1) * CAP, :]
    for k in range(n_exp):
        pick_outs[k][...] = picked[jnp.bitwise_xor(exp, k)]


def split_square(square):
    lane = lax.broadcasted_iota(jnp.int32, (square.shape[0], LANES), 1)
    high = square.astype(bf16).astype(f32)
    return jnp.where(lane == 0, high, jnp.where(lane == 1, square - high, 0.0))


def expert_in_kernel(n_exp, other, *refs):
    arrived = refs[:n_exp]
    gain, weight, out, held, sems = refs[n_exp:]
    expert = jnp.bitwise_xor(lax.axis_index("ctx") % 2, other)
    rows = out.shape[0]
    width = weight.shape[2]
    chunks = held.shape[0]
    step = width // chunks
    copies = [
        pltpu.make_async_copy(
            weight.at[expert, :, pl.ds(n * step, step)], held.at[n], sems.at[n]
        )
        for n in range(chunks)
    ]
    for copy in copies:
        copy.start()
    at = rows_at(expert * rows, rows, rows)
    total = arrived[0][at, :].astype(f32)
    for ref in arrived[1:]:
        total = total + ref[at, :].astype(f32)
    mixed = total.astype(bf16).astype(f32)
    out[:, width:] = split_square(jnp.sum(mixed * mixed, axis=1, keepdims=True)).astype(out.dtype)
    scaled = (mixed * gain[...]).astype(bf16)
    for n, copy in enumerate(copies):
        copy.wait()
        out[:, n * step : (n + 1) * step] = dot(scaled, held[n]).astype(out.dtype)


def chip_sum(mine, theirs, *outs):
    chip = lax.axis_index("ctx") // 2
    width = mine.shape[1] - LANES
    size = outs[0].shape[0]
    for k, out in enumerate(outs):
        at = rows_at(jnp.bitwise_xor(chip, k) * size, size, size)
        total = mine[at, :] + theirs[at, :].astype(f32)
        out[:, :width] = total[:, :width].astype(bf16)
        out[:, width:] = split_square(
            jnp.sum(total[:, width:], axis=1, keepdims=True)
        ).astype(bf16)


def activate(features, *refs):
    out = refs[-1]
    total = refs[0][...].astype(f32)
    for ref in refs[1:-1]:
        total = total + ref[...].astype(f32)
    hidden = out.shape[1]
    square = jnp.sum(total[:, 2 * hidden :], axis=1, keepdims=True)
    inverse = lax.rsqrt(square / features + eps_norm)
    gate = total[:, :hidden] * inverse
    up = total[:, hidden : 2 * hidden] * inverse
    out[...] = (gate / (1.0 + jnp.exp(-gate)) * up).astype(bf16)


def load_expert(weight, other, held, sem):
    expert = jnp.bitwise_xor(lax.axis_index("ctx") % 2, other)
    return pltpu.make_async_copy(weight.at[expert], held, sem)


def expert_out_first(active, weight, out, held, sem):
    copy = load_expert(weight, 0, held, sem)
    copy.start()
    copy.wait()
    out[...] = dot(active[...], held[...]).astype(bf16)


def expert_out_second(n_exp, active, weight, first, *refs):
    outs = refs[:n_exp]
    held, whole, sem = refs[n_exp:]
    copy = load_expert(weight, 1, held, sem)
    copy.start()
    ctx, exp = lax.axis_index("ctx"), lax.axis_index("exp")
    core, chip = ctx % 2, ctx // 2
    chips = lax.axis_size("ctx") // 2
    size = active.shape[0] // chips
    copy.wait()
    second = dot(active[...], held[...]).astype(bf16)
    for k in range(chips):
        at = rows_at(jnp.bitwise_xor(chip, k) * size, size, size)
        here = slice(k * size, (k + 1) * size)
        whole[core, at, :] = first[here, :]
        whole[1 - core, at, :] = second[here, :]
    for k in range(n_exp):
        at = rows_at(jnp.bitwise_xor(exp, k) * CAP, CAP, CAP)
        for j in range(whole.shape[0]):
            outs[k][j * CAP : (j + 1) * CAP, :] = whole[j, at, :]


def combine(n_exp, rank, gate, *refs):
    returned, out = refs[:n_exp], refs[n_exp]
    exp = lax.axis_index("exp")
    tokens = rank.shape[1]
    local = rank.shape[0] // n_exp
    slot = lax.broadcasted_iota(jnp.int32, (CAP, tokens), 0).astype(f32)
    tables = []
    for k in range(n_exp):
        for j in range(local):
            at = pl.ds(jnp.bitwise_xor(exp, k) * local + j, 1)
            tables.append(jnp.where(rank[at, :] == slot, gate[at, :], 0.0))
    table = jnp.concatenate(tables, axis=0).T
    rows = jnp.concatenate([ref[...] for ref in returned], axis=0)
    high = table.astype(bf16)
    low = (table - high.astype(f32)).astype(bf16)
    out[...] = (dot(high, rows) + dot(low, rows)).astype(bf16)


def permute(x, axis, k):
    n = lax.axis_size(axis)
    return lax.ppermute(x, axis, [(i, i ^ k) for i in range(n)])


def body(
    queries,
    cache_keys,
    cache_values,
    block_keys,
    block_values,
    seg_starts,
    out_weight,
    residual,
    norm_gain,
    routes,
    gate_values,
    expert_in,
    expert_out,
):
    n_ctx, n_exp = lax.axis_size("ctx"), lax.axis_size("exp")
    chips = n_ctx // 2
    span = queries.shape[0]
    heads = queries.shape[1] // HEAD
    cache = cache_keys.shape[0]
    tokens = routes.shape[0]
    local, features, width = expert_in.shape
    hidden = width // 2
    columns = out_weight.shape[1]
    flight = n_exp * local

    def over_chips(x):
        return [permute(x, "ctx", 2 * k) for k in range(1, chips)]

    def over_exp(xs):
        return [permute(x, "exp", k) for k, x in zip(range(1, n_exp), xs)]

    local_kv = call(
        functools.partial(pick_kv, heads),
        shape((cache + span, 2 * HEAD), bf16),
        [ANY] * 4,
        [pltpu.SemaphoreType.DMA((4,))],
        vmem=4,
    )(cache_keys, cache_values, block_keys, block_values)
    kv_same = jnp.concatenate([local_kv] + over_chips(local_kv), axis=0)
    kv_other = permute(kv_same, "ctx", 1)

    rank, gate = call(
        rank_kernel,
        [shape((flight, tokens), f32)] * 2,
        [VMEM] * 2,
        vmem=4,
    )(routes.T, gate_values.T)
    ranks = [rank] + over_exp([rank] * (n_exp - 1))

    rows = heads * span
    cost = dict(flops=4 * rows * kv_same.shape[0] * HEAD, nbytes=4 * MIB)
    stats = call(
        functools.partial(attend_first, span, cache, heads),
        [shape((rows, HEAD), f32), shape((rows, LANES), f32), shape((rows, LANES), f32)],
        [SMEM, VMEM, VMEM],
        vmem=24,
        **cost,
    )(seg_starts, queries, kv_same)
    heads_out = call(
        functools.partial(attend_second, span, cache, heads),
        shape((span, heads * HEAD), bf16),
        [SMEM] + [VMEM] * 5,
        vmem=24,
        **cost,
    )(seg_starts, queries, kv_other, *stats)

    heads_same = jnp.concatenate([heads_out] + over_chips(heads_out), axis=0)
    heads_other = permute(heads_same, "ctx", 1)
    cost = dict(
        flops=2 * heads_same.shape[0] * heads_same.shape[1] * columns, nbytes=4 * MIB
    )
    first = call(
        project_first,
        shape((heads_same.shape[0], columns), f32),
        [VMEM] * 2,
        vmem=16,
        **cost,
    )(heads_same, out_weight)
    per_exp = local * n_exp * CAP
    outs = call(
        functools.partial(project_second, n_exp, span),
        [shape((tokens, columns), f32)]
        + [shape((tokens, columns), bf16)] * (n_exp - 1)
        + [shape((per_exp, columns), bf16)] * n_exp,
        [VMEM] * (4 + n_exp),
        [
            pltpu.VMEM((n_ctx * span, columns), f32),
            pltpu.VMEM((n_exp, per_exp, columns), bf16),
        ],
        vmem=24,
        **cost,
    )(heads_other, out_weight, first, residual, *ranks)
    own, parts, picks = outs[0], outs[1:n_exp], outs[n_exp:]
    arrived = [picks[0]] + over_exp(picks[1:])

    gain = norm_gain.reshape(1, features)
    expert_rows = n_exp * CAP
    chunks = 6

    def gate_up(other, dtype):
        return call(
            functools.partial(expert_in_kernel, n_exp, other),
            shape((expert_rows, width + LANES), dtype),
            [VMEM] * (n_exp + 1) + [ANY],
            [
                pltpu.VMEM((chunks, features, width // chunks), bf16),
                pltpu.SemaphoreType.DMA((chunks,)),
            ],
            vmem=16,
            flops=2 * expert_rows * features * width,
            nbytes=4 * MIB,
        )(*arrived, gain, expert_in)

    sent = gate_up(1, bf16)
    theirs = permute(sent, "ctx", 1)
    mine = gate_up(0, f32)

    parts, mine = lax.optimization_barrier((parts, mine))
    part_sum = own
    for part in over_exp(parts):
        part_sum = part_sum + part.astype(f32)
    mixed = part_sum.astype(bf16)

    size = expert_rows // chips
    chunk = call(
        chip_sum,
        [shape((size, width + LANES), bf16)] * chips,
        [VMEM] * 2,
        vmem=8,
    )(mine, theirs)
    gathered = [chunk[0]] + [permute(chunk[k], "ctx", 2 * k) for k in range(1, chips)]
    active = call(
        functools.partial(activate, n_ctx * features),
        shape((size, hidden), bf16),
        [VMEM] * chips,
        vmem=8,
    )(*gathered)
    active_same = jnp.concatenate([active] + over_chips(active), axis=0)
    active_other = permute(active_same, "ctx", 1)
    held = pltpu.VMEM((hidden, columns), bf16)
    cost = dict(flops=2 * expert_rows * hidden * columns, nbytes=2 * MIB)
    made = call(
        expert_out_first,
        shape((expert_rows, columns), bf16),
        [VMEM, ANY],
        [held, pltpu.SemaphoreType.DMA],
        vmem=8,
        **cost,
    )(active_same, expert_out)
    produced = call(
        functools.partial(expert_out_second, n_exp),
        [shape((local * CAP, columns), bf16)] * n_exp,
        [VMEM, ANY, VMEM],
        [held, pltpu.VMEM((local, expert_rows, columns), bf16), pltpu.SemaphoreType.DMA],
        vmem=8,
        **cost,
    )(active_other, expert_out, made)
    returned = [produced[0]] + over_exp(produced[1:])
    expert_sum = call(
        functools.partial(combine, n_exp),
        shape((tokens, columns), bf16),
        [VMEM] * (2 + n_exp),
        vmem=8,
    )(rank, gate, *returned)
    return (mixed, expert_sum)


def solution(mesh):
    placed = (
        P("ctx", "exp"),
        P("ctx", None),
        P("ctx", None),
        P("ctx", None),
        P("ctx", None),
        P(),
        P("exp", "ctx"),
        P("exp", "ctx"),
        P("ctx"),
        P("exp", None),
        P("exp", None),
        P("exp", "ctx", None),
        P("exp", None, "ctx"),
    )
    return jax.shard_map(
        body,
        mesh=mesh,
        in_specs=placed,
        out_specs=(P("exp", "ctx"), P("exp", "ctx")),
        check_vma=False,
    )
```

```python
import functools
import math

import jax
import jax.numpy as jnp
from jax import lax
from jax.experimental import pallas as pl
from jax.experimental.pallas import tpu as pltpu
from jax.sharding import PartitionSpec as P

QHEADS = 64
KVH = 4
HEAD = 128
CAP = 16
LANES = 128

neg_large = -1e30
eps_norm = 1e-06
bf16 = jnp.bfloat16
f32 = jnp.float32
MIB = 1024 * 1024
ALL_VMEM = 63.5

VMEM = pl.BlockSpec(memory_space=pltpu.VMEM)
SMEM = pl.BlockSpec(memory_space=pltpu.SMEM)
HBM = pl.BlockSpec(memory_space=pltpu.HBM)


def call(kernel, out_shape, in_specs, scratch=(), vmem=16, flops=0, nbytes=0):
    many = isinstance(out_shape, (list, tuple))
    return pl.pallas_call(
        kernel,
        out_shape=out_shape,
        in_specs=in_specs,
        out_specs=[VMEM] * len(out_shape) if many else VMEM,
        scratch_shapes=list(scratch),
        compiler_params=pltpu.CompilerParams(vmem_limit_bytes=int(vmem * MIB)),
        cost_estimate=pl.CostEstimate(flops=flops, bytes_accessed=nbytes, transcendentals=0),
    )


def shape(dims, dtype):
    return jax.ShapeDtypeStruct(dims, dtype)


def dot(a, b):
    return lax.dot_general(a, b, (((1,), (0,)), ((), ())), preferred_element_type=f32)


def dot_t(a, b):
    return lax.dot_general(a, b, (((1,), (1,)), ((), ())), preferred_element_type=f32)


def rows_at(start, size, step):
    return pl.ds(pl.multiple_of(start, step), size)


def pick_kv(local_heads, ck, cv, bk, bv, out, sems):
    kv = lax.axis_index("exp") * local_heads // (QHEADS // KVH)
    cols = rows_at(kv * HEAD, HEAD, HEAD)
    cache, span = ck.shape[0], bk.shape[0]
    copies = []
    for n, (src, row, size, col) in enumerate(
        ((ck, 0, cache, 0), (cv, 0, cache, HEAD), (bk, cache, span, 0), (bv, cache, span, HEAD))
    ):
        copies.append(
            pltpu.make_async_copy(
                src.at[:, cols], out.at[pl.ds(row, size), pl.ds(col, HEAD)], sems.at[n]
            )
        )
    for copy in copies:
        copy.start()
    for copy in copies:
        copy.wait()


def segment_of(position, seg_starts):
    passed = jnp.full(position.shape, -1, jnp.int32)
    for n in range(seg_starts.shape[0]):
        passed = passed + jnp.where(seg_starts[n] <= position, 1, 0)
    return passed


def mask_bias(seg_starts, other, span, cache, pieces):
    ctx = lax.axis_index("ctx")
    cache_total = cache * lax.axis_size("ctx")
    piece_rows = cache + span
    keys = pieces * piece_rows
    index = lax.broadcasted_iota(jnp.int32, (1, keys), 1)
    key_pos = jnp.zeros((1, keys), jnp.int32)
    for k in range(pieces):
        owner = jnp.bitwise_xor(ctx, 2 * k + other)
        off = index - k * piece_rows
        pos = jnp.where(off < cache, owner * cache + off, cache_total + owner * span + off - cache)
        key_pos = pos if k == 0 else jnp.where(off >= 0, pos, key_pos)
    key_seg = segment_of(key_pos, seg_starts)
    query_pos = cache_total + ctx * span + lax.broadcasted_iota(jnp.int32, (span, 1), 0)
    query_seg = segment_of(query_pos, seg_starts)
    last = seg_starts.shape[0] - 1
    seen = (key_pos <= query_pos) & (
        (key_seg == query_seg) | (key_seg == 0) | (query_seg == last)
    )
    return jnp.where(seen, 0.0, neg_large)


def prepare(
    n_exp, span, cache, seg_starts, q, routes, gates,
    stacked, bias_same, bias_other, rank, high, low, q_vmem, routes_vmem, gates_vmem, sems,
):
    copies = [
        pltpu.make_async_copy(src, dst, sems.at[n])
        for n, (src, dst) in enumerate(
            ((routes, routes_vmem), (gates, gates_vmem), (q, q_vmem))
        )
    ]
    for copy in copies:
        copy.start()
    pieces = bias_same.shape[1] // (cache + span)
    bias_same[...] = mask_bias(seg_starts, 0, span, cache, pieces)
    bias_other[...] = mask_bias(seg_starts, 1, span, cache, pieces)
    flight, tokens = rank.shape
    local = flight // n_exp
    expert = lax.broadcasted_iota(jnp.int32, (flight, tokens), 0)
    member = jnp.zeros((flight, tokens), f32)
    weight = jnp.zeros((flight, tokens), f32)
    copies[0].wait()
    copies[1].wait()
    for k in range(routes.shape[0]):
        hit = routes_vmem[k : k + 1, :] == expert
        member = jnp.where(hit, 1.0, member)
        weight = weight + jnp.where(hit, gates_vmem[k : k + 1, :], 0.0)
    before = lax.broadcasted_iota(jnp.int32, (tokens, tokens), 0) < lax.broadcasted_iota(
        jnp.int32, (tokens, tokens), 1
    )
    count = dot(member.astype(bf16), jnp.where(before, 1.0, 0.0).astype(bf16))
    slots = jnp.where(member > 0.5, count, -1.0)
    rank[...] = slots
    exp = lax.axis_index("exp")
    slot = lax.broadcasted_iota(jnp.int32, (CAP, tokens), 0).astype(f32)
    tables = []
    for e in range(flight):
        tables.append(jnp.where(slots[e : e + 1, :] == slot, weight[e : e + 1, :], 0.0))
    per = local * CAP
    table = jnp.concatenate(tables, axis=0)
    upper = table.astype(bf16)
    lower = (table - upper.astype(f32)).astype(bf16)
    for d in range(n_exp):
        at = pl.ds(pl.multiple_of(jnp.bitwise_xor(exp, d) * per, per), per)
        high[at, :] = upper[d * per : (d + 1) * per, :]
        low[at, :] = lower[d * per : (d + 1) * per, :]
    copies[2].wait()
    for h in range(q.shape[1] // HEAD):
        stacked[h * span : (h + 1) * span, :] = q_vmem[:, h * HEAD : (h + 1) * HEAD]


GROUP = 4


def attend(q, kv, bias, span, finish):
    scale = math.log2(math.e) / math.sqrt(HEAD)
    keys = kv.shape[0]
    group = min(GROUP, q.shape[0] // span)
    rows = group * span
    for g in range(q.shape[0] // rows):
        scores = dot_t(q[g * rows : (g + 1) * rows, :], kv[:, :HEAD])
        scores = (scores.reshape(group, span, keys) + bias[...][None]).reshape(rows, keys)
        top = jnp.max(scores, axis=1, keepdims=True)
        probs = jnp.exp2((scores - top) * scale)
        total = jnp.sum(probs, axis=1, keepdims=True)
        out = dot(probs.astype(bf16), kv[:, HEAD:])
        finish(g, rows, group, out, top, total)


def attend_first(span, q, kv, bias, o_out, m_out, l_out):
    def finish(g, rows, group, out, top, total):
        at = pl.ds(g * rows, rows)
        o_out[at, :] = out
        m_out[at, :] = jnp.broadcast_to(top, (rows, LANES))
        l_out[at, :] = jnp.broadcast_to(total, (rows, LANES))

    attend(q, kv, bias, span, finish)


def attend_second(span, q, kv, bias, o_in, m_in, l_in, result):
    scale = math.log2(math.e) / math.sqrt(HEAD)

    def finish(g, rows, group, out, top, total):
        at = pl.ds(g * rows, rows)
        first = m_in[at, :]
        both = jnp.maximum(first, top)
        w_first = jnp.exp2((first - both) * scale)
        w_second = jnp.exp2((top - both) * scale)
        norm = l_in[at, :] * w_first + total * w_second
        merged = ((o_in[at, :] * w_first + out * w_second) / norm).astype(bf16)
        for h in range(group):
            col = (g * group + h) * HEAD
            result[:, col : col + HEAD] = merged[h * span : (h + 1) * span, :]

    attend(q, kv, bias, span, finish)


def project_first(heads_out, weight, out):
    out[...] = dot(heads_out[...], weight[...])


def project_second(n_exp, span, heads_out, weight, first, residual, *refs):
    ranks = refs[:n_exp]
    own_out = refs[n_exp]
    part_outs = refs[n_exp + 1 : 2 * n_exp]
    pick_outs = refs[2 * n_exp : 3 * n_exp]
    whole, picked = refs[3 * n_exp :]
    ctx, exp = lax.axis_index("ctx"), lax.axis_index("exp")
    second = dot(heads_out[...], weight[...])
    for k in range(heads_out.shape[0] // span):
        here = slice(k * span, (k + 1) * span)
        whole[rows_at(jnp.bitwise_xor(ctx, 2 * k) * span, span, span), :] = first[here, :]
        whole[rows_at(jnp.bitwise_xor(ctx, 2 * k + 1) * span, span, span), :] = second[here, :]
    tokens = residual.shape[0]
    flight = ranks[0].shape[0]
    local = flight // n_exp
    slot = lax.broadcasted_iota(jnp.int32, (CAP, tokens), 0).astype(f32)
    for k in range(n_exp):
        block = jnp.bitwise_xor(exp, k)
        part = whole[rows_at(block * tokens, tokens, tokens), :]
        if k == 0:
            part = part + residual[...].astype(f32)
            own_out[...] = part
        narrow = part.astype(bf16)
        if k > 0:
            part_outs[k - 1][...] = narrow
        rank = ranks[k][...]
        table = jnp.concatenate(
            [jnp.where(rank[e : e + 1, :] == slot, 1.0, 0.0) for e in range(flight)], axis=0
        ).astype(bf16)
        rows = dot(table, narrow).astype(bf16)
        for e in range(flight):
            at = (e % local) * n_exp * CAP + block * CAP
            picked[e // local, rows_at(at, CAP, CAP), :] = rows[e * CAP : (e + 1) * CAP, :]
    for k in range(n_exp):
        pick_outs[k][...] = picked[jnp.bitwise_xor(exp, k)]


def split_square(square):
    lane = lax.broadcasted_iota(jnp.int32, (square.shape[0], LANES), 1)
    high = square.astype(bf16).astype(f32)
    return jnp.where(lane == 0, high, jnp.where(lane == 1, square - high, 0.0))


def expert_in_kernel(n_exp, other, *refs):
    arrived = refs[:n_exp]
    gain, weight, out = refs[n_exp:]
    expert = jnp.bitwise_xor(lax.axis_index("ctx") % 2, other)
    rows = out.shape[0]
    width = weight.shape[2]
    at = rows_at(expert * rows, rows, rows)
    total = arrived[0][at, :].astype(f32)
    for ref in arrived[1:]:
        total = total + ref[at, :].astype(f32)
    mixed = total.astype(bf16).astype(f32)
    out[:, width:] = split_square(jnp.sum(mixed * mixed, axis=1, keepdims=True)).astype(out.dtype)
    scaled = (mixed * gain[...]).astype(bf16)
    step = width // 6
    for n in range(0, width, step):
        out[:, n : n + step] = dot(scaled, weight[expert, :, n : n + step]).astype(out.dtype)


def chip_sum(mine, theirs, *outs):
    chip = lax.axis_index("ctx") // 2
    width = mine.shape[1] - LANES
    size = outs[0].shape[0]
    for k, out in enumerate(outs):
        at = rows_at(jnp.bitwise_xor(chip, k) * size, size, size)
        total = mine[at, :] + theirs[at, :].astype(f32)
        out[:, :width] = total[:, :width].astype(bf16)
        out[:, width:] = split_square(
            jnp.sum(total[:, width:], axis=1, keepdims=True)
        ).astype(bf16)


def activate(features, *refs):
    out = refs[-1]
    total = refs[0][...].astype(f32)
    for ref in refs[1:-1]:
        total = total + ref[...].astype(f32)
    hidden = out.shape[1]
    square = jnp.sum(total[:, 2 * hidden :], axis=1, keepdims=True)
    inverse = lax.rsqrt(square / features + eps_norm)
    gate = total[:, :hidden] * inverse
    up = total[:, hidden : 2 * hidden] * inverse
    out[...] = (gate / (1.0 + jnp.exp(-gate)) * up).astype(bf16)


def expert_out_first(active, weight, out):
    out[...] = dot(active[...], weight[lax.axis_index("ctx") % 2]).astype(bf16)


def expert_out_second(n_exp, active, weight, first, *refs):
    outs, whole = refs[:n_exp], refs[n_exp]
    ctx, exp = lax.axis_index("ctx"), lax.axis_index("exp")
    core, chip = ctx % 2, ctx // 2
    chips = lax.axis_size("ctx") // 2
    size = active.shape[0] // chips
    second = dot(active[...], weight[1 - core]).astype(bf16)
    for k in range(chips):
        at = rows_at(jnp.bitwise_xor(chip, k) * size, size, size)
        here = slice(k * size, (k + 1) * size)
        whole[core, at, :] = first[here, :]
        whole[1 - core, at, :] = second[here, :]
    for k in range(n_exp):
        at = rows_at(jnp.bitwise_xor(exp, k) * CAP, CAP, CAP)
        for j in range(whole.shape[0]):
            outs[k][j * CAP : (j + 1) * CAP, :] = whole[j, at, :]


def combine(n_exp, high, low, own, *refs):
    parts, returned = refs[: n_exp - 1], refs[n_exp - 1 : -2]
    mixed, out = refs[-2:]
    total = own[...]
    for part in parts:
        total = total + part[...].astype(f32)
    mixed[...] = total.astype(bf16)
    rows = jnp.concatenate([ref[...] for ref in returned], axis=0)
    dims = (((0,), (0,)), ((), ()))
    out[...] = (
        lax.dot_general(high[...], rows, dims, preferred_element_type=f32)
        + lax.dot_general(low[...], rows, dims, preferred_element_type=f32)
    ).astype(bf16)


def permute(x, axis, k):
    n = lax.axis_size(axis)
    return lax.ppermute(x, axis, [(i, i ^ k) for i in range(n)])


def body(
    queries,
    cache_keys,
    cache_values,
    block_keys,
    block_values,
    seg_starts,
    out_weight,
    residual,
    norm_gain,
    routes,
    gate_values,
    expert_in,
    expert_out,
):
    n_ctx, n_exp = lax.axis_size("ctx"), lax.axis_size("exp")
    chips = n_ctx // 2
    span = queries.shape[0]
    heads = queries.shape[1] // HEAD
    cache = cache_keys.shape[0]
    tokens = routes.shape[0]
    local, features, width = expert_in.shape
    hidden = width // 2
    columns = out_weight.shape[1]
    flight = n_exp * local

    def over_chips(x):
        return [permute(x, "ctx", 2 * k) for k in range(1, chips)]

    def over_exp(xs):
        return [permute(x, "exp", k) for k, x in zip(range(1, n_exp), xs)]

    local_kv = call(
        functools.partial(pick_kv, heads),
        shape((cache + span, 2 * HEAD), bf16),
        [HBM] * 4,
        [pltpu.SemaphoreType.DMA((4,))],
        vmem=ALL_VMEM,
    )(cache_keys, cache_values, block_keys, block_values)
    kv_moved = over_chips(local_kv)

    rows, keys = heads * span, chips * (cache + span)
    stacked, bias_same, bias_other, rank, high, low = call(
        functools.partial(prepare, n_exp, span, cache),
        [shape((rows, HEAD), bf16)]
        + [shape((span, keys), f32)] * 2
        + [shape((flight, tokens), f32)]
        + [shape((flight * CAP, tokens), bf16)] * 2,
        [SMEM] + [HBM] * 3,
        [
            pltpu.VMEM(queries.shape, bf16),
            pltpu.VMEM(routes.shape[::-1], jnp.int32),
            pltpu.VMEM(routes.shape[::-1], f32),
            pltpu.SemaphoreType.DMA((3,)),
        ],
        vmem=8,
        nbytes=MIB,
    )(seg_starts, queries, routes.T, gate_values.T)
    moved = over_exp([rank] * (n_exp - 1))
    kv_moved, stacked = lax.optimization_barrier((kv_moved, stacked))
    kv_same = jnp.concatenate([local_kv] + kv_moved, axis=0)
    kv_other = permute(kv_same, "ctx", 1)

    cost = dict(flops=4 * rows * keys * HEAD, nbytes=4 * MIB)
    stats = call(
        functools.partial(attend_first, span),
        [shape((rows, HEAD), f32), shape((rows, LANES), f32), shape((rows, LANES), f32)],
        [VMEM] * 3,
        vmem=24,
        **cost,
    )(stacked, kv_same, bias_same)
    kv_other, moved = lax.optimization_barrier((kv_other, moved))
    ranks = [rank] + moved
    heads_out = call(
        functools.partial(attend_second, span),
        shape((span, heads * HEAD), bf16),
        [VMEM] * 6,
        vmem=24,
        **cost,
    )(stacked, kv_other, bias_other, *stats)

    heads_same = jnp.concatenate([heads_out] + over_chips(heads_out), axis=0)
    heads_other = permute(heads_same, "ctx", 1)
    cost = dict(
        flops=2 * heads_same.shape[0] * heads_same.shape[1] * columns, nbytes=4 * MIB
    )
    first = call(
        project_first,
        shape((heads_same.shape[0], columns), f32),
        [VMEM] * 2,
        vmem=16,
        **cost,
    )(heads_same, out_weight)
    per_exp = local * n_exp * CAP
    outs = call(
        functools.partial(project_second, n_exp, span),
        [shape((tokens, columns), f32)]
        + [shape((tokens, columns), bf16)] * (n_exp - 1)
        + [shape((per_exp, columns), bf16)] * n_exp,
        [VMEM] * (4 + n_exp),
        [
            pltpu.VMEM((n_ctx * span, columns), f32),
            pltpu.VMEM((n_exp, per_exp, columns), bf16),
        ],
        vmem=24,
        **cost,
    )(heads_other, out_weight, first, residual, *ranks)
    own, parts, picks = outs[0], outs[1:n_exp], outs[n_exp:]
    arrived = [picks[0]] + over_exp(picks[1:])

    gain = norm_gain.reshape(1, features)
    expert_rows = n_exp * CAP

    def gate_up(other, dtype):
        return call(
            functools.partial(expert_in_kernel, n_exp, other),
            shape((expert_rows, width + LANES), dtype),
            [VMEM] * (n_exp + 2),
            vmem=16,
            flops=2 * expert_rows * features * width,
            nbytes=4 * MIB,
        )(*arrived, gain, expert_in)

    sent = gate_up(1, bf16)
    theirs = permute(sent, "ctx", 1)
    mine = gate_up(0, f32)

    size = expert_rows // chips
    chunk = call(
        chip_sum,
        [shape((size, width + LANES), bf16)] * chips,
        [VMEM] * 2,
        vmem=8,
    )(mine, theirs)
    order = [k for k in range(2, n_exp)] + [1]
    share = -(-len(order) // 3)
    turns = [order[:share], order[share : 2 * share], order[2 * share :]]
    moved_parts = {}

    def beside(turn, ready, step):
        ready, sent = lax.optimization_barrier((ready, [parts[k - 1] for k in turns[turn]]))
        got = [permute(x, "exp", k) for k, x in zip(turns[turn], sent)]
        done, got = lax.optimization_barrier((step(ready), got))
        moved_parts.update(zip(turns[turn], got))
        return ready, done

    chunk, gathered = beside(
        0, chunk, lambda c: [permute(c[k], "ctx", 2 * k) for k in range(1, chips)]
    )
    active = call(
        functools.partial(activate, n_ctx * features),
        shape((size, hidden), bf16),
        [VMEM] * chips,
        vmem=8,
    )(chunk[0], *gathered)
    active, gathered = beside(1, active, over_chips)
    active_same = jnp.concatenate([active] + gathered, axis=0)
    active_other = permute(active_same, "ctx", 1)
    cost = dict(flops=2 * expert_rows * hidden * columns, nbytes=2 * MIB)
    made = call(
        expert_out_first,
        shape((expert_rows, columns), bf16),
        [VMEM] * 2,
        vmem=8,
        **cost,
    )(active_same, expert_out)
    produced = call(
        functools.partial(expert_out_second, n_exp),
        [shape((local * CAP, columns), bf16)] * n_exp,
        [VMEM] * 3,
        [pltpu.VMEM((local, expert_rows, columns), bf16)],
        vmem=8,
        **cost,
    )(active_other, expert_out, made)
    produced, returned = beside(2, produced, lambda x: over_exp(x[1:]))
    mixed, expert_sum = call(
        functools.partial(combine, n_exp),
        [shape((tokens, columns), bf16)] * 2,
        [VMEM] * (2 + 2 * n_exp),
        vmem=8,
    )(high, low, own, *[moved_parts[k] for k in range(1, n_exp)], produced[0], *returned)
    return (mixed, expert_sum)


def solution(mesh):
    placed = (
        P("ctx", "exp"),
        P("ctx", None),
        P("ctx", None),
        P("ctx", None),
        P("ctx", None),
        P(),
        P("exp", "ctx"),
        P("exp", "ctx"),
        P("ctx"),
        P("exp", None),
        P("exp", None),
        P("exp", "ctx", None),
        P("exp", None, "ctx"),
    )
    return jax.shard_map(
        body,
        mesh=mesh,
        in_specs=placed,
        out_specs=(P("exp", "ctx"), P("exp", "ctx")),
        check_vma=False,
    )
```

```python
import functools
import math

import jax
import jax.numpy as jnp
from jax import lax
from jax.experimental import pallas as pl
from jax.experimental.pallas import tpu as pltpu
from jax.sharding import PartitionSpec as P

QHEADS = 64
KVH = 4
HEAD = 128
CAP = 16
LANES = 128

neg_large = -1e30
eps_norm = 1e-06
bf16 = jnp.bfloat16
f32 = jnp.float32
MIB = 1024 * 1024
ALL_VMEM = 63.5

VMEM = pl.BlockSpec(memory_space=pltpu.VMEM)
SMEM = pl.BlockSpec(memory_space=pltpu.SMEM)
HBM = pl.BlockSpec(memory_space=pltpu.HBM)


def call(kernel, out_shape, in_specs, scratch=(), vmem=16, flops=0, nbytes=0):
    many = isinstance(out_shape, (list, tuple))
    return pl.pallas_call(
        kernel,
        out_shape=out_shape,
        in_specs=in_specs,
        out_specs=[VMEM] * len(out_shape) if many else VMEM,
        scratch_shapes=list(scratch),
        compiler_params=pltpu.CompilerParams(vmem_limit_bytes=int(vmem * MIB)),
        cost_estimate=pl.CostEstimate(flops=flops, bytes_accessed=nbytes, transcendentals=0),
    )


def shape(dims, dtype):
    return jax.ShapeDtypeStruct(dims, dtype)


def dot(a, b):
    return lax.dot_general(a, b, (((1,), (0,)), ((), ())), preferred_element_type=f32)


def dot_t(a, b):
    return lax.dot_general(a, b, (((1,), (1,)), ((), ())), preferred_element_type=f32)


def rows_at(start, size, step):
    return pl.ds(pl.multiple_of(start, step), size)


def pick_kv(local_heads, ck, cv, bk, bv, out, sems):
    kv = lax.axis_index("exp") * local_heads // (QHEADS // KVH)
    cols = rows_at(kv * HEAD, HEAD, HEAD)
    cache, span = ck.shape[0], bk.shape[0]
    copies = []
    for n, (src, row, size, col) in enumerate(
        ((ck, 0, cache, 0), (cv, 0, cache, HEAD), (bk, cache, span, 0), (bv, cache, span, HEAD))
    ):
        copies.append(
            pltpu.make_async_copy(
                src.at[:, cols], out.at[pl.ds(row, size), pl.ds(col, HEAD)], sems.at[n]
            )
        )
    for copy in copies:
        copy.start()
    for copy in copies:
        copy.wait()


def segment_of(position, seg_starts):
    passed = jnp.full(position.shape, -1, jnp.int32)
    for n in range(seg_starts.shape[0]):
        passed = passed + jnp.where(seg_starts[n] <= position, 1, 0)
    return passed


def mask_bias(seg_starts, other, span, cache, pieces):
    ctx = lax.axis_index("ctx")
    cache_total = cache * lax.axis_size("ctx")
    piece_rows = cache + span
    keys = pieces * piece_rows
    index = lax.broadcasted_iota(jnp.int32, (1, keys), 1)
    key_pos = jnp.zeros((1, keys), jnp.int32)
    for k in range(pieces):
        owner = jnp.bitwise_xor(ctx, 2 * k + other)
        off = index - k * piece_rows
        pos = jnp.where(off < cache, owner * cache + off, cache_total + owner * span + off - cache)
        key_pos = pos if k == 0 else jnp.where(off >= 0, pos, key_pos)
    key_seg = segment_of(key_pos, seg_starts)
    query_pos = cache_total + ctx * span + lax.broadcasted_iota(jnp.int32, (span, 1), 0)
    query_seg = segment_of(query_pos, seg_starts)
    last = seg_starts.shape[0] - 1
    seen = (key_pos <= query_pos) & (
        (key_seg == query_seg) | (key_seg == 0) | (query_seg == last)
    )
    return jnp.where(seen, 0.0, neg_large)


def mask_kernel(span, cache, seg_starts, bias_same, bias_other):
    pieces = bias_same.shape[1] // (cache + span)
    bias_same[...] = mask_bias(seg_starts, 0, span, cache, pieces)
    bias_other[...] = mask_bias(seg_starts, 1, span, cache, pieces)


def route_kernel(n_exp, routes, gates, rank, high, low):
    flight, tokens = rank.shape
    local = flight // n_exp
    expert = lax.broadcasted_iota(jnp.int32, (flight, tokens), 0)
    member = jnp.zeros((flight, tokens), f32)
    weight = jnp.zeros((flight, tokens), f32)
    for k in range(routes.shape[0]):
        hit = routes[k : k + 1, :] == expert
        member = jnp.where(hit, 1.0, member)
        weight = weight + jnp.where(hit, gates[k : k + 1, :], 0.0)
    before = lax.broadcasted_iota(jnp.int32, (tokens, tokens), 0) < lax.broadcasted_iota(
        jnp.int32, (tokens, tokens), 1
    )
    count = dot(member.astype(bf16), jnp.where(before, 1.0, 0.0).astype(bf16))
    slots = jnp.where(member > 0.5, count, -1.0)
    rank[...] = slots
    exp = lax.axis_index("exp")
    slot = lax.broadcasted_iota(jnp.int32, (CAP, tokens), 0).astype(f32)
    tables = []
    for e in range(flight):
        tables.append(jnp.where(slots[e : e + 1, :] == slot, weight[e : e + 1, :], 0.0))
    per = local * CAP
    table = jnp.concatenate(tables, axis=0)
    upper = table.astype(bf16)
    lower = (table - upper.astype(f32)).astype(bf16)
    for d in range(n_exp):
        at = pl.ds(pl.multiple_of(jnp.bitwise_xor(exp, d) * per, per), per)
        high[at, :] = upper[d * per : (d + 1) * per, :]
        low[at, :] = lower[d * per : (d + 1) * per, :]


GROUP = 4


def attend(q, kv, bias, span, finish):
    scale = math.log2(math.e) / math.sqrt(HEAD)
    keys = kv.shape[0]
    group = min(GROUP, q.shape[0] // span)
    rows = group * span
    for g in range(q.shape[0] // rows):
        scores = dot_t(q[g * rows : (g + 1) * rows, :], kv[:, :HEAD])
        scores = (scores.reshape(group, span, keys) + bias[...][None]).reshape(rows, keys)
        top = jnp.max(scores, axis=1, keepdims=True)
        probs = jnp.exp2((scores - top) * scale)
        total = jnp.sum(probs, axis=1, keepdims=True)
        out = dot(probs.astype(bf16), kv[:, HEAD:])
        finish(g, rows, group, out, top, total)


def attend_first(span, q, kv, bias, o_out, m_out, l_out):
    def finish(g, rows, group, out, top, total):
        at = pl.ds(g * rows, rows)
        o_out[at, :] = out
        m_out[at, :] = jnp.broadcast_to(top, (rows, LANES))
        l_out[at, :] = jnp.broadcast_to(total, (rows, LANES))

    attend(q, kv, bias, span, finish)


def attend_second(span, q, kv, bias, o_in, m_in, l_in, *results):
    scale = math.log2(math.e) / math.sqrt(HEAD)
    half = results[0].shape[1] // HEAD

    def finish(g, rows, group, out, top, total):
        at = pl.ds(g * rows, rows)
        first = m_in[at, :]
        both = jnp.maximum(first, top)
        w_first = jnp.exp2((first - both) * scale)
        w_second = jnp.exp2((top - both) * scale)
        norm = l_in[at, :] * w_first + total * w_second
        merged = ((o_in[at, :] * w_first + out * w_second) / norm).astype(bf16)
        for h in range(group):
            head = g * group + h
            result = results[head // half]
            col = head % half * HEAD
            result[:, col : col + HEAD] = merged[h * span : (h + 1) * span, :]

    attend(q, kv, bias, span, finish)


def project_first(heads_out, weight, out):
    out[...] = dot(heads_out[...], weight[...])


def project_second(n_exp, span, heads_out, weight, first, residual, ranks, *refs):
    own_out, odd_out = refs[:2]
    even_outs = refs[2 : n_exp // 2 + 1]
    pick_outs = refs[n_exp // 2 + 1 : -2]
    whole, picked = refs[-2:]
    ctx, exp = lax.axis_index("ctx"), lax.axis_index("exp")
    second = dot(heads_out[...], weight[...])
    for k in range(heads_out.shape[0] // span):
        here = slice(k * span, (k + 1) * span)
        whole[rows_at(jnp.bitwise_xor(ctx, 2 * k) * span, span, span), :] = first[here, :]
        whole[rows_at(jnp.bitwise_xor(ctx, 2 * k + 1) * span, span, span), :] = second[here, :]
    tokens = residual.shape[0]
    flight = ranks.shape[0] // n_exp
    local = flight // n_exp
    slot = lax.broadcasted_iota(jnp.int32, (CAP, tokens), 0).astype(f32)
    for k in range(n_exp):
        block = jnp.bitwise_xor(exp, k)
        part = whole[rows_at(block * tokens, tokens, tokens), :]
        if k == 0:
            part = part + residual[...].astype(f32)
            own_out[...] = part
        narrow = part.astype(bf16)
        if k % 2:
            odd_out[k // 2 * tokens : (k // 2 + 1) * tokens, :] = narrow
        elif k:
            even_outs[k // 2 - 1][...] = narrow
        rank = ranks[k * flight : (k + 1) * flight, :]
        table = jnp.concatenate(
            [jnp.where(rank[e : e + 1, :] == slot, 1.0, 0.0) for e in range(flight)], axis=0
        ).astype(bf16)
        rows = dot(table, narrow).astype(bf16)
        for e in range(flight):
            at = (e % local) * n_exp * CAP + block * CAP
            picked[e // local, rows_at(at, CAP, CAP), :] = rows[e * CAP : (e + 1) * CAP, :]
    for k in range(n_exp):
        pick_outs[k][...] = picked[jnp.bitwise_xor(exp, k)]


def split_square(square):
    lane = lax.broadcasted_iota(jnp.int32, (square.shape[0], LANES), 1)
    high = square.astype(bf16).astype(f32)
    return jnp.where(lane == 0, high, jnp.where(lane == 1, square - high, 0.0))


def expert_in_kernel(n_exp, other, *refs):
    arrived = refs[:n_exp]
    gain, weight, out = refs[n_exp:]
    expert = jnp.bitwise_xor(lax.axis_index("ctx") % 2, other)
    rows = out.shape[0]
    width = weight.shape[2]
    at = rows_at(expert * rows, rows, rows)
    total = arrived[0][at, :].astype(f32)
    for ref in arrived[1:]:
        total = total + ref[at, :].astype(f32)
    mixed = total.astype(bf16).astype(f32)
    out[:, width:] = split_square(jnp.sum(mixed * mixed, axis=1, keepdims=True)).astype(out.dtype)
    scaled = (mixed * gain[...]).astype(bf16)
    step = width // 6
    for n in range(0, width, step):
        out[:, n : n + step] = dot(scaled, weight[expert, :, n : n + step]).astype(out.dtype)


def chip_sum(mine, theirs, *outs):
    chip = lax.axis_index("ctx") // 2
    width = mine.shape[1] - LANES
    size = outs[0].shape[0]
    for k, out in enumerate(outs):
        at = rows_at(jnp.bitwise_xor(chip, k) * size, size, size)
        total = mine[at, :] + theirs[at, :].astype(f32)
        out[:, :width] = total[:, :width].astype(bf16)
        out[:, width:] = split_square(
            jnp.sum(total[:, width:], axis=1, keepdims=True)
        ).astype(bf16)


def activate(features, *refs):
    out = refs[-1]
    total = refs[0][...].astype(f32)
    for ref in refs[1:-1]:
        total = total + ref[...].astype(f32)
    hidden = out.shape[1]
    square = jnp.sum(total[:, 2 * hidden :], axis=1, keepdims=True)
    inverse = lax.rsqrt(square / features + eps_norm)
    gate = total[:, :hidden] * inverse
    up = total[:, hidden : 2 * hidden] * inverse
    out[...] = (gate / (1.0 + jnp.exp(-gate)) * up).astype(bf16)


def expert_out_first(active, weight, out):
    out[...] = dot(active[...], weight[lax.axis_index("ctx") % 2]).astype(bf16)


def expert_out_second(n_exp, active, weight, first, *refs):
    outs, whole = refs[:n_exp], refs[n_exp]
    ctx, exp = lax.axis_index("ctx"), lax.axis_index("exp")
    core, chip = ctx % 2, ctx // 2
    chips = lax.axis_size("ctx") // 2
    size = active.shape[0] // chips
    second = dot(active[...], weight[1 - core]).astype(bf16)
    for k in range(chips):
        at = rows_at(jnp.bitwise_xor(chip, k) * size, size, size)
        here = slice(k * size, (k + 1) * size)
        whole[core, at, :] = first[here, :]
        whole[1 - core, at, :] = second[here, :]
    for k in range(n_exp):
        at = rows_at(jnp.bitwise_xor(exp, k) * CAP, CAP, CAP)
        for j in range(whole.shape[0]):
            outs[k][j * CAP : (j + 1) * CAP, :] = whole[j, at, :]


def combine(high, low, own, odd, *refs):
    n_exp = high.shape[0] // refs[0].shape[0]
    returned, parts = refs[:n_exp], refs[n_exp:-2]
    mixed, out = refs[-2:]
    total = own[...] + odd[: own.shape[0], :].astype(f32)
    for part in parts:
        total = total + part[...].astype(f32)
    mixed[...] = total.astype(bf16)
    rows = jnp.concatenate([ref[...] for ref in returned], axis=0)
    dims = (((0,), (0,)), ((), ()))
    out[...] = (
        lax.dot_general(high[...], rows, dims, preferred_element_type=f32)
        + lax.dot_general(low[...], rows, dims, preferred_element_type=f32)
    ).astype(bf16)


def permute(x, axis, k):
    n = lax.axis_size(axis)
    return lax.ppermute(x, axis, [(i, i ^ k) for i in range(n)])


def gather_halves(halves, chips):
    low, high = halves
    if chips != 4:
        return [[low, high]] + [
            [permute(low, "ctx", 2 * k), permute(high, "ctx", 2 * k)] for k in range(1, chips)
        ]
    x_low, y_high = permute(low, "ctx", 2), permute(high, "ctx", 4)
    x_high, y_low = permute(high, "ctx", 2), permute(low, "ctx", 4)
    far_low, far_high = permute(x_low, "ctx", 4), permute(y_high, "ctx", 2)
    return [[low, high], [x_low, x_high], [y_low, y_high], [far_low, far_high]]


def body(
    queries,
    cache_keys,
    cache_values,
    block_keys,
    block_values,
    seg_starts,
    out_weight,
    residual,
    norm_gain,
    routes,
    gate_values,
    expert_in,
    expert_out,
):
    n_ctx, n_exp = lax.axis_size("ctx"), lax.axis_size("exp")
    chips = n_ctx // 2
    span = queries.shape[0]
    heads = queries.shape[1] // HEAD
    cache = cache_keys.shape[0]
    tokens = routes.shape[0]
    local, features, width = expert_in.shape
    hidden = width // 2
    columns = out_weight.shape[1]
    flight = n_exp * local

    def over_chips(x):
        return [permute(x, "ctx", 2 * k) for k in range(1, chips)]

    def over_exp(xs):
        return [permute(x, "exp", k) for k, x in zip(range(1, n_exp), xs)]

    local_kv = call(
        functools.partial(pick_kv, heads),
        shape((cache + span, 2 * HEAD), bf16),
        [HBM] * 4,
        [pltpu.SemaphoreType.DMA((4,))],
        vmem=ALL_VMEM,
    )(cache_keys, cache_values, block_keys, block_values)
    kv_moved = over_chips(local_kv)

    rows, keys = heads * span, chips * (cache + span)
    bias_same, bias_other = call(
        functools.partial(mask_kernel, span, cache),
        [shape((span, keys), f32)] * 2,
        [SMEM],
        vmem=8,
        nbytes=MIB,
    )(seg_starts)
    stacked = queries.reshape(span, heads, HEAD).transpose(1, 0, 2).reshape(rows, HEAD)
    rank, high, low = call(
        functools.partial(route_kernel, n_exp),
        [shape((flight, tokens), f32)] + [shape((flight * CAP, tokens), bf16)] * 2,
        [VMEM] * 2,
        vmem=8,
    )(routes.T, gate_values.T)
    kv_moved, stacked, bias_same, bias_other, rank = lax.optimization_barrier(
        (kv_moved, stacked, bias_same, bias_other, rank)
    )
    kv_same = jnp.concatenate([local_kv] + kv_moved, axis=0)
    kv_other = permute(kv_same, "ctx", 1)

    cost = dict(flops=4 * rows * keys * HEAD, nbytes=4 * MIB)
    stats = call(
        functools.partial(attend_first, span),
        [shape((rows, HEAD), f32), shape((rows, LANES), f32), shape((rows, LANES), f32)],
        [VMEM] * 3,
        vmem=24,
        **cost,
    )(stacked, kv_same, bias_same)
    halves = call(
        functools.partial(attend_second, span),
        [shape((span, rows // span * HEAD // 2), bf16)] * 2,
        [VMEM] * 6,
        vmem=24,
        **cost,
    )(stacked, kv_other, bias_other, *stats)

    halves, ranks = lax.optimization_barrier((halves, rank))
    step = 1
    while step < n_exp:
        ranks = jnp.concatenate([ranks, permute(ranks, "exp", step)], axis=0)
        step *= 2
    pieces = gather_halves(halves, chips)
    pieces, ranks = lax.optimization_barrier((pieces, ranks))
    heads_same = jnp.concatenate([jnp.concatenate(pair, axis=1) for pair in pieces], axis=0)
    heads_other = permute(heads_same, "ctx", 1)
    cost = dict(
        flops=2 * heads_same.shape[0] * heads_same.shape[1] * columns, nbytes=4 * MIB
    )
    first = call(
        project_first,
        shape((heads_same.shape[0], columns), f32),
        [VMEM] * 2,
        vmem=16,
        **cost,
    )(heads_same, out_weight)
    per_exp = local * n_exp * CAP
    outs = call(
        functools.partial(project_second, n_exp, span),
        [shape((tokens, columns), f32)]
        + [shape((n_exp // 2 * tokens, columns), bf16)]
        + [shape((tokens, columns), bf16)] * (n_exp // 2 - 1)
        + [shape((per_exp, columns), bf16)] * n_exp,
        [VMEM] * 5,
        [
            pltpu.VMEM((n_ctx * span, columns), f32),
            pltpu.VMEM((n_exp, per_exp, columns), bf16),
        ],
        vmem=24,
        **cost,
    )(heads_other, out_weight, first, residual, ranks)
    own, odd, even, picks = outs[0], outs[1], outs[2 : n_exp // 2 + 1], outs[n_exp // 2 + 1 :]
    passed = [permute(picks[2 * k + 1], "exp", 1) for k in range(1, n_exp // 2)]
    arrived = [picks[0], permute(picks[1], "exp", 1)]
    for k, got in enumerate(passed, 1):
        pair = (picks[2 * k].astype(f32) + got.astype(f32)).astype(bf16)
        arrived.append(permute(pair, "exp", 2 * k))

    gain = norm_gain.reshape(1, features)
    expert_rows = n_exp * CAP

    def gate_up(other, dtype):
        return call(
            functools.partial(expert_in_kernel, len(arrived), other),
            shape((expert_rows, width + LANES), dtype),
            [VMEM] * (len(arrived) + 2),
            vmem=16,
            flops=2 * expert_rows * features * width,
            nbytes=4 * MIB,
        )(*arrived, gain, expert_in)

    sent = gate_up(1, bf16)
    theirs = permute(sent, "ctx", 1)
    mine = gate_up(0, f32)

    size = expert_rows // chips
    chunk = call(
        chip_sum,
        [shape((size, width + LANES), bf16)] * chips,
        [VMEM] * 2,
        vmem=8,
    )(mine, theirs)
    def beside(ready, sent, step, exchange):
        ready, sent = lax.optimization_barrier((ready, sent))
        return (ready, *lax.optimization_barrier((step(ready), exchange(sent))))

    chunk, gathered, odd = beside(
        chunk,
        odd,
        lambda c: [permute(c[k], "ctx", 2 * k) for k in range(1, chips)],
        lambda x: permute(x, "exp", 1),
    )
    active = call(
        functools.partial(activate, n_ctx * features),
        shape((size, hidden), bf16),
        [VMEM] * chips,
        vmem=8,
    )(chunk[0], *gathered)
    even = [
        (x.astype(f32) + odd[k * tokens : (k + 1) * tokens].astype(f32)).astype(bf16)
        for k, x in enumerate(even, 1)
    ]
    active, gathered, even = beside(
        active,
        even,
        over_chips,
        lambda xs: [permute(x, "exp", 2 * k) for k, x in enumerate(xs, 1)],
    )
    active_same = jnp.concatenate([active] + gathered, axis=0)
    active_other = permute(active_same, "ctx", 1)
    cost = dict(flops=2 * expert_rows * hidden * columns, nbytes=2 * MIB)
    made = call(
        expert_out_first,
        shape((expert_rows, columns), bf16),
        [VMEM] * 2,
        vmem=8,
        **cost,
    )(active_same, expert_out)
    produced = call(
        functools.partial(expert_out_second, n_exp),
        [shape((local * CAP, columns), bf16)] * n_exp,
        [VMEM] * 3,
        [pltpu.VMEM((local, expert_rows, columns), bf16)],
        vmem=8,
        **cost,
    )(active_other, expert_out, made)
    returned = over_exp(produced[1:])
    mixed, expert_sum = call(
        combine,
        [shape((tokens, columns), bf16)] * 2,
        [VMEM] * (4 + n_exp + len(even)),
        vmem=8,
    )(high, low, own, odd, produced[0], *returned, *even)
    return (mixed, expert_sum)


def solution(mesh):
    placed = (
        P("ctx", "exp"),
        P("ctx", None),
        P("ctx", None),
        P("ctx", None),
        P("ctx", None),
        P(),
        P("exp", "ctx"),
        P("exp", "ctx"),
        P("ctx"),
        P("exp", None),
        P("exp", None),
        P("exp", "ctx", None),
        P("exp", None, "ctx"),
    )
    return jax.shard_map(
        body,
        mesh=mesh,
        in_specs=placed,
        out_specs=(P("exp", "ctx"), P("exp", "ctx")),
        check_vma=False,
    )
```

```python
import functools
import math

import jax
import jax.numpy as jnp
from jax import lax
from jax.experimental import pallas as pl
from jax.experimental.pallas import tpu as pltpu
from jax.sharding import PartitionSpec as P

QHEADS = 64
KVH = 4
HEAD = 128
CAP = 16
LANES = 128

neg_large = -1e30
eps_norm = 1e-06
bf16 = jnp.bfloat16
f32 = jnp.float32
MIB = 1024 * 1024
ALL_VMEM = 63.5

VMEM = pl.BlockSpec(memory_space=pltpu.VMEM)
SMEM = pl.BlockSpec(memory_space=pltpu.SMEM)
HBM = pl.BlockSpec(memory_space=pltpu.HBM)


def call(kernel, out_shape, in_specs, scratch=(), vmem=16, flops=0, nbytes=0):
    many = isinstance(out_shape, (list, tuple))
    return pl.pallas_call(
        kernel,
        out_shape=out_shape,
        in_specs=in_specs,
        out_specs=[VMEM] * len(out_shape) if many else VMEM,
        scratch_shapes=list(scratch),
        compiler_params=pltpu.CompilerParams(vmem_limit_bytes=int(vmem * MIB)),
        cost_estimate=pl.CostEstimate(flops=flops, bytes_accessed=nbytes, transcendentals=0),
    )


def shape(dims, dtype):
    return jax.ShapeDtypeStruct(dims, dtype)


def dot(a, b):
    return lax.dot_general(a, b, (((1,), (0,)), ((), ())), preferred_element_type=f32)


def dot_t(a, b):
    return lax.dot_general(a, b, (((1,), (1,)), ((), ())), preferred_element_type=f32)


def rows_at(start, size, step):
    return pl.ds(pl.multiple_of(start, step), size)


def pick_kv(local_heads, ck, cv, bk, bv, out, sems):
    kv = lax.axis_index("exp") * local_heads // (QHEADS // KVH)
    cols = rows_at(kv * HEAD, HEAD, HEAD)
    cache, span = ck.shape[0], bk.shape[0]
    copies = []
    for n, (src, row, size, col) in enumerate(
        ((ck, 0, cache, 0), (cv, 0, cache, HEAD), (bk, cache, span, 0), (bv, cache, span, HEAD))
    ):
        copies.append(
            pltpu.make_async_copy(
                src.at[:, cols], out.at[pl.ds(row, size), pl.ds(col, HEAD)], sems.at[n]
            )
        )
    for copy in copies:
        copy.start()
    for copy in copies:
        copy.wait()


def segment_of(position, seg_starts):
    passed = jnp.full(position.shape, -1, jnp.int32)
    for n in range(seg_starts.shape[0]):
        passed = passed + jnp.where(seg_starts[n] <= position, 1, 0)
    return passed


def mask_bias(seg_starts, other, span, cache, pieces):
    ctx = lax.axis_index("ctx")
    cache_total = cache * lax.axis_size("ctx")
    piece_rows = cache + span
    keys = pieces * piece_rows
    index = lax.broadcasted_iota(jnp.int32, (1, keys), 1)
    key_pos = jnp.zeros((1, keys), jnp.int32)
    for k in range(pieces):
        owner = jnp.bitwise_xor(ctx, 2 * k + other)
        off = index - k * piece_rows
        pos = jnp.where(off < cache, owner * cache + off, cache_total + owner * span + off - cache)
        key_pos = pos if k == 0 else jnp.where(off >= 0, pos, key_pos)
    key_seg = segment_of(key_pos, seg_starts)
    query_pos = cache_total + ctx * span + lax.broadcasted_iota(jnp.int32, (span, 1), 0)
    query_seg = segment_of(query_pos, seg_starts)
    last = seg_starts.shape[0] - 1
    seen = (key_pos <= query_pos) & (
        (key_seg == query_seg) | (key_seg == 0) | (query_seg == last)
    )
    return jnp.where(seen, 0.0, neg_large)


def mask_kernel(span, cache, seg_starts, kv, bias_same, bias_other, kv_copy):
    kv_copy[...] = kv[...]
    pieces = bias_same.shape[1] // (cache + span)
    bias_same[...] = mask_bias(seg_starts, 0, span, cache, pieces)
    bias_other[...] = mask_bias(seg_starts, 1, span, cache, pieces)


def route_kernel(n_exp, routes, gates, rank, high, low):
    flight, tokens = rank.shape
    local = flight // n_exp
    expert = lax.broadcasted_iota(jnp.int32, (flight, tokens), 0)
    member = jnp.zeros((flight, tokens), f32)
    weight = jnp.zeros((flight, tokens), f32)
    for k in range(routes.shape[0]):
        hit = routes[k : k + 1, :] == expert
        member = jnp.where(hit, 1.0, member)
        weight = weight + jnp.where(hit, gates[k : k + 1, :], 0.0)
    before = lax.broadcasted_iota(jnp.int32, (tokens, tokens), 0) < lax.broadcasted_iota(
        jnp.int32, (tokens, tokens), 1
    )
    count = dot(member.astype(bf16), jnp.where(before, 1.0, 0.0).astype(bf16))
    slots = jnp.where(member > 0.5, count, -1.0)
    rank[...] = slots
    exp = lax.axis_index("exp")
    slot = lax.broadcasted_iota(jnp.int32, (CAP, tokens), 0).astype(f32)
    tables = []
    for e in range(flight):
        tables.append(jnp.where(slots[e : e + 1, :] == slot, weight[e : e + 1, :], 0.0))
    per = local * CAP
    table = jnp.concatenate(tables, axis=0)
    upper = table.astype(bf16)
    lower = (table - upper.astype(f32)).astype(bf16)
    for d in range(n_exp):
        at = pl.ds(pl.multiple_of(jnp.bitwise_xor(exp, d) * per, per), per)
        high[at, :] = upper[d * per : (d + 1) * per, :]
        low[at, :] = lower[d * per : (d + 1) * per, :]


GROUP = 4


def attend(q, kv, bias, span, finish):
    scale = math.log2(math.e) / math.sqrt(HEAD)
    keys = kv.shape[0]
    group = min(GROUP, q.shape[0] // span)
    rows = group * span
    for g in range(q.shape[0] // rows):
        scores = dot_t(q[g * rows : (g + 1) * rows, :], kv[:, :HEAD])
        scores = (scores.reshape(group, span, keys) + bias[...][None]).reshape(rows, keys)
        top = jnp.max(scores, axis=1, keepdims=True)
        probs = jnp.exp2((scores - top) * scale)
        total = jnp.sum(probs, axis=1, keepdims=True)
        out = dot(probs.astype(bf16), kv[:, HEAD:])
        finish(g, rows, group, out, top, total)


def attend_first(span, q, kv, bias, o_out, m_out, l_out):
    def finish(g, rows, group, out, top, total):
        at = pl.ds(g * rows, rows)
        o_out[at, :] = out
        m_out[at, :] = jnp.broadcast_to(top, (rows, LANES))
        l_out[at, :] = jnp.broadcast_to(total, (rows, LANES))

    attend(q, kv, bias, span, finish)


def attend_second(span, q, kv, bias, o_in, m_in, l_in, *results):
    scale = math.log2(math.e) / math.sqrt(HEAD)
    half = results[0].shape[1] // HEAD

    def finish(g, rows, group, out, top, total):
        at = pl.ds(g * rows, rows)
        first = m_in[at, :]
        both = jnp.maximum(first, top)
        w_first = jnp.exp2((first - both) * scale)
        w_second = jnp.exp2((top - both) * scale)
        norm = l_in[at, :] * w_first + total * w_second
        merged = ((o_in[at, :] * w_first + out * w_second) / norm).astype(bf16)
        for h in range(group):
            head = g * group + h
            result = results[head // half]
            col = head % half * HEAD
            result[:, col : col + HEAD] = merged[h * span : (h + 1) * span, :]

    attend(q, kv, bias, span, finish)


def project_first(heads_out, weight, out):
    out[...] = dot(heads_out[...], weight[...])


def project_second(n_exp, span, heads_out, weight, first, residual, ranks, *refs):
    own_out, odd_out = refs[:2]
    even_outs = refs[2 : n_exp // 2 + 1]
    pick_outs = refs[n_exp // 2 + 1 : -2]
    whole, picked = refs[-2:]
    ctx, exp = lax.axis_index("ctx"), lax.axis_index("exp")
    second = dot(heads_out[...], weight[...])
    for k in range(heads_out.shape[0] // span):
        here = slice(k * span, (k + 1) * span)
        whole[rows_at(jnp.bitwise_xor(ctx, 2 * k) * span, span, span), :] = first[here, :]
        whole[rows_at(jnp.bitwise_xor(ctx, 2 * k + 1) * span, span, span), :] = second[here, :]
    tokens = residual.shape[0]
    flight = ranks.shape[0] // n_exp
    local = flight // n_exp
    slot = lax.broadcasted_iota(jnp.int32, (CAP, tokens), 0).astype(f32)
    for k in range(n_exp):
        block = jnp.bitwise_xor(exp, k)
        part = whole[rows_at(block * tokens, tokens, tokens), :]
        if k == 0:
            part = part + residual[...].astype(f32)
            own_out[...] = part
        narrow = part.astype(bf16)
        if k % 2:
            odd_out[k // 2 * tokens : (k // 2 + 1) * tokens, :] = narrow
        elif k:
            even_outs[k // 2 - 1][...] = narrow
        rank = ranks[k * flight : (k + 1) * flight, :]
        table = jnp.concatenate(
            [jnp.where(rank[e : e + 1, :] == slot, 1.0, 0.0) for e in range(flight)], axis=0
        ).astype(bf16)
        rows = dot(table, narrow).astype(bf16)
        for e in range(flight):
            at = (e % local) * n_exp * CAP + block * CAP
            picked[e // local, rows_at(at, CAP, CAP), :] = rows[e * CAP : (e + 1) * CAP, :]
    for k in range(n_exp):
        pick_outs[k][...] = picked[jnp.bitwise_xor(exp, k)]


def split_square(square):
    lane = lax.broadcasted_iota(jnp.int32, (square.shape[0], LANES), 1)
    high = square.astype(bf16).astype(f32)
    return jnp.where(lane == 0, high, jnp.where(lane == 1, square - high, 0.0))


def expert_in_kernel(n_exp, other, *refs):
    arrived = refs[:n_exp]
    gain, weight, out = refs[n_exp:]
    expert = jnp.bitwise_xor(lax.axis_index("ctx") % 2, other)
    rows = out.shape[0]
    width = weight.shape[2]
    at = rows_at(expert * rows, rows, rows)
    total = arrived[0][at, :].astype(f32)
    for ref in arrived[1:]:
        total = total + ref[at, :].astype(f32)
    mixed = total.astype(bf16).astype(f32)
    out[:, width:] = split_square(jnp.sum(mixed * mixed, axis=1, keepdims=True)).astype(out.dtype)
    scaled = (mixed * gain[...]).astype(bf16)
    step = width // 6
    for n in range(0, width, step):
        out[:, n : n + step] = dot(scaled, weight[expert, :, n : n + step]).astype(out.dtype)


def chip_sum(mine, theirs, *outs):
    chip = lax.axis_index("ctx") // 2
    width = mine.shape[1] - LANES
    size = outs[0].shape[0]
    for k, out in enumerate(outs):
        at = rows_at(jnp.bitwise_xor(chip, k) * size, size, size)
        total = mine[at, :] + theirs[at, :].astype(f32)
        out[:, :width] = total[:, :width].astype(bf16)
        out[:, width:] = split_square(
            jnp.sum(total[:, width:], axis=1, keepdims=True)
        ).astype(bf16)


def activate(features, *refs):
    out = refs[-1]
    total = refs[0][...].astype(f32)
    for ref in refs[1:-1]:
        total = total + ref[...].astype(f32)
    hidden = out.shape[1]
    square = jnp.sum(total[:, 2 * hidden :], axis=1, keepdims=True)
    inverse = lax.rsqrt(square / features + eps_norm)
    gate = total[:, :hidden] * inverse
    up = total[:, hidden : 2 * hidden] * inverse
    out[...] = (gate / (1.0 + jnp.exp(-gate)) * up).astype(bf16)


def expert_out_first(active, weight, out):
    out[...] = dot(active[...], weight[lax.axis_index("ctx") % 2]).astype(bf16)


def expert_out_second(n_exp, active, weight, first, *refs):
    outs, whole = refs[:n_exp], refs[n_exp]
    ctx, exp = lax.axis_index("ctx"), lax.axis_index("exp")
    core, chip = ctx % 2, ctx // 2
    chips = lax.axis_size("ctx") // 2
    size = active.shape[0] // chips
    second = dot(active[...], weight[1 - core]).astype(bf16)
    for k in range(chips):
        at = rows_at(jnp.bitwise_xor(chip, k) * size, size, size)
        here = slice(k * size, (k + 1) * size)
        whole[core, at, :] = first[here, :]
        whole[1 - core, at, :] = second[here, :]
    for k in range(n_exp):
        at = rows_at(jnp.bitwise_xor(exp, k) * CAP, CAP, CAP)
        for j in range(whole.shape[0]):
            outs[k][j * CAP : (j + 1) * CAP, :] = whole[j, at, :]


def combine(high, low, own, odd, *refs):
    n_exp = high.shape[0] // refs[0].shape[0]
    returned, parts = refs[:n_exp], refs[n_exp:-2]
    mixed, out = refs[-2:]
    total = own[...] + odd[: own.shape[0], :].astype(f32)
    for part in parts:
        total = total + part[...].astype(f32)
    mixed[...] = total.astype(bf16)
    rows = jnp.concatenate([ref[...] for ref in returned], axis=0)
    dims = (((0,), (0,)), ((), ()))
    out[...] = (
        lax.dot_general(high[...], rows, dims, preferred_element_type=f32)
        + lax.dot_general(low[...], rows, dims, preferred_element_type=f32)
    ).astype(bf16)


def permute(x, axis, k):
    n = lax.axis_size(axis)
    return lax.ppermute(x, axis, [(i, i ^ k) for i in range(n)])


def gather_halves(halves, chips):
    low, high = halves
    if chips != 4:
        return [[low, high]] + [
            [permute(low, "ctx", 2 * k), permute(high, "ctx", 2 * k)] for k in range(1, chips)
        ]
    x_low, y_high = permute(low, "ctx", 2), permute(high, "ctx", 4)
    x_high, y_low = permute(high, "ctx", 2), permute(low, "ctx", 4)
    far_low, far_high = permute(x_low, "ctx", 4), permute(y_high, "ctx", 2)
    return [[low, high], [x_low, x_high], [y_low, y_high], [far_low, far_high]]


def body(
    queries,
    cache_keys,
    cache_values,
    block_keys,
    block_values,
    seg_starts,
    out_weight,
    residual,
    norm_gain,
    routes,
    gate_values,
    expert_in,
    expert_out,
):
    n_ctx, n_exp = lax.axis_size("ctx"), lax.axis_size("exp")
    chips = n_ctx // 2
    span = queries.shape[0]
    heads = queries.shape[1] // HEAD
    cache = cache_keys.shape[0]
    tokens = routes.shape[0]
    local, features, width = expert_in.shape
    hidden = width // 2
    columns = out_weight.shape[1]
    flight = n_exp * local

    def over_chips(x):
        return [permute(x, "ctx", 2 * k) for k in range(1, chips)]

    def over_exp(xs):
        return [permute(x, "exp", k) for k, x in zip(range(1, n_exp), xs)]

    local_kv = call(
        functools.partial(pick_kv, heads),
        shape((cache + span, 2 * HEAD), bf16),
        [HBM] * 4,
        [pltpu.SemaphoreType.DMA((4,))],
        vmem=ALL_VMEM,
    )(cache_keys, cache_values, block_keys, block_values)
    kv_moved = over_chips(local_kv)

    rows, keys = heads * span, chips * (cache + span)
    bias_same, bias_other, own_kv = call(
        functools.partial(mask_kernel, span, cache),
        [shape((span, keys), f32)] * 2 + [shape(local_kv.shape, bf16)],
        [SMEM, VMEM],
        vmem=8,
        nbytes=1 * MIB,
    )(seg_starts, local_kv)
    stacked = queries.reshape(span, heads, HEAD).transpose(1, 0, 2).reshape(rows, HEAD)
    rank, high, low = call(
        functools.partial(route_kernel, n_exp),
        [shape((flight, tokens), f32)] + [shape((flight * CAP, tokens), bf16)] * 2,
        [VMEM] * 2,
        vmem=8,
        nbytes=1 * MIB,
    )(routes.T, gate_values.T)
    kv_moved, stacked, bias_same, bias_other, own_kv, rank = lax.optimization_barrier(
        (kv_moved, stacked, bias_same, bias_other, own_kv, rank)
    )
    kv_same = jnp.concatenate([own_kv] + kv_moved, axis=0)
    kv_other = permute(kv_same, "ctx", 1)

    cost = dict(flops=4 * rows * keys * HEAD, nbytes=4 * MIB)
    stats = call(
        functools.partial(attend_first, span),
        [shape((rows, HEAD), f32), shape((rows, LANES), f32), shape((rows, LANES), f32)],
        [VMEM] * 3,
        vmem=24,
        **cost,
    )(stacked, kv_same, bias_same)
    halves = call(
        functools.partial(attend_second, span),
        [shape((span, rows // span * HEAD // 2), bf16)] * 2,
        [VMEM] * 6,
        vmem=24,
        **cost,
    )(stacked, kv_other, bias_other, *stats)

    halves, ranks = lax.optimization_barrier((halves, rank))
    step = 1
    while step < n_exp:
        ranks = jnp.concatenate([ranks, permute(ranks, "exp", step)], axis=0)
        step *= 2
    pieces = gather_halves(halves, chips)
    pieces, ranks = lax.optimization_barrier((pieces, ranks))
    heads_same = jnp.concatenate([jnp.concatenate(pair, axis=1) for pair in pieces], axis=0)
    heads_other = permute(heads_same, "ctx", 1)
    cost = dict(
        flops=2 * heads_same.shape[0] * heads_same.shape[1] * columns, nbytes=4 * MIB
    )
    first = call(
        project_first,
        shape((heads_same.shape[0], columns), f32),
        [VMEM] * 2,
        vmem=16,
        **cost,
    )(heads_same, out_weight)
    per_exp = local * n_exp * CAP
    outs = call(
        functools.partial(project_second, n_exp, span),
        [shape((tokens, columns), f32)]
        + [shape((n_exp // 2 * tokens, columns), bf16)]
        + [shape((tokens, columns), bf16)] * (n_exp // 2 - 1)
        + [shape((per_exp, columns), bf16)] * n_exp,
        [VMEM] * 5,
        [
            pltpu.VMEM((n_ctx * span, columns), f32),
            pltpu.VMEM((n_exp, per_exp, columns), bf16),
        ],
        vmem=24,
        **cost,
    )(heads_other, out_weight, first, residual, ranks)
    own, odd, even, picks = outs[0], outs[1], outs[2 : n_exp // 2 + 1], outs[n_exp // 2 + 1 :]
    passed = [permute(picks[2 * k + 1], "exp", 1) for k in range(1, n_exp // 2)]
    arrived = [picks[0], permute(picks[1], "exp", 1)]
    for k, got in enumerate(passed, 1):
        pair = (picks[2 * k].astype(f32) + got.astype(f32)).astype(bf16)
        arrived.append(permute(pair, "exp", 2 * k))

    gain = norm_gain.reshape(1, features)
    expert_rows = n_exp * CAP

    def gate_up(other, dtype):
        return call(
            functools.partial(expert_in_kernel, len(arrived), other),
            shape((expert_rows, width + LANES), dtype),
            [VMEM] * (len(arrived) + 2),
            vmem=16,
            flops=2 * expert_rows * features * width,
            nbytes=4 * MIB,
        )(*arrived, gain, expert_in)

    sent = gate_up(1, bf16)
    theirs = permute(sent, "ctx", 1)
    mine = gate_up(0, f32)

    size = expert_rows // chips
    chunk = call(
        chip_sum,
        [shape((size, width + LANES), bf16)] * chips,
        [VMEM] * 2,
        vmem=8,
    )(mine, theirs)
    def beside(ready, sent, step, exchange):
        ready, sent = lax.optimization_barrier((ready, sent))
        return (ready, *lax.optimization_barrier((step(ready), exchange(sent))))

    chunk, gathered, odd = beside(
        chunk,
        odd,
        lambda c: [permute(c[k], "ctx", 2 * k) for k in range(1, chips)],
        lambda x: permute(x, "exp", 1),
    )
    active = call(
        functools.partial(activate, n_ctx * features),
        shape((size, hidden), bf16),
        [VMEM] * chips,
        vmem=8,
    )(chunk[0], *gathered)
    even = [
        (x.astype(f32) + odd[k * tokens : (k + 1) * tokens].astype(f32)).astype(bf16)
        for k, x in enumerate(even, 1)
    ]
    even = [permute(x, "exp", 2 * k) for k, x in enumerate(even, 1)]
    gathered, even = lax.optimization_barrier((over_chips(active), even))
    active_same = jnp.concatenate([active] + gathered, axis=0)
    active_other = permute(active_same, "ctx", 1)
    cost = dict(flops=2 * expert_rows * hidden * columns, nbytes=2 * MIB)
    made = call(
        expert_out_first,
        shape((expert_rows, columns), bf16),
        [VMEM] * 2,
        vmem=8,
        **cost,
    )(active_same, expert_out)
    produced = call(
        functools.partial(expert_out_second, n_exp),
        [shape((local * CAP, columns), bf16)] * n_exp,
        [VMEM] * 3,
        [pltpu.VMEM((local, expert_rows, columns), bf16)],
        vmem=8,
        **cost,
    )(active_other, expert_out, made)
    returned = over_exp(produced[1:])
    mixed, expert_sum = call(
        combine,
        [shape((tokens, columns), bf16)] * 2,
        [VMEM] * (4 + n_exp + len(even)),
        vmem=8,
    )(high, low, own, odd, produced[0], *returned, *even)
    return (mixed, expert_sum)


def solution(mesh):
    placed = (
        P("ctx", "exp"),
        P("ctx", None),
        P("ctx", None),
        P("ctx", None),
        P("ctx", None),
        P(),
        P("exp", "ctx"),
        P("exp", "ctx"),
        P("ctx"),
        P("exp", None),
        P("exp", None),
        P("exp", "ctx", None),
        P("exp", None, "ctx"),
    )
    return jax.shard_map(
        body,
        mesh=mesh,
        in_specs=placed,
        out_specs=(P("exp", "ctx"), P("exp", "ctx")),
        check_vma=False,
    )
```

```python
import functools
import math

import jax
import jax.numpy as jnp
from jax import lax
from jax.experimental import pallas as pl
from jax.experimental.pallas import tpu as pltpu
from jax.sharding import PartitionSpec as P

QHEADS = 64
KVH = 4
HEAD = 128
CAP = 16
LANES = 128

neg_large = -1e30
eps_norm = 1e-06
bf16 = jnp.bfloat16
f32 = jnp.float32
MIB = 1024 * 1024
ALL_VMEM = 63.5

VMEM = pl.BlockSpec(memory_space=pltpu.VMEM)
SMEM = pl.BlockSpec(memory_space=pltpu.SMEM)
HBM = pl.BlockSpec(memory_space=pltpu.HBM)


def call(kernel, out_shape, in_specs, scratch=(), vmem=16, flops=0, nbytes=0):
    many = isinstance(out_shape, (list, tuple))
    return pl.pallas_call(
        kernel,
        out_shape=out_shape,
        in_specs=in_specs,
        out_specs=[VMEM] * len(out_shape) if many else VMEM,
        scratch_shapes=list(scratch),
        compiler_params=pltpu.CompilerParams(vmem_limit_bytes=int(vmem * MIB)),
        cost_estimate=pl.CostEstimate(flops=flops, bytes_accessed=nbytes, transcendentals=0),
    )


def shape(dims, dtype):
    return jax.ShapeDtypeStruct(dims, dtype)


def dot(a, b):
    return lax.dot_general(a, b, (((1,), (0,)), ((), ())), preferred_element_type=f32)


def dot_t(a, b):
    return lax.dot_general(a, b, (((1,), (1,)), ((), ())), preferred_element_type=f32)


def rows_at(start, size, step):
    return pl.ds(pl.multiple_of(start, step), size)


def pick_kv(local_heads, ck, cv, bk, bv, out, sems):
    kv = lax.axis_index("exp") * local_heads // (QHEADS // KVH)
    cols = rows_at(kv * HEAD, HEAD, HEAD)
    cache, span = ck.shape[0], bk.shape[0]
    copies = []
    for n, (src, row, size, col) in enumerate(
        ((ck, 0, cache, 0), (cv, 0, cache, HEAD), (bk, cache, span, 0), (bv, cache, span, HEAD))
    ):
        copies.append(
            pltpu.make_async_copy(
                src.at[:, cols], out.at[pl.ds(row, size), pl.ds(col, HEAD)], sems.at[n]
            )
        )
    for copy in copies:
        copy.start()
    for copy in copies:
        copy.wait()


def segment_of(position, seg_starts):
    passed = jnp.full(position.shape, -1, jnp.int32)
    for n in range(seg_starts.shape[0]):
        passed = passed + jnp.where(seg_starts[n] <= position, 1, 0)
    return passed


def mask_bias(seg_starts, other, span, cache, pieces):
    ctx = lax.axis_index("ctx")
    cache_total = cache * lax.axis_size("ctx")
    piece_rows = cache + span
    keys = pieces * piece_rows
    index = lax.broadcasted_iota(jnp.int32, (1, keys), 1)
    key_pos = jnp.zeros((1, keys), jnp.int32)
    for k in range(pieces):
        owner = jnp.bitwise_xor(ctx, 2 * k + other)
        off = index - k * piece_rows
        pos = jnp.where(off < cache, owner * cache + off, cache_total + owner * span + off - cache)
        key_pos = pos if k == 0 else jnp.where(off >= 0, pos, key_pos)
    key_seg = segment_of(key_pos, seg_starts)
    query_pos = cache_total + ctx * span + lax.broadcasted_iota(jnp.int32, (span, 1), 0)
    query_seg = segment_of(query_pos, seg_starts)
    last = seg_starts.shape[0] - 1
    seen = (key_pos <= query_pos) & (
        (key_seg == query_seg) | (key_seg == 0) | (query_seg == last)
    )
    return jnp.where(seen, 0.0, neg_large)


def mask_kernel(span, cache, seg_starts, kv, bias_same, bias_other, kv_copy):
    kv_copy[...] = kv[...]
    pieces = bias_same.shape[1] // (cache + span)
    bias_same[...] = mask_bias(seg_starts, 0, span, cache, pieces)
    bias_other[...] = mask_bias(seg_starts, 1, span, cache, pieces)


def route_kernel(n_exp, routes, gates, rank, high, low):
    flight, tokens = rank.shape
    local = flight // n_exp
    expert = lax.broadcasted_iota(jnp.int32, (flight, tokens), 0)
    member = jnp.zeros((flight, tokens), f32)
    weight = jnp.zeros((flight, tokens), f32)
    for k in range(routes.shape[0]):
        hit = routes[k : k + 1, :] == expert
        member = jnp.where(hit, 1.0, member)
        weight = weight + jnp.where(hit, gates[k : k + 1, :], 0.0)
    before = lax.broadcasted_iota(jnp.int32, (tokens, tokens), 0) < lax.broadcasted_iota(
        jnp.int32, (tokens, tokens), 1
    )
    count = dot(member.astype(bf16), jnp.where(before, 1.0, 0.0).astype(bf16))
    slots = jnp.where(member > 0.5, count, -1.0)
    rank[...] = slots
    exp = lax.axis_index("exp")
    slot = lax.broadcasted_iota(jnp.int32, (CAP, tokens), 0).astype(f32)
    tables = []
    for e in range(flight):
        tables.append(jnp.where(slots[e : e + 1, :] == slot, weight[e : e + 1, :], 0.0))
    per = local * CAP
    table = jnp.concatenate(tables, axis=0)
    upper = table.astype(bf16)
    lower = (table - upper.astype(f32)).astype(bf16)
    for d in range(n_exp):
        at = pl.ds(pl.multiple_of(jnp.bitwise_xor(exp, d) * per, per), per)
        high[at, :] = upper[d * per : (d + 1) * per, :]
        low[at, :] = lower[d * per : (d + 1) * per, :]


GROUP = 8


def attend(q, kv, bias, span, finish):
    scale = math.log2(math.e) / math.sqrt(HEAD)
    keys = kv.shape[0]
    group = min(GROUP, q.shape[0] // span)
    rows = group * span
    for g in range(q.shape[0] // rows):
        scores = dot_t(q[g * rows : (g + 1) * rows, :], kv[:, :HEAD])
        scores = (scores.reshape(group, span, keys) + bias[...][None]).reshape(rows, keys)
        top = jnp.max(scores, axis=1, keepdims=True)
        probs = jnp.exp2((scores - top) * scale)
        total = jnp.sum(probs, axis=1, keepdims=True)
        out = dot(probs.astype(bf16), kv[:, HEAD:])
        finish(g, rows, group, out, top, total)


def attend_first(span, q, kv, bias, o_out, m_out, l_out):
    def finish(g, rows, group, out, top, total):
        at = pl.ds(g * rows, rows)
        o_out[at, :] = out
        m_out[at, :] = jnp.broadcast_to(top, (rows, LANES))
        l_out[at, :] = jnp.broadcast_to(total, (rows, LANES))

    attend(q, kv, bias, span, finish)


def attend_second(span, q, kv, bias, o_in, m_in, l_in, *results):
    scale = math.log2(math.e) / math.sqrt(HEAD)
    half = results[0].shape[1] // HEAD

    def finish(g, rows, group, out, top, total):
        at = pl.ds(g * rows, rows)
        first = m_in[at, :]
        both = jnp.maximum(first, top)
        w_first = jnp.exp2((first - both) * scale)
        w_second = jnp.exp2((top - both) * scale)
        norm = l_in[at, :] * w_first + total * w_second
        merged = ((o_in[at, :] * w_first + out * w_second) / norm).astype(bf16)
        for h in range(group):
            head = g * group + h
            result = results[head // half]
            col = head % half * HEAD
            result[:, col : col + HEAD] = merged[h * span : (h + 1) * span, :]

    attend(q, kv, bias, span, finish)


def project_first(heads_out, weight, out):
    out[...] = dot(heads_out[...], weight[...])


def project_second(n_exp, span, heads_out, weight, first, residual, ranks, *refs):
    own_out, odd_out = refs[:2]
    even_outs = refs[2 : n_exp // 2 + 1]
    pick_outs, second = refs[n_exp // 2 + 1 : -1], refs[-1]
    second[...] = dot(heads_out[...], weight[...])
    ctx, exp = lax.axis_index("ctx"), lax.axis_index("exp")
    core, chip = ctx % 2, ctx // 2
    tokens, columns = residual.shape
    half = columns // 2
    flight = ranks.shape[0] // n_exp
    local = flight // n_exp
    slot = lax.broadcasted_iota(jnp.int32, (CAP, tokens), 0).astype(f32)
    for k in range(n_exp):
        block = jnp.bitwise_xor(exp, k)
        here = rows_at(jnp.bitwise_xor(chip, block) * span, span, span)
        same, other = first[here, :], second[here, :]
        part = jnp.concatenate(
            [jnp.where(core == 0, same, other), jnp.where(core == 0, other, same)], axis=0
        )
        if k == 0:
            part = part + residual[...].astype(f32)
            own_out[...] = part
        narrow = part.astype(bf16)
        if k % 2:
            odd_out[k // 2 * tokens : (k // 2 + 1) * tokens, :] = narrow
        elif k:
            even_outs[k // 2 - 1][...] = narrow
        table = []
        for d in range(n_exp):
            for j in range(local):
                row = k * flight + jnp.bitwise_xor(exp, d) * local + j
                table.append(jnp.where(ranks[pl.ds(row, 1), :] == slot, 1.0, 0.0))
        rows = dot(jnp.concatenate(table, axis=0).astype(bf16), narrow).astype(bf16)
        for d in range(n_exp):
            for j in range(local):
                at = rows_at(j * n_exp * CAP + block * CAP, CAP, CAP)
                value = rows[(d * local + j) * CAP : (d * local + j + 1) * CAP, :]
                if d < 2:
                    pick_outs[d][at, :] = value
                else:
                    pick_outs[2 * d - 2][at, :] = value[:, :half]
                    pick_outs[2 * d - 1][at, :] = value[:, half:]


def split_square(square):
    lane = lax.broadcasted_iota(jnp.int32, (square.shape[0], LANES), 1)
    high = square.astype(bf16).astype(f32)
    return jnp.where(lane == 0, high, jnp.where(lane == 1, square - high, 0.0))


def expert_in_kernel(n_arrived, direct, other, *refs):
    arrived = refs[:n_arrived]
    gain, weight, out = refs[n_arrived:]
    expert = jnp.bitwise_xor(lax.axis_index("ctx") % 2, other)
    rows = out.shape[0]
    width = weight.shape[2]
    at = rows_at(expert * rows, rows, rows)
    total = arrived[0][at, :].astype(f32) + arrived[1][at, :].astype(f32)
    halves = [0.0, 0.0]
    for n, ref in enumerate(arrived[2:]):
        halves[n >= direct] = halves[n >= direct] + ref[at, :].astype(f32)
    mixed = (total + jnp.concatenate(halves, axis=1)).astype(bf16).astype(f32)
    out[:, width:] = split_square(jnp.sum(mixed * mixed, axis=1, keepdims=True)).astype(out.dtype)
    scaled = (mixed * gain[...]).astype(bf16)
    step = width // 6
    for n in range(0, width, step):
        out[:, n : n + step] = dot(scaled, weight[expert, :, n : n + step]).astype(out.dtype)


def chip_sum(mine, theirs, *outs):
    chip = lax.axis_index("ctx") // 2
    width = mine.shape[1] - LANES
    size = outs[0].shape[0]
    for k, out in enumerate(outs):
        at = rows_at(jnp.bitwise_xor(chip, k) * size, size, size)
        total = mine[at, :] + theirs[at, :].astype(f32)
        out[:, :width] = total[:, :width].astype(bf16)
        out[:, width:] = split_square(
            jnp.sum(total[:, width:], axis=1, keepdims=True)
        ).astype(bf16)


def activate(features, *refs):
    out = refs[-1]
    total = refs[0][...].astype(f32)
    for ref in refs[1:-1]:
        total = total + ref[...].astype(f32)
    hidden = out.shape[1]
    square = jnp.sum(total[:, 2 * hidden :], axis=1, keepdims=True)
    inverse = lax.rsqrt(square / features + eps_norm)
    gate = total[:, :hidden] * inverse
    up = total[:, hidden : 2 * hidden] * inverse
    out[...] = (gate / (1.0 + jnp.exp(-gate)) * up).astype(bf16)


def expert_out_first(active, weight, out):
    out[...] = dot(active[...], weight[lax.axis_index("ctx") % 2]).astype(bf16)


def expert_out_second(n_exp, active, weight, first, *refs):
    outs, whole = refs[:n_exp], refs[n_exp]
    ctx, exp = lax.axis_index("ctx"), lax.axis_index("exp")
    core, chip = ctx % 2, ctx // 2
    chips = lax.axis_size("ctx") // 2
    size = active.shape[0] // chips
    second = dot(active[...], weight[1 - core]).astype(bf16)
    for k in range(chips):
        at = rows_at(jnp.bitwise_xor(chip, k) * size, size, size)
        here = slice(k * size, (k + 1) * size)
        whole[core, at, :] = first[here, :]
        whole[1 - core, at, :] = second[here, :]
    for k in range(n_exp):
        at = rows_at(jnp.bitwise_xor(exp, k) * CAP, CAP, CAP)
        for j in range(whole.shape[0]):
            outs[k][j * CAP : (j + 1) * CAP, :] = whole[j, at, :]


def combine(high, low, *refs):
    out = refs[-1]
    rows = jnp.concatenate([ref[...] for ref in refs[:-1]], axis=0)
    dims = (((0,), (0,)), ((), ()))
    out[...] = (
        lax.dot_general(high[...], rows, dims, preferred_element_type=f32)
        + lax.dot_general(low[...], rows, dims, preferred_element_type=f32)
    ).astype(bf16)


def permute(x, axis, k):
    n = lax.axis_size(axis)
    return lax.ppermute(x, axis, [(i, i ^ k) for i in range(n)])


def gather_halves(halves, chips):
    low, high = halves
    if chips != 4:
        return [[low, high]] + [
            [permute(low, "ctx", 2 * k), permute(high, "ctx", 2 * k)] for k in range(1, chips)
        ]
    x_low, y_high = permute(low, "ctx", 2), permute(high, "ctx", 4)
    x_high, y_low = permute(high, "ctx", 2), permute(low, "ctx", 4)
    far_low, far_high = permute(x_low, "ctx", 4), permute(y_high, "ctx", 2)
    return [[low, high], [x_low, x_high], [y_low, y_high], [far_low, far_high]]


def body(
    queries,
    cache_keys,
    cache_values,
    block_keys,
    block_values,
    seg_starts,
    out_weight,
    residual,
    norm_gain,
    routes,
    gate_values,
    expert_in,
    expert_out,
):
    n_ctx, n_exp = lax.axis_size("ctx"), lax.axis_size("exp")
    chips = n_ctx // 2
    span = queries.shape[0]
    heads = queries.shape[1] // HEAD
    cache = cache_keys.shape[0]
    tokens = routes.shape[0]
    local, features, width = expert_in.shape
    hidden = width // 2
    columns = out_weight.shape[1]
    flight = n_exp * local

    def over_chips(x):
        return [permute(x, "ctx", 2 * k) for k in range(1, chips)]

    def over_exp(xs):
        return [permute(x, "exp", k) for k, x in zip(range(1, n_exp), xs)]

    local_kv = call(
        functools.partial(pick_kv, heads),
        shape((cache + span, 2 * HEAD), bf16),
        [HBM] * 4,
        [pltpu.SemaphoreType.DMA((4,))],
        vmem=ALL_VMEM,
    )(cache_keys, cache_values, block_keys, block_values)
    kv_moved = over_chips(local_kv)

    rows, keys = heads * span, chips * (cache + span)
    bias_same, bias_other, own_kv = call(
        functools.partial(mask_kernel, span, cache),
        [shape((span, keys), f32)] * 2 + [shape(local_kv.shape, bf16)],
        [SMEM, VMEM],
        vmem=8,
        nbytes=1 * MIB,
    )(seg_starts, local_kv)
    stacked = queries.reshape(span, heads, HEAD).transpose(1, 0, 2).reshape(rows, HEAD)
    rank, high, low = call(
        functools.partial(route_kernel, n_exp),
        [shape((flight, tokens), f32)] + [shape((flight * CAP, tokens), bf16)] * 2,
        [VMEM] * 2,
        vmem=8,
        nbytes=1 * MIB,
    )(routes.T, gate_values.T)
    kv_moved, stacked, bias_same, bias_other, own_kv, rank = lax.optimization_barrier(
        (kv_moved, stacked, bias_same, bias_other, own_kv, rank)
    )
    kv_same = jnp.concatenate([own_kv] + kv_moved, axis=0)
    kv_other = permute(kv_same, "ctx", 1)

    cost = dict(flops=4 * rows * keys * HEAD, nbytes=4 * MIB)
    stats = call(
        functools.partial(attend_first, span),
        [shape((rows, HEAD), f32), shape((rows, LANES), f32), shape((rows, LANES), f32)],
        [VMEM] * 3,
        vmem=24,
        **cost,
    )(stacked, kv_same, bias_same)
    halves = call(
        functools.partial(attend_second, span),
        [shape((span, rows // span * HEAD // 2), bf16)] * 2,
        [VMEM] * 6,
        vmem=24,
        **cost,
    )(stacked, kv_other, bias_other, *stats)

    halves, ranks = lax.optimization_barrier((halves, rank))
    step = 1
    while step < n_exp:
        ranks = jnp.concatenate([ranks, permute(ranks, "exp", step)], axis=0)
        step *= 2
    pieces = gather_halves(halves, chips)
    pieces, ranks = lax.optimization_barrier((pieces, ranks))
    heads_same = jnp.concatenate([jnp.concatenate(pair, axis=1) for pair in pieces], axis=0)
    heads_other = permute(heads_same, "ctx", 1)
    cost = dict(
        flops=2 * heads_same.shape[0] * heads_same.shape[1] * columns, nbytes=4 * MIB
    )
    first = call(
        project_first,
        shape((heads_same.shape[0], columns), f32),
        [VMEM] * 2,
        vmem=16,
        **cost,
    )(heads_same, out_weight)
    per_exp = local * n_exp * CAP
    outs = call(
        functools.partial(project_second, n_exp, span),
        [shape((tokens, columns), f32)]
        + [shape((n_exp // 2 * tokens, columns), bf16)]
        + [shape((tokens, columns), bf16)] * (n_exp // 2 - 1)
        + [shape((per_exp, columns), bf16)] * 2
        + [shape((per_exp, columns // 2), bf16)] * (2 * n_exp - 4),
        [VMEM] * 5,
        [pltpu.VMEM(first.shape, f32)],
        vmem=24,
        **cost,
    )(heads_other, out_weight, first, residual, ranks)
    own, odd, even, picks = outs[0], outs[1], outs[2 : n_exp // 2 + 1], outs[n_exp // 2 + 1 :]
    left, right = picks[2::2], picks[3::2]
    passed = [permute(right[2 * k - 1], "exp", 1) for k in range(1, n_exp // 2)]
    direct = [permute(x, "exp", k) for k, x in enumerate(left, 2)]
    arrived = [picks[0], permute(picks[1], "exp", 1)] + direct
    for k, got in enumerate(passed, 1):
        pair = (right[2 * k - 2].astype(f32) + got.astype(f32)).astype(bf16)
        arrived.append(permute(pair, "exp", 2 * k))
    gain = norm_gain.reshape(1, features)
    expert_rows = n_exp * CAP

    def gate_up(other, dtype):
        return call(
            functools.partial(expert_in_kernel, len(arrived), len(direct), other),
            shape((expert_rows, width + LANES), dtype),
            [VMEM] * (len(arrived) + 2),
            vmem=16,
            flops=2 * expert_rows * features * width,
            nbytes=4 * MIB,
        )(*arrived, gain, expert_in)

    sent = gate_up(1, bf16)
    theirs = permute(sent, "ctx", 1)
    mine = gate_up(0, f32)

    size = expert_rows // chips
    chunk = call(
        chip_sum,
        [shape((size, width + LANES), bf16)] * chips,
        [VMEM] * 2,
        vmem=8,
    )(mine, theirs)
    def beside(ready, sent, step, exchange):
        ready, sent = lax.optimization_barrier((ready, sent))
        return (ready, *lax.optimization_barrier((step(ready), exchange(sent))))

    chunk, gathered, odd = beside(
        chunk,
        odd,
        lambda c: [permute(c[k], "ctx", 2 * k) for k in range(1, chips)],
        lambda x: permute(x, "exp", 1),
    )
    active = call(
        functools.partial(activate, n_ctx * features),
        shape((size, hidden), bf16),
        [VMEM] * chips,
        vmem=8,
    )(chunk[0], *gathered)
    even = [
        (x.astype(f32) + odd[k * tokens : (k + 1) * tokens].astype(f32)).astype(bf16)
        for k, x in enumerate(even, 1)
    ]
    even = [permute(x, "exp", 2 * k) for k, x in enumerate(even, 1)]
    gathered, even = lax.optimization_barrier((over_chips(active), even))
    active_same = jnp.concatenate([active] + gathered, axis=0)
    active_other = permute(active_same, "ctx", 1)
    cost = dict(flops=2 * expert_rows * hidden * columns, nbytes=2 * MIB)
    made = call(
        expert_out_first,
        shape((expert_rows, columns), bf16),
        [VMEM] * 2,
        vmem=8,
        **cost,
    )(active_same, expert_out)
    produced = call(
        functools.partial(expert_out_second, n_exp),
        [shape((local * CAP, columns), bf16)] * n_exp,
        [VMEM] * 3,
        [pltpu.VMEM((local, expert_rows, columns), bf16)],
        vmem=8,
        **cost,
    )(active_other, expert_out, made)
    returned = over_exp(produced[1:])
    mixed = own + odd[:tokens].astype(f32)
    for part in even:
        mixed = mixed + part.astype(f32)
    mixed = mixed.astype(bf16)
    expert_sum = call(
        combine,
        shape((tokens, columns), bf16),
        [VMEM] * (2 + n_exp),
        vmem=8,
    )(high, low, produced[0], *returned)
    return (mixed, expert_sum)


def solution(mesh):
    placed = (
        P("ctx", "exp"),
        P("ctx", None),
        P("ctx", None),
        P("ctx", None),
        P("ctx", None),
        P(),
        P("exp", "ctx"),
        P("exp", "ctx"),
        P("ctx"),
        P("exp", None),
        P("exp", None),
        P("exp", "ctx", None),
        P("exp", None, "ctx"),
    )
    return jax.shard_map(
        body,
        mesh=mesh,
        in_specs=placed,
        out_specs=(P("exp", "ctx"), P("exp", "ctx")),
        check_vma=False,
    )
```

```python
import functools
import math

import jax
import jax.numpy as jnp
from jax import lax
from jax.experimental import pallas as pl
from jax.experimental.pallas import tpu as pltpu
from jax.sharding import PartitionSpec as P

QHEADS = 64
KVH = 4
HEAD = 128
CAP = 16
LANES = 128

neg_large = -1e30
eps_norm = 1e-06
bf16 = jnp.bfloat16
f32 = jnp.float32
MIB = 1024 * 1024
ALL_VMEM = 63.5

VMEM = pl.BlockSpec(memory_space=pltpu.VMEM)
SMEM = pl.BlockSpec(memory_space=pltpu.SMEM)
HBM = pl.BlockSpec(memory_space=pltpu.HBM)


def call(kernel, out_shape, in_specs, scratch=(), vmem=16, flops=0, nbytes=0):
    many = isinstance(out_shape, (list, tuple))
    return pl.pallas_call(
        kernel,
        out_shape=out_shape,
        in_specs=in_specs,
        out_specs=[VMEM] * len(out_shape) if many else VMEM,
        scratch_shapes=list(scratch),
        compiler_params=pltpu.CompilerParams(vmem_limit_bytes=int(vmem * MIB)),
        cost_estimate=pl.CostEstimate(flops=flops, bytes_accessed=nbytes, transcendentals=0),
    )


def shape(dims, dtype):
    return jax.ShapeDtypeStruct(dims, dtype)


def dot(a, b):
    return lax.dot_general(a, b, (((1,), (0,)), ((), ())), preferred_element_type=f32)


def dot_t(a, b):
    return lax.dot_general(a, b, (((1,), (1,)), ((), ())), preferred_element_type=f32)


def rows_at(start, size, step):
    return pl.ds(pl.multiple_of(start, step), size)


def pick_kv(local_heads, ck, cv, bk, bv, out, sems):
    kv = lax.axis_index("exp") * local_heads // (QHEADS // KVH)
    cols = rows_at(kv * HEAD, HEAD, HEAD)
    cache, span = ck.shape[0], bk.shape[0]
    copies = []
    for n, (src, row, size, col) in enumerate(
        ((ck, 0, cache, 0), (cv, 0, cache, HEAD), (bk, cache, span, 0), (bv, cache, span, HEAD))
    ):
        copies.append(
            pltpu.make_async_copy(
                src.at[:, cols], out.at[pl.ds(row, size), pl.ds(col, HEAD)], sems.at[n]
            )
        )
    for copy in copies:
        copy.start()
    for copy in copies:
        copy.wait()


def segment_of(position, seg_starts):
    passed = jnp.full(position.shape, -1, jnp.int32)
    for n in range(seg_starts.shape[1]):
        passed = passed + jnp.where(seg_starts[:, n : n + 1] <= position, 1, 0)
    return passed


def mask_bias(seg_starts, other, span, cache, pieces):
    ctx = lax.axis_index("ctx")
    cache_total = cache * lax.axis_size("ctx")
    piece_rows = cache + span
    keys = pieces * piece_rows
    index = lax.broadcasted_iota(jnp.int32, (1, keys), 1)
    key_pos = jnp.zeros((1, keys), jnp.int32)
    for k in range(pieces):
        owner = jnp.bitwise_xor(ctx, 2 * k + other)
        off = index - k * piece_rows
        pos = jnp.where(off < cache, owner * cache + off, cache_total + owner * span + off - cache)
        key_pos = pos if k == 0 else jnp.where(off >= 0, pos, key_pos)
    key_seg = segment_of(key_pos, seg_starts)
    query_pos = cache_total + ctx * span + lax.broadcasted_iota(jnp.int32, (span, 1), 0)
    query_seg = segment_of(query_pos, seg_starts)
    last = seg_starts.shape[1] - 1
    seen = (key_pos <= query_pos) & (
        (key_seg == query_seg) | (key_seg == 0) | (query_seg == last)
    )
    return jnp.where(seen, 0.0, neg_large)


def prepare(n_exp, top, segments, span, cache, small, kv, bias_same, bias_other, kv_copy, rank, high, low):
    kv_copy[...] = kv[...]
    pieces = bias_same.shape[1] // (cache + span)
    seg_starts = small[2 * top : 2 * top + 1, :].astype(jnp.int32)[:, :segments]
    bias_same[...] = mask_bias(seg_starts, 0, span, cache, pieces)
    bias_other[...] = mask_bias(seg_starts, 1, span, cache, pieces)
    routes = small[:top, :].astype(jnp.int32)
    gates = small[top : 2 * top, :]
    flight, tokens = rank.shape
    local = flight // n_exp
    expert = lax.broadcasted_iota(jnp.int32, (flight, tokens), 0)
    member = jnp.zeros((flight, tokens), f32)
    weight = jnp.zeros((flight, tokens), f32)
    for k in range(routes.shape[0]):
        hit = routes[k : k + 1, :] == expert
        member = jnp.where(hit, 1.0, member)
        weight = weight + jnp.where(hit, gates[k : k + 1, :], 0.0)
    before = lax.broadcasted_iota(jnp.int32, (tokens, tokens), 0) < lax.broadcasted_iota(
        jnp.int32, (tokens, tokens), 1
    )
    count = dot(member.astype(bf16), jnp.where(before, 1.0, 0.0).astype(bf16))
    slots = jnp.where(member > 0.5, count, -1.0)
    rank[...] = slots
    exp = lax.axis_index("exp")
    slot = lax.broadcasted_iota(jnp.int32, (CAP, tokens), 0).astype(f32)
    tables = []
    for e in range(flight):
        tables.append(jnp.where(slots[e : e + 1, :] == slot, weight[e : e + 1, :], 0.0))
    per = local * CAP
    table = jnp.concatenate(tables, axis=0)
    upper = table.astype(bf16)
    lower = (table - upper.astype(f32)).astype(bf16)
    for d in range(n_exp):
        at = pl.ds(pl.multiple_of(jnp.bitwise_xor(exp, d) * per, per), per)
        high[at, :] = upper[d * per : (d + 1) * per, :]
        low[at, :] = lower[d * per : (d + 1) * per, :]


GROUP = 8


def attend(q, kv, bias, span, finish):
    scale = math.log2(math.e) / math.sqrt(HEAD)
    keys = kv.shape[0]
    group = min(GROUP, q.shape[0] // span)
    rows = group * span
    for g in range(q.shape[0] // rows):
        scores = dot_t(q[g * rows : (g + 1) * rows, :], kv[:, :HEAD])
        scores = (scores.reshape(group, span, keys) + bias[...][None]).reshape(rows, keys)
        top = jnp.max(scores, axis=1, keepdims=True)
        probs = jnp.exp2((scores - top) * scale)
        total = jnp.sum(probs, axis=1, keepdims=True)
        out = dot(probs.astype(bf16), kv[:, HEAD:])
        finish(g, rows, group, out, top, total)


def attend_first(span, q, kv, bias, o_out, m_out, l_out):
    def finish(g, rows, group, out, top, total):
        at = pl.ds(g * rows, rows)
        o_out[at, :] = out
        m_out[at, :] = jnp.broadcast_to(top, (rows, LANES))
        l_out[at, :] = jnp.broadcast_to(total, (rows, LANES))

    attend(q, kv, bias, span, finish)


def attend_second(span, q, kv, bias, o_in, m_in, l_in, *results):
    scale = math.log2(math.e) / math.sqrt(HEAD)
    half = results[0].shape[1] // HEAD

    def finish(g, rows, group, out, top, total):
        at = pl.ds(g * rows, rows)
        first = m_in[at, :]
        both = jnp.maximum(first, top)
        w_first = jnp.exp2((first - both) * scale)
        w_second = jnp.exp2((top - both) * scale)
        norm = l_in[at, :] * w_first + total * w_second
        merged = ((o_in[at, :] * w_first + out * w_second) / norm).astype(bf16)
        for h in range(group):
            head = g * group + h
            result = results[head // half]
            col = head % half * HEAD
            result[:, col : col + HEAD] = merged[h * span : (h + 1) * span, :]

    attend(q, kv, bias, span, finish)


def project_first(heads_out, weight, out):
    out[...] = dot(heads_out[...], weight[...])


def project_second(n_exp, span, heads_out, weight, first, residual, ranks, *refs):
    own_out, odd_out = refs[:2]
    even_outs = refs[2 : n_exp // 2 + 1]
    pick_outs, second = refs[n_exp // 2 + 1 : -1], refs[-1]
    second[...] = dot(heads_out[...], weight[...])
    ctx, exp = lax.axis_index("ctx"), lax.axis_index("exp")
    core, chip = ctx % 2, ctx // 2
    tokens, columns = residual.shape
    half = columns // 2
    flight = ranks.shape[0] // n_exp
    local = flight // n_exp
    slot = lax.broadcasted_iota(jnp.int32, (CAP, tokens), 0).astype(f32)
    for k in range(n_exp):
        block = jnp.bitwise_xor(exp, k)
        here = rows_at(jnp.bitwise_xor(chip, block) * span, span, span)
        same, other = first[here, :], second[here, :]
        part = jnp.concatenate(
            [jnp.where(core == 0, same, other), jnp.where(core == 0, other, same)], axis=0
        )
        if k == 0:
            part = part + residual[...].astype(f32)
            own_out[...] = part
        narrow = part.astype(bf16)
        if k % 2:
            odd_out[k // 2 * tokens : (k // 2 + 1) * tokens, :] = narrow
        elif k:
            even_outs[k // 2 - 1][...] = narrow
        table = []
        for d in range(n_exp):
            for j in range(local):
                row = k * flight + jnp.bitwise_xor(exp, d) * local + j
                table.append(jnp.where(ranks[pl.ds(row, 1), :] == slot, 1.0, 0.0))
        rows = dot(jnp.concatenate(table, axis=0).astype(bf16), narrow).astype(bf16)
        for d in range(n_exp):
            for j in range(local):
                at = rows_at(j * n_exp * CAP + block * CAP, CAP, CAP)
                value = rows[(d * local + j) * CAP : (d * local + j + 1) * CAP, :]
                if d < 2:
                    pick_outs[d][at, :] = value
                else:
                    pick_outs[2 * d - 2][at, :] = value[:, :half]
                    pick_outs[2 * d - 1][at, :] = value[:, half:]


def split_square(square):
    lane = lax.broadcasted_iota(jnp.int32, (square.shape[0], LANES), 1)
    high = square.astype(bf16).astype(f32)
    return jnp.where(lane == 0, high, jnp.where(lane == 1, square - high, 0.0))


def expert_in_kernel(n_arrived, direct, other, *refs):
    arrived = refs[:n_arrived]
    gain, weight, out = refs[n_arrived:]
    expert = jnp.bitwise_xor(lax.axis_index("ctx") % 2, other)
    rows = out.shape[0]
    width = weight.shape[2]
    at = rows_at(expert * rows, rows, rows)
    total = arrived[0][at, :].astype(f32) + arrived[1 + direct][at, :].astype(f32)
    halves = [0.0, 0.0]
    for n, ref in enumerate(arrived[1 : 1 + direct] + arrived[2 + direct :]):
        halves[n >= direct] = halves[n >= direct] + ref[at, :].astype(f32)
    mixed = (total + jnp.concatenate(halves, axis=1)).astype(bf16).astype(f32)
    out[:, width:] = split_square(jnp.sum(mixed * mixed, axis=1, keepdims=True)).astype(out.dtype)
    scaled = (mixed * gain[...]).astype(bf16)
    step = width // 6
    for n in range(0, width, step):
        out[:, n : n + step] = dot(scaled, weight[expert, :, n : n + step]).astype(out.dtype)


def chip_sum(mine, theirs, *outs):
    chip = lax.axis_index("ctx") // 2
    width = mine.shape[1] - LANES
    size = outs[0].shape[0]
    for k, out in enumerate(outs):
        at = rows_at(jnp.bitwise_xor(chip, k) * size, size, size)
        total = mine[at, :] + theirs[at, :].astype(f32)
        out[:, :width] = total[:, :width].astype(bf16)
        out[:, width:] = split_square(
            jnp.sum(total[:, width:], axis=1, keepdims=True)
        ).astype(bf16)


def activate(features, *refs):
    out = refs[-1]
    total = refs[0][...].astype(f32)
    for ref in refs[1:-1]:
        total = total + ref[...].astype(f32)
    hidden = out.shape[1]
    square = jnp.sum(total[:, 2 * hidden :], axis=1, keepdims=True)
    inverse = lax.rsqrt(square / features + eps_norm)
    gate = total[:, :hidden] * inverse
    up = total[:, hidden : 2 * hidden] * inverse
    out[...] = (gate / (1.0 + jnp.exp(-gate)) * up).astype(bf16)


def expert_out_first(active, weight, out):
    out[...] = dot(active[...], weight[lax.axis_index("ctx") % 2]).astype(bf16)


def expert_out_second(n_exp, active, weight, first, *refs):
    outs, whole = refs[:n_exp], refs[n_exp]
    ctx, exp = lax.axis_index("ctx"), lax.axis_index("exp")
    core, chip = ctx % 2, ctx // 2
    chips = lax.axis_size("ctx") // 2
    size = active.shape[0] // chips
    second = dot(active[...], weight[1 - core]).astype(bf16)
    for k in range(chips):
        at = rows_at(jnp.bitwise_xor(chip, k) * size, size, size)
        here = slice(k * size, (k + 1) * size)
        whole[core, at, :] = first[here, :]
        whole[1 - core, at, :] = second[here, :]
    for k in range(n_exp):
        at = rows_at(jnp.bitwise_xor(exp, k) * CAP, CAP, CAP)
        for j in range(whole.shape[0]):
            outs[k][j * CAP : (j + 1) * CAP, :] = whole[j, at, :]


def combine(high, low, *refs):
    out = refs[-1]
    rows = jnp.concatenate([ref[...] for ref in refs[:-1]], axis=0)
    dims = (((0,), (0,)), ((), ()))
    out[...] = (
        lax.dot_general(high[...], rows, dims, preferred_element_type=f32)
        + lax.dot_general(low[...], rows, dims, preferred_element_type=f32)
    ).astype(bf16)


def permute(x, axis, k):
    n = lax.axis_size(axis)
    return lax.ppermute(x, axis, [(i, i ^ k) for i in range(n)])


def gather_halves(halves, chips):
    low, high = halves
    if chips != 4:
        return [[low, high]] + [
            [permute(low, "ctx", 2 * k), permute(high, "ctx", 2 * k)] for k in range(1, chips)
        ]
    x_low, y_high = permute(low, "ctx", 2), permute(high, "ctx", 4)
    x_high, y_low = permute(high, "ctx", 2), permute(low, "ctx", 4)
    far_low, far_high = permute(x_low, "ctx", 4), permute(y_high, "ctx", 2)
    return [[low, high], [x_low, x_high], [y_low, y_high], [far_low, far_high]]


def body(
    queries,
    cache_keys,
    cache_values,
    block_keys,
    block_values,
    seg_starts,
    out_weight,
    residual,
    norm_gain,
    routes,
    gate_values,
    expert_in,
    expert_out,
):
    n_ctx, n_exp = lax.axis_size("ctx"), lax.axis_size("exp")
    chips = n_ctx // 2
    span = queries.shape[0]
    heads = queries.shape[1] // HEAD
    cache = cache_keys.shape[0]
    tokens = routes.shape[0]
    local, features, width = expert_in.shape
    hidden = width // 2
    columns = out_weight.shape[1]
    flight = n_exp * local

    def over_chips(x):
        return [permute(x, "ctx", 2 * k) for k in range(1, chips)]

    def over_exp(xs):
        return [permute(x, "exp", k) for k, x in zip(range(1, n_exp), xs)]

    local_kv = call(
        functools.partial(pick_kv, heads),
        shape((cache + span, 2 * HEAD), bf16),
        [HBM] * 4,
        [pltpu.SemaphoreType.DMA((4,))],
        vmem=ALL_VMEM,
    )(cache_keys, cache_values, block_keys, block_values)
    kv_moved = over_chips(local_kv)

    rows, keys = heads * span, chips * (cache + span)
    top, segments = routes.shape[1], seg_starts.shape[0]
    small = jnp.concatenate(
        [
            routes.T.astype(f32),
            gate_values.T,
            jnp.pad(seg_starts.astype(f32)[None], ((0, 0), (0, tokens - segments))),
        ],
        axis=0,
    )
    bias_same, bias_other, own_kv, rank, high, low = call(
        functools.partial(prepare, n_exp, top, segments, span, cache),
        [shape((span, keys), f32)] * 2
        + [shape(local_kv.shape, bf16)]
        + [shape((flight, tokens), f32)]
        + [shape((flight * CAP, tokens), bf16)] * 2,
        [VMEM] * 2,
        vmem=8,
        nbytes=2 * MIB,
    )(small, local_kv)
    stacked = queries.reshape(span, heads, HEAD).transpose(1, 0, 2).reshape(rows, HEAD)
    kv_moved, stacked, bias_same, bias_other, own_kv, rank = lax.optimization_barrier(
        (kv_moved, stacked, bias_same, bias_other, own_kv, rank)
    )
    kv_same = jnp.concatenate([own_kv] + kv_moved, axis=0)
    kv_other = permute(kv_same, "ctx", 1)

    cost = dict(flops=4 * rows * keys * HEAD, nbytes=4 * MIB)
    stats = call(
        functools.partial(attend_first, span),
        [shape((rows, HEAD), f32), shape((rows, LANES), f32), shape((rows, LANES), f32)],
        [VMEM] * 3,
        vmem=24,
        **cost,
    )(stacked, kv_same, bias_same)
    halves = call(
        functools.partial(attend_second, span),
        [shape((span, rows // span * HEAD // 2), bf16)] * 2,
        [VMEM] * 6,
        vmem=24,
        **cost,
    )(stacked, kv_other, bias_other, *stats)

    halves, ranks = lax.optimization_barrier((halves, rank))
    step = 1
    while step < n_exp:
        ranks = jnp.concatenate([ranks, permute(ranks, "exp", step)], axis=0)
        step *= 2
    pieces = gather_halves(halves, chips)
    pieces, ranks = lax.optimization_barrier((pieces, ranks))
    heads_same = jnp.concatenate([jnp.concatenate(pair, axis=1) for pair in pieces], axis=0)
    heads_other = permute(heads_same, "ctx", 1)
    cost = dict(
        flops=2 * heads_same.shape[0] * heads_same.shape[1] * columns, nbytes=4 * MIB
    )
    first = call(
        project_first,
        shape((heads_same.shape[0], columns), f32),
        [VMEM] * 2,
        vmem=16,
        **cost,
    )(heads_same, out_weight)
    per_exp = local * n_exp * CAP
    outs = call(
        functools.partial(project_second, n_exp, span),
        [shape((tokens, columns), f32)]
        + [shape((n_exp // 2 * tokens, columns), bf16)]
        + [shape((tokens, columns), bf16)] * (n_exp // 2 - 1)
        + [shape((per_exp, columns), bf16)] * 2
        + [shape((per_exp, columns // 2), bf16)] * (2 * n_exp - 4),
        [VMEM] * 5,
        [pltpu.VMEM(first.shape, f32)],
        vmem=24,
        **cost,
    )(heads_other, out_weight, first, residual, ranks)
    own, odd, even, picks = outs[0], outs[1], outs[2 : n_exp // 2 + 1], outs[n_exp // 2 + 1 :]
    left, right = picks[2::2], picks[3::2]
    passed = [permute(right[2 * k - 1], "exp", 1) for k in range(1, n_exp // 2)]
    direct = [permute(x, "exp", k) for k, x in enumerate(left, 2)]
    arrived = [picks[0]] + direct + [permute(picks[1], "exp", 1)]
    for k, got in enumerate(passed, 1):
        pair = (right[2 * k - 2].astype(f32) + got.astype(f32)).astype(bf16)
        arrived.append(permute(pair, "exp", 2 * k))
    gain = norm_gain.reshape(1, features)
    expert_rows = n_exp * CAP

    def gate_up(other, dtype):
        return call(
            functools.partial(expert_in_kernel, len(arrived), len(direct), other),
            shape((expert_rows, width + LANES), dtype),
            [VMEM] * (len(arrived) + 2),
            vmem=16,
            flops=2 * expert_rows * features * width,
            nbytes=4 * MIB,
        )(*arrived, gain, expert_in)

    sent = gate_up(1, bf16)
    sent, odd = lax.optimization_barrier((sent, odd))
    odd = permute(odd, "exp", 1)
    theirs = permute(sent, "ctx", 1)
    mine = gate_up(0, f32)

    size = expert_rows // chips
    chunk = call(
        chip_sum,
        [shape((size, width + LANES), bf16)] * chips,
        [VMEM] * 2,
        vmem=8,
    )(mine, theirs)
    def beside(ready, sent, step, exchange):
        ready, sent = lax.optimization_barrier((ready, sent))
        return (ready, *lax.optimization_barrier((step(ready), exchange(sent))))

    gathered = [permute(chunk[k], "ctx", 2 * k) for k in range(1, chips)]
    gathered, odd = lax.optimization_barrier((gathered, odd))
    active = call(
        functools.partial(activate, n_ctx * features),
        shape((size, hidden), bf16),
        [VMEM] * chips,
        vmem=8,
    )(chunk[0], *gathered)
    even = [
        (x.astype(f32) + odd[k * tokens : (k + 1) * tokens].astype(f32)).astype(bf16)
        for k, x in enumerate(even, 1)
    ]
    even = [permute(x, "exp", 2 * k) for k, x in enumerate(even, 1)]
    gathered, even = lax.optimization_barrier((over_chips(active), even))
    active_same = jnp.concatenate([active] + gathered, axis=0)
    active_other = permute(active_same, "ctx", 1)
    cost = dict(flops=2 * expert_rows * hidden * columns, nbytes=2 * MIB)
    made = call(
        expert_out_first,
        shape((expert_rows, columns), bf16),
        [VMEM] * 2,
        vmem=8,
        **cost,
    )(active_same, expert_out)
    produced = call(
        functools.partial(expert_out_second, n_exp),
        [shape((local * CAP, columns), bf16)] * n_exp,
        [VMEM] * 3,
        [pltpu.VMEM((local, expert_rows, columns), bf16)],
        vmem=8,
        **cost,
    )(active_other, expert_out, made)
    returned = over_exp(produced[1:])
    mixed = own + odd[:tokens].astype(f32)
    for part in even:
        mixed = mixed + part.astype(f32)
    mixed = mixed.astype(bf16)
    expert_sum = call(
        combine,
        shape((tokens, columns), bf16),
        [VMEM] * (2 + n_exp),
        vmem=8,
    )(high, low, produced[0], *returned)
    return (mixed, expert_sum)


def solution(mesh):
    placed = (
        P("ctx", "exp"),
        P("ctx", None),
        P("ctx", None),
        P("ctx", None),
        P("ctx", None),
        P(),
        P("exp", "ctx"),
        P("exp", "ctx"),
        P("ctx"),
        P("exp", None),
        P("exp", None),
        P("exp", "ctx", None),
        P("exp", None, "ctx"),
    )
    return jax.shard_map(
        body,
        mesh=mesh,
        in_specs=placed,
        out_specs=(P("exp", "ctx"), P("exp", "ctx")),
        check_vma=False,
    )
```

```python
import functools
import math

import jax
import jax.numpy as jnp
from jax import lax
from jax.experimental import pallas as pl
from jax.experimental.pallas import tpu as pltpu
from jax.sharding import PartitionSpec as P

QHEADS = 64
KVH = 4
HEAD = 128
CAP = 16
LANES = 128

neg_large = -1e30
eps_norm = 1e-06
bf16 = jnp.bfloat16
f32 = jnp.float32
MIB = 1024 * 1024
ALL_VMEM = 63.5

VMEM = pl.BlockSpec(memory_space=pltpu.VMEM)
SMEM = pl.BlockSpec(memory_space=pltpu.SMEM)
HBM = pl.BlockSpec(memory_space=pltpu.HBM)


def call(kernel, out_shape, in_specs, scratch=(), vmem=16, flops=0, nbytes=0):
    many = isinstance(out_shape, (list, tuple))
    return pl.pallas_call(
        kernel,
        out_shape=out_shape,
        in_specs=in_specs,
        out_specs=[VMEM] * len(out_shape) if many else VMEM,
        scratch_shapes=list(scratch),
        compiler_params=pltpu.CompilerParams(vmem_limit_bytes=int(vmem * MIB)),
        cost_estimate=pl.CostEstimate(flops=flops, bytes_accessed=nbytes, transcendentals=0),
    )


def shape(dims, dtype):
    return jax.ShapeDtypeStruct(dims, dtype)


def dot(a, b):
    return lax.dot_general(a, b, (((1,), (0,)), ((), ())), preferred_element_type=f32)


def dot_t(a, b):
    return lax.dot_general(a, b, (((1,), (1,)), ((), ())), preferred_element_type=f32)


def turn(k, chips):
    return (chips - k) % chips


def rows_at(start, size, step):
    return pl.ds(pl.multiple_of(start, step), size)


def pick_kv(local_heads, ck, cv, bk, bv, out, sems):
    kv = lax.axis_index("exp") * local_heads // (QHEADS // KVH)
    cols = rows_at(kv * HEAD, HEAD, HEAD)
    cache, span = ck.shape[0], bk.shape[0]
    copies = []
    for n, (src, row, size, col) in enumerate(
        ((ck, 0, cache, 0), (cv, 0, cache, HEAD), (bk, cache, span, 0), (bv, cache, span, HEAD))
    ):
        copies.append(
            pltpu.make_async_copy(
                src.at[:, cols], out.at[pl.ds(row, size), pl.ds(col, HEAD)], sems.at[n]
            )
        )
    for copy in copies:
        copy.start()
    for copy in copies:
        copy.wait()


def segment_of(position, seg_starts):
    passed = jnp.full(position.shape, -1, jnp.int32)
    for n in range(seg_starts.shape[1]):
        passed = passed + jnp.where(seg_starts[:, n : n + 1] <= position, 1, 0)
    return passed


def mask_bias(seg_starts, other, span, cache, pieces):
    ctx = lax.axis_index("ctx")
    cache_total = cache * lax.axis_size("ctx")
    piece_rows = cache + span
    keys = pieces * piece_rows
    index = lax.broadcasted_iota(jnp.int32, (1, keys), 1)
    key_pos = jnp.zeros((1, keys), jnp.int32)
    for k in range(pieces):
        owner = jnp.bitwise_xor(ctx, 2 * turn(k, pieces) + other)
        off = index - k * piece_rows
        pos = jnp.where(off < cache, owner * cache + off, cache_total + owner * span + off - cache)
        key_pos = pos if k == 0 else jnp.where(off >= 0, pos, key_pos)
    key_seg = segment_of(key_pos, seg_starts)
    query_pos = cache_total + ctx * span + lax.broadcasted_iota(jnp.int32, (span, 1), 0)
    query_seg = segment_of(query_pos, seg_starts)
    last = seg_starts.shape[1] - 1
    seen = (key_pos <= query_pos) & (
        (key_seg == query_seg) | (key_seg == 0) | (query_seg == last)
    )
    return jnp.where(seen, 0.0, neg_large)


def prepare(n_exp, top, segments, span, cache, small, kv, bias_same, bias_other, kv_copy, rank, high, low):
    kv_copy[...] = kv[...]
    pieces = bias_same.shape[1] // (cache + span)
    seg_starts = small[2 * top : 2 * top + 1, :].astype(jnp.int32)[:, :segments]
    bias_same[...] = mask_bias(seg_starts, 0, span, cache, pieces)
    bias_other[...] = mask_bias(seg_starts, 1, span, cache, pieces)
    routes = small[:top, :].astype(jnp.int32)
    gates = small[top : 2 * top, :]
    flight, tokens = rank.shape
    local = flight // n_exp
    expert = lax.broadcasted_iota(jnp.int32, (flight, tokens), 0)
    member = jnp.zeros((flight, tokens), f32)
    weight = jnp.zeros((flight, tokens), f32)
    for k in range(routes.shape[0]):
        hit = routes[k : k + 1, :] == expert
        member = jnp.where(hit, 1.0, member)
        weight = weight + jnp.where(hit, gates[k : k + 1, :], 0.0)
    before = lax.broadcasted_iota(jnp.int32, (tokens, tokens), 0) < lax.broadcasted_iota(
        jnp.int32, (tokens, tokens), 1
    )
    count = dot(member.astype(bf16), jnp.where(before, 1.0, 0.0).astype(bf16))
    slots = jnp.where(member > 0.5, count, -1.0)
    rank[...] = slots
    exp = lax.axis_index("exp")
    slot = lax.broadcasted_iota(jnp.int32, (CAP, tokens), 0).astype(f32)
    tables = []
    for e in range(flight):
        tables.append(jnp.where(slots[e : e + 1, :] == slot, weight[e : e + 1, :], 0.0))
    per = local * CAP
    table = jnp.concatenate(tables, axis=0)
    upper = table.astype(bf16)
    lower = (table - upper.astype(f32)).astype(bf16)
    for d in range(n_exp):
        at = pl.ds(pl.multiple_of(jnp.bitwise_xor(exp, d) * per, per), per)
        high[at, :] = upper[d * per : (d + 1) * per, :]
        low[at, :] = lower[d * per : (d + 1) * per, :]


GROUP = 8


def attend(q, kv, bias, span, finish):
    scale = math.log2(math.e) / math.sqrt(HEAD)
    keys = kv.shape[0]
    group = min(GROUP, q.shape[0] // span)
    rows = group * span
    for g in range(q.shape[0] // rows):
        scores = dot_t(q[g * rows : (g + 1) * rows, :], kv[:, :HEAD])
        scores = (scores.reshape(group, span, keys) + bias[...][None]).reshape(rows, keys)
        top = jnp.max(scores, axis=1, keepdims=True)
        probs = jnp.exp2((scores - top) * scale)
        total = jnp.sum(probs, axis=1, keepdims=True)
        out = dot(probs.astype(bf16), kv[:, HEAD:])
        finish(g, rows, group, out, top, total)


def attend_first(span, q, kv, bias, o_out, m_out, l_out):
    def finish(g, rows, group, out, top, total):
        at = pl.ds(g * rows, rows)
        o_out[at, :] = out
        m_out[at, :] = jnp.broadcast_to(top, (rows, LANES))
        l_out[at, :] = jnp.broadcast_to(total, (rows, LANES))

    attend(q, kv, bias, span, finish)


def attend_second(span, q, kv, bias, o_in, m_in, l_in, *results):
    scale = math.log2(math.e) / math.sqrt(HEAD)
    half = results[0].shape[1] // HEAD

    def finish(g, rows, group, out, top, total):
        at = pl.ds(g * rows, rows)
        first = m_in[at, :]
        both = jnp.maximum(first, top)
        w_first = jnp.exp2((first - both) * scale)
        w_second = jnp.exp2((top - both) * scale)
        norm = l_in[at, :] * w_first + total * w_second
        merged = ((o_in[at, :] * w_first + out * w_second) / norm).astype(bf16)
        for h in range(group):
            head = g * group + h
            result = results[head // half]
            col = head % half * HEAD
            result[:, col : col + HEAD] = merged[h * span : (h + 1) * span, :]

    attend(q, kv, bias, span, finish)


def project_first(heads_out, weight, out):
    out[...] = dot(heads_out[...], weight[...])


def project_second(n_exp, span, heads_out, weight, first, residual, ranks, *refs):
    own_out, odd_out = refs[:2]
    even_outs = refs[2 : n_exp // 2 + 1]
    pick_outs, second = refs[n_exp // 2 + 1 : -1], refs[-1]
    second[...] = dot(heads_out[...], weight[...])
    ctx, exp = lax.axis_index("ctx"), lax.axis_index("exp")
    core, chip = ctx % 2, ctx // 2
    tokens, columns = residual.shape
    half = columns // 2
    flight = ranks.shape[0] // n_exp
    local = flight // n_exp
    slot = lax.broadcasted_iota(jnp.int32, (CAP, tokens), 0).astype(f32)
    for k in range(n_exp):
        block = jnp.bitwise_xor(exp, k)
        here = rows_at(jnp.bitwise_xor(chip, block) * span, span, span)
        same, other = first[here, :], second[here, :]
        part = jnp.concatenate(
            [jnp.where(core == 0, same, other), jnp.where(core == 0, other, same)], axis=0
        )
        if k == 0:
            part = part + residual[...].astype(f32)
            own_out[...] = part
        narrow = part.astype(bf16)
        if k % 2:
            odd_out[k // 2 * tokens : (k // 2 + 1) * tokens, :] = narrow
        elif k:
            even_outs[k // 2 - 1][...] = narrow
        table = []
        for d in range(n_exp):
            for j in range(local):
                row = k * flight + jnp.bitwise_xor(exp, d) * local + j
                table.append(jnp.where(ranks[pl.ds(row, 1), :] == slot, 1.0, 0.0))
        rows = dot(jnp.concatenate(table, axis=0).astype(bf16), narrow).astype(bf16)
        for d in range(n_exp):
            for j in range(local):
                at = rows_at(j * n_exp * CAP + block * CAP, CAP, CAP)
                value = rows[(d * local + j) * CAP : (d * local + j + 1) * CAP, :]
                if d < 2:
                    pick_outs[d][at, :] = value
                else:
                    pick_outs[2 * d - 2][at, :] = value[:, :half]
                    pick_outs[2 * d - 1][at, :] = value[:, half:]


def split_square(square):
    lane = lax.broadcasted_iota(jnp.int32, (square.shape[0], LANES), 1)
    high = square.astype(bf16).astype(f32)
    return jnp.where(lane == 0, high, jnp.where(lane == 1, square - high, 0.0))


def expert_in_kernel(n_arrived, direct, other, *refs):
    arrived = refs[:n_arrived]
    gain, weight, out = refs[n_arrived:]
    expert = jnp.bitwise_xor(lax.axis_index("ctx") % 2, other)
    rows = out.shape[0]
    width = weight.shape[2]
    at = rows_at(expert * rows, rows, rows)
    total = arrived[0][at, :].astype(f32) + arrived[1 + direct][at, :].astype(f32)
    halves = [0.0, 0.0]
    for n, ref in enumerate(arrived[1 : 1 + direct] + arrived[2 + direct :]):
        halves[n >= direct] = halves[n >= direct] + ref[at, :].astype(f32)
    mixed = (total + jnp.concatenate(halves, axis=1)).astype(bf16).astype(f32)
    out[:, width:] = split_square(jnp.sum(mixed * mixed, axis=1, keepdims=True)).astype(out.dtype)
    scaled = (mixed * gain[...]).astype(bf16)
    step = width // 6
    for n in range(0, width, step):
        out[:, n : n + step] = dot(scaled, weight[expert, :, n : n + step]).astype(out.dtype)


def chip_sum(mine, theirs, *outs):
    chip = lax.axis_index("ctx") // 2
    width = mine.shape[1] - LANES
    size = outs[0].shape[0]
    for k, out in enumerate(outs):
        at = rows_at(jnp.bitwise_xor(chip, k) * size, size, size)
        total = mine[at, :] + theirs[at, :].astype(f32)
        out[:, :width] = total[:, :width].astype(bf16)
        out[:, width:] = split_square(
            jnp.sum(total[:, width:], axis=1, keepdims=True)
        ).astype(bf16)


def activate(features, *refs):
    out = refs[-1]
    total = refs[0][...].astype(f32)
    for ref in refs[1:-1]:
        total = total + ref[...].astype(f32)
    hidden = out.shape[1]
    square = jnp.sum(total[:, 2 * hidden :], axis=1, keepdims=True)
    inverse = lax.rsqrt(square / features + eps_norm)
    gate = total[:, :hidden] * inverse
    up = total[:, hidden : 2 * hidden] * inverse
    out[...] = (gate / (1.0 + jnp.exp(-gate)) * up).astype(bf16)


def expert_out_first(active, weight, out):
    out[...] = dot(active[...], weight[lax.axis_index("ctx") % 2]).astype(bf16)


def expert_out_second(n_exp, active, weight, first, *refs):
    outs, whole = refs[:n_exp], refs[n_exp]
    ctx, exp = lax.axis_index("ctx"), lax.axis_index("exp")
    core, chip = ctx % 2, ctx // 2
    chips = lax.axis_size("ctx") // 2
    size = active.shape[0] // chips
    second = dot(active[...], weight[1 - core]).astype(bf16)
    for k in range(chips):
        at = rows_at(jnp.bitwise_xor(chip, turn(k, chips)) * size, size, size)
        here = slice(k * size, (k + 1) * size)
        whole[core, at, :] = first[here, :]
        whole[1 - core, at, :] = second[here, :]
    for k in range(n_exp):
        at = rows_at(jnp.bitwise_xor(exp, k) * CAP, CAP, CAP)
        for j in range(whole.shape[0]):
            outs[k][j * CAP : (j + 1) * CAP, :] = whole[j, at, :]


def combine(high, low, *refs):
    out = refs[-1]
    rows = jnp.concatenate([ref[...] for ref in (refs[0], *refs[-2:0:-1])], axis=0)
    dims = (((0,), (0,)), ((), ()))
    out[...] = (
        lax.dot_general(high[...], rows, dims, preferred_element_type=f32)
        + lax.dot_general(low[...], rows, dims, preferred_element_type=f32)
    ).astype(bf16)


def permute(x, axis, k):
    n = lax.axis_size(axis)
    return lax.ppermute(x, axis, [(i, i ^ k) for i in range(n)])


def gather_halves(halves, chips):
    low, high = halves
    if chips != 4:
        return [[low, high]] + [
            [permute(low, "ctx", 2 * k), permute(high, "ctx", 2 * k)] for k in range(1, chips)
        ]
    x_low, y_high = permute(low, "ctx", 2), permute(high, "ctx", 4)
    x_high, y_low = permute(high, "ctx", 2), permute(low, "ctx", 4)
    far_low, far_high = permute(x_low, "ctx", 4), permute(y_high, "ctx", 2)
    return [[low, high], [x_low, x_high], [y_low, y_high], [far_low, far_high]]


def body(
    queries,
    cache_keys,
    cache_values,
    block_keys,
    block_values,
    seg_starts,
    out_weight,
    residual,
    norm_gain,
    routes,
    gate_values,
    expert_in,
    expert_out,
):
    n_ctx, n_exp = lax.axis_size("ctx"), lax.axis_size("exp")
    chips = n_ctx // 2
    span = queries.shape[0]
    heads = queries.shape[1] // HEAD
    cache = cache_keys.shape[0]
    tokens = routes.shape[0]
    local, features, width = expert_in.shape
    hidden = width // 2
    columns = out_weight.shape[1]
    flight = n_exp * local

    def over_chips(x):
        return [permute(x, "ctx", 2 * k) for k in reversed(range(1, chips))]

    def over_exp(xs):
        return [permute(x, "exp", k) for k, x in zip(range(1, n_exp), xs)]

    local_kv = call(
        functools.partial(pick_kv, heads),
        shape((cache + span, 2 * HEAD), bf16),
        [HBM] * 4,
        [pltpu.SemaphoreType.DMA((4,))],
        vmem=ALL_VMEM,
    )(cache_keys, cache_values, block_keys, block_values)
    kv_moved = over_chips(local_kv)

    rows, keys = heads * span, chips * (cache + span)
    top, segments = routes.shape[1], seg_starts.shape[0]
    small = jnp.concatenate(
        [
            routes.T.astype(f32),
            gate_values.T,
            jnp.pad(seg_starts.astype(f32)[None], ((0, 0), (0, tokens - segments))),
        ],
        axis=0,
    )
    bias_same, bias_other, own_kv, rank, high, low = call(
        functools.partial(prepare, n_exp, top, segments, span, cache),
        [shape((span, keys), f32)] * 2
        + [shape(local_kv.shape, bf16)]
        + [shape((flight, tokens), f32)]
        + [shape((flight * CAP, tokens), bf16)] * 2,
        [VMEM] * 2,
        vmem=8,
        nbytes=2 * MIB,
    )(small, local_kv)
    stacked = queries.reshape(span, heads, HEAD).transpose(1, 0, 2).reshape(rows, HEAD)
    kv_moved, stacked, bias_same, bias_other, own_kv, rank = lax.optimization_barrier(
        (kv_moved, stacked, bias_same, bias_other, own_kv, rank)
    )
    kv_same = jnp.concatenate([own_kv] + kv_moved, axis=0)
    kv_other = permute(kv_same, "ctx", 1)

    cost = dict(flops=4 * rows * keys * HEAD, nbytes=4 * MIB)
    stats = call(
        functools.partial(attend_first, span),
        [shape((rows, HEAD), f32), shape((rows, LANES), f32), shape((rows, LANES), f32)],
        [VMEM] * 3,
        vmem=24,
        **cost,
    )(stacked, kv_same, bias_same)
    halves = call(
        functools.partial(attend_second, span),
        [shape((span, rows // span * HEAD // 2), bf16)] * 2,
        [VMEM] * 6,
        vmem=24,
        **cost,
    )(stacked, kv_other, bias_other, *stats)

    halves, ranks = lax.optimization_barrier((halves, rank))
    step = 1
    while step < n_exp:
        ranks = jnp.concatenate([ranks, permute(ranks, "exp", step)], axis=0)
        step *= 2
    pieces = gather_halves(halves, chips)
    pieces, ranks = lax.optimization_barrier((pieces, ranks))
    heads_same = jnp.concatenate([jnp.concatenate(pair, axis=1) for pair in pieces], axis=0)
    heads_other = permute(heads_same, "ctx", 1)
    cost = dict(
        flops=2 * heads_same.shape[0] * heads_same.shape[1] * columns, nbytes=4 * MIB
    )
    first = call(
        project_first,
        shape((heads_same.shape[0], columns), f32),
        [VMEM] * 2,
        vmem=16,
        **cost,
    )(heads_same, out_weight)
    per_exp = local * n_exp * CAP
    outs = call(
        functools.partial(project_second, n_exp, span),
        [shape((tokens, columns), f32)]
        + [shape((n_exp // 2 * tokens, columns), bf16)]
        + [shape((tokens, columns), bf16)] * (n_exp // 2 - 1)
        + [shape((per_exp, columns), bf16)] * 2
        + [shape((per_exp, columns // 2), bf16)] * (2 * n_exp - 4),
        [VMEM] * 5,
        [pltpu.VMEM(first.shape, f32)],
        vmem=24,
        **cost,
    )(heads_other, out_weight, first, residual, ranks)
    own, odd, even, picks = outs[0], outs[1], outs[2 : n_exp // 2 + 1], outs[n_exp // 2 + 1 :]
    left, right = picks[2::2], picks[3::2]
    passed = [permute(right[2 * k - 1], "exp", 1) for k in range(1, n_exp // 2)]
    direct = [permute(x, "exp", k) for k, x in enumerate(left, 2)][::-1]
    arrived = [picks[0]] + direct + [permute(picks[1], "exp", 1)]
    for k, got in enumerate(passed, 1):
        pair = (right[2 * k - 2].astype(f32) + got.astype(f32)).astype(bf16)
        arrived.append(permute(pair, "exp", 2 * k))
    gain = norm_gain.reshape(1, features)
    expert_rows = n_exp * CAP

    def gate_up(other, dtype):
        return call(
            functools.partial(expert_in_kernel, len(arrived), len(direct), other),
            shape((expert_rows, width + LANES), dtype),
            [VMEM] * (len(arrived) + 2),
            vmem=16,
            flops=2 * expert_rows * features * width,
            nbytes=4 * MIB,
        )(*arrived, gain, expert_in)

    sent = gate_up(1, bf16)
    sent, odd = lax.optimization_barrier((sent, odd))
    odd = permute(odd, "exp", 1)
    theirs = permute(sent, "ctx", 1)
    mine = gate_up(0, f32)

    size = expert_rows // chips
    chunk = call(
        chip_sum,
        [shape((size, width + LANES), bf16)] * chips,
        [VMEM] * 2,
        vmem=8,
    )(mine, theirs)
    def beside(ready, sent, step, exchange):
        ready, sent = lax.optimization_barrier((ready, sent))
        return (ready, *lax.optimization_barrier((step(ready), exchange(sent))))

    gathered = [permute(chunk[k], "ctx", 2 * k) for k in range(1, chips)]
    gathered, odd = lax.optimization_barrier((gathered, odd))
    active = call(
        functools.partial(activate, n_ctx * features),
        shape((size, hidden), bf16),
        [VMEM] * chips,
        vmem=8,
    )(chunk[0], *gathered)
    even = [
        (x.astype(f32) + odd[k * tokens : (k + 1) * tokens].astype(f32)).astype(bf16)
        for k, x in enumerate(even, 1)
    ]
    even = [permute(x, "exp", 2 * k) for k, x in enumerate(even, 1)]
    gathered, even = lax.optimization_barrier((over_chips(active), even))
    active_same = jnp.concatenate([active] + gathered, axis=0)
    active_other = permute(active_same, "ctx", 1)
    cost = dict(flops=2 * expert_rows * hidden * columns, nbytes=2 * MIB)
    made = call(
        expert_out_first,
        shape((expert_rows, columns), bf16),
        [VMEM] * 2,
        vmem=8,
        **cost,
    )(active_same, expert_out)
    produced = call(
        functools.partial(expert_out_second, n_exp),
        [shape((local * CAP, columns), bf16)] * n_exp,
        [VMEM] * 3,
        [pltpu.VMEM((local, expert_rows, columns), bf16)],
        vmem=8,
        **cost,
    )(active_other, expert_out, made)
    returned = [permute(produced[k], "exp", k) for k in reversed(range(1, n_exp))]
    mixed = own + odd[:tokens].astype(f32)
    for part in even:
        mixed = mixed + part.astype(f32)
    mixed = mixed.astype(bf16)
    expert_sum = call(
        combine,
        shape((tokens, columns), bf16),
        [VMEM] * (2 + n_exp),
        vmem=8,
    )(high, low, produced[0], *returned)
    return (mixed, expert_sum)


def solution(mesh):
    placed = (
        P("ctx", "exp"),
        P("ctx", None),
        P("ctx", None),
        P("ctx", None),
        P("ctx", None),
        P(),
        P("exp", "ctx"),
        P("exp", "ctx"),
        P("ctx"),
        P("exp", None),
        P("exp", None),
        P("exp", "ctx", None),
        P("exp", None, "ctx"),
    )
    return jax.shard_map(
        body,
        mesh=mesh,
        in_specs=placed,
        out_specs=(P("exp", "ctx"), P("exp", "ctx")),
        check_vma=False,
    )
```

```python
import functools
import math

import jax
import jax.numpy as jnp
from jax import lax
from jax.experimental import pallas as pl
from jax.experimental.pallas import tpu as pltpu
from jax.sharding import PartitionSpec as P

QHEADS = 64
KVH = 4
HEAD = 128
CAP = 16
LANES = 128

neg_large = -1e30
eps_norm = 1e-06
bf16 = jnp.bfloat16
f32 = jnp.float32
MIB = 1024 * 1024
ALL_VMEM = 63.5

VMEM = pl.BlockSpec(memory_space=pltpu.VMEM)
SMEM = pl.BlockSpec(memory_space=pltpu.SMEM)
HBM = pl.BlockSpec(memory_space=pltpu.HBM)


def call(kernel, out_shape, in_specs, scratch=(), vmem=16, flops=0, nbytes=0):
    many = isinstance(out_shape, (list, tuple))
    return pl.pallas_call(
        kernel,
        out_shape=out_shape,
        in_specs=in_specs,
        out_specs=[VMEM] * len(out_shape) if many else VMEM,
        scratch_shapes=list(scratch),
        compiler_params=pltpu.CompilerParams(vmem_limit_bytes=int(vmem * MIB)),
        cost_estimate=pl.CostEstimate(flops=flops, bytes_accessed=nbytes, transcendentals=0),
    )


def shape(dims, dtype):
    return jax.ShapeDtypeStruct(dims, dtype)


def dot(a, b):
    return lax.dot_general(a, b, (((1,), (0,)), ((), ())), preferred_element_type=f32)


def dot_t(a, b):
    return lax.dot_general(a, b, (((1,), (1,)), ((), ())), preferred_element_type=f32)


def turn(k, chips):
    return (chips - k) % chips


def rows_at(start, size, step):
    return pl.ds(pl.multiple_of(start, step), size)


def pick_kv(local_heads, ck, cv, bk, bv, out, sems):
    kv = lax.axis_index("exp") * local_heads // (QHEADS // KVH)
    cols = rows_at(kv * HEAD, HEAD, HEAD)
    cache, span = ck.shape[0], bk.shape[0]
    copies = []
    for n, (src, row, size, col) in enumerate(
        ((ck, 0, cache, 0), (cv, 0, cache, HEAD), (bk, cache, span, 0), (bv, cache, span, HEAD))
    ):
        copies.append(
            pltpu.make_async_copy(
                src.at[:, cols], out.at[pl.ds(row, size), pl.ds(col, HEAD)], sems.at[n]
            )
        )
    for copy in copies:
        copy.start()
    for copy in copies:
        copy.wait()


def segment_of(position, seg_starts):
    passed = jnp.full(position.shape, -1, jnp.int32)
    for n in range(seg_starts.shape[1]):
        passed = passed + jnp.where(seg_starts[:, n : n + 1] <= position, 1, 0)
    return passed


def mask_bias(seg_starts, other, span, cache, pieces):
    ctx = lax.axis_index("ctx")
    cache_total = cache * lax.axis_size("ctx")
    piece_rows = cache + span
    keys = pieces * piece_rows
    index = lax.broadcasted_iota(jnp.int32, (1, keys), 1)
    key_pos = jnp.zeros((1, keys), jnp.int32)
    for k in range(pieces):
        owner = jnp.bitwise_xor(ctx, 2 * turn(k, pieces) + other)
        off = index - k * piece_rows
        pos = jnp.where(off < cache, owner * cache + off, cache_total + owner * span + off - cache)
        key_pos = pos if k == 0 else jnp.where(off >= 0, pos, key_pos)
    key_seg = segment_of(key_pos, seg_starts)
    query_pos = cache_total + ctx * span + lax.broadcasted_iota(jnp.int32, (span, 1), 0)
    query_seg = segment_of(query_pos, seg_starts)
    last = seg_starts.shape[1] - 1
    seen = (key_pos <= query_pos) & (
        (key_seg == query_seg) | (key_seg == 0) | (query_seg == last)
    )
    return jnp.where(seen, 0.0, neg_large)


def prepare(n_exp, top, segments, span, cache, small, kv, bias_same, bias_other, kv_copy, rank, high, low):
    kv_copy[...] = kv[...]
    pieces = bias_same.shape[1] // (cache + span)
    seg_starts = small[2 * top : 2 * top + 1, :].astype(jnp.int32)[:, :segments]
    bias_same[...] = mask_bias(seg_starts, 0, span, cache, pieces)
    bias_other[...] = mask_bias(seg_starts, 1, span, cache, pieces)
    routes = small[:top, :].astype(jnp.int32)
    gates = small[top : 2 * top, :]
    flight, tokens = rank.shape
    local = flight // n_exp
    expert = lax.broadcasted_iota(jnp.int32, (flight, tokens), 0)
    member = jnp.zeros((flight, tokens), f32)
    weight = jnp.zeros((flight, tokens), f32)
    for k in range(routes.shape[0]):
        hit = routes[k : k + 1, :] == expert
        member = jnp.where(hit, 1.0, member)
        weight = weight + jnp.where(hit, gates[k : k + 1, :], 0.0)
    before = lax.broadcasted_iota(jnp.int32, (tokens, tokens), 0) < lax.broadcasted_iota(
        jnp.int32, (tokens, tokens), 1
    )
    count = dot(member.astype(bf16), jnp.where(before, 1.0, 0.0).astype(bf16))
    slots = jnp.where(member > 0.5, count, -1.0)
    rank[...] = slots
    exp = lax.axis_index("exp")
    slot = lax.broadcasted_iota(jnp.int32, (CAP, tokens), 0).astype(f32)
    tables = []
    for e in range(flight):
        tables.append(jnp.where(slots[e : e + 1, :] == slot, weight[e : e + 1, :], 0.0))
    per = local * CAP
    table = jnp.concatenate(tables, axis=0)
    upper = table.astype(bf16)
    lower = (table - upper.astype(f32)).astype(bf16)
    for d in range(n_exp):
        at = pl.ds(pl.multiple_of(jnp.bitwise_xor(exp, d) * per, per), per)
        high[at, :] = upper[d * per : (d + 1) * per, :]
        low[at, :] = lower[d * per : (d + 1) * per, :]


GROUP = 8


def attend(q, kv, bias, span, finish):
    scale = math.log2(math.e) / math.sqrt(HEAD)
    keys = kv.shape[0]
    group = min(GROUP, q.shape[0] // span)
    rows = group * span
    for g in range(q.shape[0] // rows):
        scores = dot_t(q[g * rows : (g + 1) * rows, :], kv[:, :HEAD])
        scores = (scores.reshape(group, span, keys) + bias[...][None]).reshape(rows, keys)
        top = jnp.max(scores, axis=1, keepdims=True)
        probs = jnp.exp2((scores - top) * scale)
        total = jnp.sum(probs, axis=1, keepdims=True)
        out = dot(probs.astype(bf16), kv[:, HEAD:])
        finish(g, rows, group, out, top, total)


def attend_first(span, q, kv, bias, o_out, m_out, l_out):
    def finish(g, rows, group, out, top, total):
        at = pl.ds(g * rows, rows)
        o_out[at, :] = out
        m_out[at, :] = jnp.broadcast_to(top, (rows, LANES))
        l_out[at, :] = jnp.broadcast_to(total, (rows, LANES))

    attend(q, kv, bias, span, finish)


def attend_second(span, q, kv, bias, o_in, m_in, l_in, *results):
    scale = math.log2(math.e) / math.sqrt(HEAD)
    half = results[0].shape[1] // HEAD

    def finish(g, rows, group, out, top, total):
        at = pl.ds(g * rows, rows)
        first = m_in[at, :]
        both = jnp.maximum(first, top)
        w_first = jnp.exp2((first - both) * scale)
        w_second = jnp.exp2((top - both) * scale)
        norm = l_in[at, :] * w_first + total * w_second
        merged = ((o_in[at, :] * w_first + out * w_second) / norm).astype(bf16)
        for h in range(group):
            head = g * group + h
            result = results[head // half]
            col = head % half * HEAD
            result[:, col : col + HEAD] = merged[h * span : (h + 1) * span, :]

    attend(q, kv, bias, span, finish)


def project_first(heads_out, weight, out):
    out[...] = dot(heads_out[...], weight[...])


def project_second(n_exp, span, heads_out, weight, first, residual, ranks, *refs):
    own_out, odd_out = refs[:2]
    even_outs = refs[2 : n_exp // 2 + 1]
    pick_outs, second = refs[n_exp // 2 + 1 : -1], refs[-1]
    second[...] = dot(heads_out[...], weight[...])
    ctx, exp = lax.axis_index("ctx"), lax.axis_index("exp")
    core, chip = ctx % 2, ctx // 2
    tokens, columns = residual.shape
    half = columns // 2
    flight = ranks.shape[0] // n_exp
    local = flight // n_exp
    slot = lax.broadcasted_iota(jnp.int32, (CAP, tokens), 0).astype(f32)
    held, step = [0], n_exp // 2
    while step:
        held, step = held + [k ^ step for k in held], step // 2
    for k in range(n_exp):
        block = jnp.bitwise_xor(exp, k)
        here = rows_at(jnp.bitwise_xor(chip, block) * span, span, span)
        same, other = first[here, :], second[here, :]
        part = jnp.concatenate(
            [jnp.where(core == 0, same, other), jnp.where(core == 0, other, same)], axis=0
        )
        if k == 0:
            part = part + residual[...].astype(f32)
            own_out[...] = part
        narrow = part.astype(bf16)
        if k % 2:
            odd_out[k // 2 * tokens : (k // 2 + 1) * tokens, :] = narrow
        elif k:
            even_outs[k // 2 - 1][...] = narrow
        table = []
        for d in range(n_exp):
            for j in range(local):
                row = held.index(k) * flight + jnp.bitwise_xor(exp, d) * local + j
                table.append(jnp.where(ranks[pl.ds(row, 1), :] == slot, 1.0, 0.0))
        rows = dot(jnp.concatenate(table, axis=0).astype(bf16), narrow).astype(bf16)
        for d in range(n_exp):
            for j in range(local):
                at = rows_at(j * n_exp * CAP + block * CAP, CAP, CAP)
                value = rows[(d * local + j) * CAP : (d * local + j + 1) * CAP, :]
                if d == 0:
                    pick_outs[d][at, :] = value
                else:
                    pick_outs[2 * d - 1][at, :] = value[:, :half]
                    pick_outs[2 * d][at, :] = value[:, half:]


def split_square(square):
    lane = lax.broadcasted_iota(jnp.int32, (square.shape[0], LANES), 1)
    high = square.astype(bf16).astype(f32)
    return jnp.where(lane == 0, high, jnp.where(lane == 1, square - high, 0.0))


def expert_in_kernel(n_arrived, direct, other, *refs):
    arrived = refs[:n_arrived]
    gain, weight, out = refs[n_arrived:]
    expert = jnp.bitwise_xor(lax.axis_index("ctx") % 2, other)
    rows = out.shape[0]
    width = weight.shape[2]
    at = rows_at(expert * rows, rows, rows)
    total = arrived[0][at, :].astype(f32)
    halves = [0.0, 0.0]
    for n, ref in enumerate(arrived[1:]):
        halves[n >= direct] = halves[n >= direct] + ref[at, :].astype(f32)
    mixed = (total + jnp.concatenate(halves, axis=1)).astype(bf16).astype(f32)
    out[:, width:] = split_square(jnp.sum(mixed * mixed, axis=1, keepdims=True)).astype(out.dtype)
    scaled = (mixed * gain[...]).astype(bf16)
    step = width // 6
    for n in range(0, width, step):
        out[:, n : n + step] = dot(scaled, weight[expert, :, n : n + step]).astype(out.dtype)


def chip_sum(mine, theirs, *outs):
    chip = lax.axis_index("ctx") // 2
    width = mine.shape[1] - LANES
    size = outs[0].shape[0]
    for k, out in enumerate(outs):
        at = rows_at(jnp.bitwise_xor(chip, k) * size, size, size)
        total = mine[at, :] + theirs[at, :].astype(f32)
        out[:, :width] = total[:, :width].astype(bf16)
        out[:, width:] = split_square(
            jnp.sum(total[:, width:], axis=1, keepdims=True)
        ).astype(bf16)


def activate(features, *refs):
    out = refs[-1]
    total = refs[0][...].astype(f32)
    for ref in refs[1:-1]:
        total = total + ref[...].astype(f32)
    hidden = out.shape[1]
    square = jnp.sum(total[:, 2 * hidden :], axis=1, keepdims=True)
    inverse = lax.rsqrt(square / features + eps_norm)
    gate = total[:, :hidden] * inverse
    up = total[:, hidden : 2 * hidden] * inverse
    out[...] = (gate / (1.0 + jnp.exp(-gate)) * up).astype(bf16)


def expert_out_first(active, weight, out):
    out[...] = dot(active[...], weight[lax.axis_index("ctx") % 2]).astype(bf16)


def expert_out_second(n_exp, active, weight, first, *refs):
    outs, whole = refs[:n_exp], refs[n_exp]
    ctx, exp = lax.axis_index("ctx"), lax.axis_index("exp")
    core, chip = ctx % 2, ctx // 2
    chips = lax.axis_size("ctx") // 2
    size = active.shape[0] // chips
    second = dot(active[...], weight[1 - core]).astype(bf16)
    for k in range(chips):
        at = rows_at(jnp.bitwise_xor(chip, turn(k, chips)) * size, size, size)
        here = slice(k * size, (k + 1) * size)
        whole[core, at, :] = first[here, :]
        whole[1 - core, at, :] = second[here, :]
    for k in range(n_exp):
        at = rows_at(jnp.bitwise_xor(exp, k) * CAP, CAP, CAP)
        for j in range(whole.shape[0]):
            outs[k][j * CAP : (j + 1) * CAP, :] = whole[j, at, :]


def combine(high, low, *refs):
    out = refs[-1]
    rows = jnp.concatenate([ref[...] for ref in (refs[0], *refs[-2:0:-1])], axis=0)
    dims = (((0,), (0,)), ((), ()))
    out[...] = (
        lax.dot_general(high[...], rows, dims, preferred_element_type=f32)
        + lax.dot_general(low[...], rows, dims, preferred_element_type=f32)
    ).astype(bf16)


def permute(x, axis, k):
    n = lax.axis_size(axis)
    return lax.ppermute(x, axis, [(i, i ^ k) for i in range(n)])


def gather_halves(halves, chips):
    low, high = halves
    if chips != 4:
        return [[low, high]] + [
            [permute(low, "ctx", 2 * k), permute(high, "ctx", 2 * k)] for k in range(1, chips)
        ]
    x_low, y_high = permute(low, "ctx", 2), permute(high, "ctx", 4)
    x_high, y_low = permute(high, "ctx", 2), permute(low, "ctx", 4)
    far_low, far_high = permute(x_low, "ctx", 4), permute(y_high, "ctx", 2)
    return [[low, high], [x_low, x_high], [y_low, y_high], [far_low, far_high]]


def body(
    queries,
    cache_keys,
    cache_values,
    block_keys,
    block_values,
    seg_starts,
    out_weight,
    residual,
    norm_gain,
    routes,
    gate_values,
    expert_in,
    expert_out,
):
    n_ctx, n_exp = lax.axis_size("ctx"), lax.axis_size("exp")
    chips = n_ctx // 2
    span = queries.shape[0]
    heads = queries.shape[1] // HEAD
    cache = cache_keys.shape[0]
    tokens = routes.shape[0]
    local, features, width = expert_in.shape
    hidden = width // 2
    columns = out_weight.shape[1]
    flight = n_exp * local

    def over_chips(x):
        return [permute(x, "ctx", 2 * k) for k in reversed(range(1, chips))]

    def over_exp(xs):
        return [permute(x, "exp", k) for k, x in zip(range(1, n_exp), xs)]

    local_kv = call(
        functools.partial(pick_kv, heads),
        shape((cache + span, 2 * HEAD), bf16),
        [HBM] * 4,
        [pltpu.SemaphoreType.DMA((4,))],
        vmem=ALL_VMEM,
    )(cache_keys, cache_values, block_keys, block_values)
    kv_moved = over_chips(local_kv)

    rows, keys = heads * span, chips * (cache + span)
    top, segments = routes.shape[1], seg_starts.shape[0]
    small = jnp.concatenate(
        [
            routes.T.astype(f32),
            gate_values.T,
            jnp.pad(seg_starts.astype(f32)[None], ((0, 0), (0, tokens - segments))),
        ],
        axis=0,
    )
    bias_same, bias_other, own_kv, rank, high, low = call(
        functools.partial(prepare, n_exp, top, segments, span, cache),
        [shape((span, keys), f32)] * 2
        + [shape(local_kv.shape, bf16)]
        + [shape((flight, tokens), f32)]
        + [shape((flight * CAP, tokens), bf16)] * 2,
        [VMEM] * 2,
        vmem=8,
        nbytes=2 * MIB,
    )(small, local_kv)
    stacked = queries.reshape(span, heads, HEAD).transpose(1, 0, 2).reshape(rows, HEAD)
    kv_moved, stacked, bias_same, bias_other, own_kv, rank = lax.optimization_barrier(
        (kv_moved, stacked, bias_same, bias_other, own_kv, rank)
    )
    kv_same = jnp.concatenate([own_kv] + kv_moved, axis=0)
    kv_other = permute(kv_same, "ctx", 1)

    cost = dict(flops=4 * rows * keys * HEAD, nbytes=4 * MIB)
    stats = call(
        functools.partial(attend_first, span),
        [shape((rows, HEAD), f32), shape((rows, LANES), f32), shape((rows, LANES), f32)],
        [VMEM] * 3,
        vmem=24,
        **cost,
    )(stacked, kv_same, bias_same)
    halves = call(
        functools.partial(attend_second, span),
        [shape((span, rows // span * HEAD // 2), bf16)] * 2,
        [VMEM] * 6,
        vmem=24,
        **cost,
    )(stacked, kv_other, bias_other, *stats)

    halves, ranks = lax.optimization_barrier((halves, rank))
    step = n_exp // 2
    while step:
        ranks = jnp.concatenate([ranks, permute(ranks, "exp", step)], axis=0)
        step //= 2
    pieces = gather_halves(halves, chips)
    pieces, ranks = lax.optimization_barrier((pieces, ranks))
    heads_same = jnp.concatenate([jnp.concatenate(pair, axis=1) for pair in pieces], axis=0)
    heads_other = permute(heads_same, "ctx", 1)
    cost = dict(
        flops=2 * heads_same.shape[0] * heads_same.shape[1] * columns, nbytes=4 * MIB
    )
    first = call(
        project_first,
        shape((heads_same.shape[0], columns), f32),
        [VMEM] * 2,
        vmem=16,
        **cost,
    )(heads_same, out_weight)
    per_exp = local * n_exp * CAP
    outs = call(
        functools.partial(project_second, n_exp, span),
        [shape((tokens, columns), f32)]
        + [shape((n_exp // 2 * tokens, columns), bf16)]
        + [shape((tokens, columns), bf16)] * (n_exp // 2 - 1)
        + [shape((per_exp, columns), bf16)]
        + [shape((per_exp, columns // 2), bf16)] * (2 * n_exp - 2),
        [VMEM] * 5,
        [pltpu.VMEM(first.shape, f32)],
        vmem=24,
        **cost,
    )(heads_other, out_weight, first, residual, ranks)
    own, odd, even, picks = outs[0], outs[1], outs[2 : n_exp // 2 + 1], outs[n_exp // 2 + 1 :]
    left, right = picks[3::2], picks[4::2]
    passed = [permute(right[2 * k - 1], "exp", 1) for k in range(1, n_exp // 2)]
    direct = [permute(x, "exp", k) for k, x in enumerate(left, 2)][::-1]
    direct.append(permute(picks[1], "exp", 1))
    arrived = [picks[0]] + direct + [permute(picks[2], "exp", 1)]
    for k, got in enumerate(passed, 1):
        pair = (right[2 * k - 2].astype(f32) + got.astype(f32)).astype(bf16)
        arrived.append(permute(pair, "exp", 2 * k))
    gain = norm_gain.reshape(1, features)
    expert_rows = n_exp * CAP

    def gate_up(other, dtype):
        return call(
            functools.partial(expert_in_kernel, len(arrived), len(direct), other),
            shape((expert_rows, width + LANES), dtype),
            [VMEM] * (len(arrived) + 2),
            vmem=16,
            flops=2 * expert_rows * features * width,
            nbytes=4 * MIB,
        )(*arrived, gain, expert_in)

    sent = gate_up(1, bf16)
    sent, odd = lax.optimization_barrier((sent, odd))
    odd = permute(odd, "exp", 1)
    theirs = permute(sent, "ctx", 1)
    mine = gate_up(0, f32)

    size = expert_rows // chips
    chunk = call(
        chip_sum,
        [shape((size, width + LANES), bf16)] * chips,
        [VMEM] * 2,
        vmem=8,
    )(mine, theirs)
    def beside(ready, sent, step, exchange):
        ready, sent = lax.optimization_barrier((ready, sent))
        return (ready, *lax.optimization_barrier((step(ready), exchange(sent))))

    gathered = [permute(chunk[k], "ctx", 2 * k) for k in range(1, chips)]
    gathered, odd = lax.optimization_barrier((gathered, odd))
    active = call(
        functools.partial(activate, n_ctx * features),
        shape((size, hidden), bf16),
        [VMEM] * chips,
        vmem=8,
    )(chunk[0], *gathered)
    even = [
        (x.astype(f32) + odd[k * tokens : (k + 1) * tokens].astype(f32)).astype(bf16)
        for k, x in enumerate(even, 1)
    ]
    even = [permute(x, "exp", 2 * k) for k, x in enumerate(even, 1)]
    gathered, even = lax.optimization_barrier((over_chips(active), even))
    active_same = jnp.concatenate([active] + gathered, axis=0)
    active_other = permute(active_same, "ctx", 1)
    cost = dict(flops=2 * expert_rows * hidden * columns, nbytes=2 * MIB)
    made = call(
        expert_out_first,
        shape((expert_rows, columns), bf16),
        [VMEM] * 2,
        vmem=8,
        **cost,
    )(active_same, expert_out)
    produced = call(
        functools.partial(expert_out_second, n_exp),
        [shape((local * CAP, columns), bf16)] * n_exp,
        [VMEM] * 3,
        [pltpu.VMEM((local, expert_rows, columns), bf16)],
        vmem=8,
        **cost,
    )(active_other, expert_out, made)
    returned = [permute(produced[k], "exp", k) for k in reversed(range(1, n_exp))]
    mixed = own + odd[:tokens].astype(f32)
    for part in even:
        mixed = mixed + part.astype(f32)
    mixed = mixed.astype(bf16)
    expert_sum = call(
        combine,
        shape((tokens, columns), bf16),
        [VMEM] * (2 + n_exp),
        vmem=8,
    )(high, low, produced[0], *returned)
    return (mixed, expert_sum)


def solution(mesh):
    placed = (
        P("ctx", "exp"),
        P("ctx", None),
        P("ctx", None),
        P("ctx", None),
        P("ctx", None),
        P(),
        P("exp", "ctx"),
        P("exp", "ctx"),
        P("ctx"),
        P("exp", None),
        P("exp", None),
        P("exp", "ctx", None),
        P("exp", None, "ctx"),
    )
    return jax.shard_map(
        body,
        mesh=mesh,
        in_specs=placed,
        out_specs=(P("exp", "ctx"), P("exp", "ctx")),
        check_vma=False,
    )
```

```python
import functools
import math

import jax
import jax.numpy as jnp
from jax import lax
from jax.experimental import pallas as pl
from jax.experimental.pallas import tpu as pltpu
from jax.sharding import PartitionSpec as P

QHEADS = 64
KVH = 4
HEAD = 128
CAP = 16
LANES = 128

neg_large = -1e30
eps_norm = 1e-06
bf16 = jnp.bfloat16
f32 = jnp.float32
MIB = 1024 * 1024
ALL_VMEM = 63.5

VMEM = pl.BlockSpec(memory_space=pltpu.VMEM)
SMEM = pl.BlockSpec(memory_space=pltpu.SMEM)
HBM = pl.BlockSpec(memory_space=pltpu.HBM)


def call(kernel, out_shape, in_specs, scratch=(), vmem=16, flops=0, nbytes=0):
    many = isinstance(out_shape, (list, tuple))
    return pl.pallas_call(
        kernel,
        out_shape=out_shape,
        in_specs=in_specs,
        out_specs=[VMEM] * len(out_shape) if many else VMEM,
        scratch_shapes=list(scratch),
        compiler_params=pltpu.CompilerParams(vmem_limit_bytes=int(vmem * MIB)),
        cost_estimate=pl.CostEstimate(flops=flops, bytes_accessed=nbytes, transcendentals=0),
    )


def shape(dims, dtype):
    return jax.ShapeDtypeStruct(dims, dtype)


def dot(a, b):
    return lax.dot_general(a, b, (((1,), (0,)), ((), ())), preferred_element_type=f32)


def dot_t(a, b):
    return lax.dot_general(a, b, (((1,), (1,)), ((), ())), preferred_element_type=f32)


def turn(k, chips):
    return (chips - k) % chips


def rows_at(start, size, step):
    return pl.ds(pl.multiple_of(start, step), size)


def pick_kv(local_heads, ck, cv, bk, bv, out, sems):
    kv = lax.axis_index("exp") * local_heads // (QHEADS // KVH)
    cols = rows_at(kv * HEAD, HEAD, HEAD)
    cache, span = ck.shape[0], bk.shape[0]
    copies = []
    for n, (src, row, size, col) in enumerate(
        ((ck, 0, cache, 0), (cv, 0, cache, HEAD), (bk, cache, span, 0), (bv, cache, span, HEAD))
    ):
        copies.append(
            pltpu.make_async_copy(
                src.at[:, cols], out.at[pl.ds(row, size), pl.ds(col, HEAD)], sems.at[n]
            )
        )
    for copy in copies:
        copy.start()
    for copy in copies:
        copy.wait()


def segment_of(position, seg_starts):
    passed = jnp.full(position.shape, -1, jnp.int32)
    for n in range(seg_starts.shape[1]):
        passed = passed + jnp.where(seg_starts[:, n : n + 1] <= position, 1, 0)
    return passed


def mask_bias(seg_starts, other, span, cache, pieces):
    ctx = lax.axis_index("ctx")
    cache_total = cache * lax.axis_size("ctx")
    piece_rows = cache + span
    keys = pieces * piece_rows
    index = lax.broadcasted_iota(jnp.int32, (1, keys), 1)
    key_pos = jnp.zeros((1, keys), jnp.int32)
    for k in range(pieces):
        owner = jnp.bitwise_xor(ctx, 2 * turn(k, pieces) + other)
        off = index - k * piece_rows
        pos = jnp.where(off < cache, owner * cache + off, cache_total + owner * span + off - cache)
        key_pos = pos if k == 0 else jnp.where(off >= 0, pos, key_pos)
    key_seg = segment_of(key_pos, seg_starts)
    query_pos = cache_total + ctx * span + lax.broadcasted_iota(jnp.int32, (span, 1), 0)
    query_seg = segment_of(query_pos, seg_starts)
    last = seg_starts.shape[1] - 1
    seen = (key_pos <= query_pos) & (
        (key_seg == query_seg) | (key_seg == 0) | (query_seg == last)
    )
    return jnp.where(seen, 0.0, neg_large)


def prepare(n_exp, top, segments, span, cache, small, kv, bias_same, bias_other, kv_copy, rank, high, low):
    kv_copy[...] = kv[...]
    pieces = bias_same.shape[1] // (cache + span)
    seg_starts = small[2 * top : 2 * top + 1, :].astype(jnp.int32)[:, :segments]
    bias_same[...] = mask_bias(seg_starts, 0, span, cache, pieces)
    bias_other[...] = mask_bias(seg_starts, 1, span, cache, pieces)
    routes = small[:top, :].astype(jnp.int32)
    gates = small[top : 2 * top, :]
    flight, tokens = rank.shape
    local = flight // n_exp
    expert = lax.broadcasted_iota(jnp.int32, (flight, tokens), 0)
    member = jnp.zeros((flight, tokens), f32)
    weight = jnp.zeros((flight, tokens), f32)
    for k in range(routes.shape[0]):
        hit = routes[k : k + 1, :] == expert
        member = jnp.where(hit, 1.0, member)
        weight = weight + jnp.where(hit, gates[k : k + 1, :], 0.0)
    before = lax.broadcasted_iota(jnp.int32, (tokens, tokens), 0) < lax.broadcasted_iota(
        jnp.int32, (tokens, tokens), 1
    )
    count = dot(member.astype(bf16), jnp.where(before, 1.0, 0.0).astype(bf16))
    slots = jnp.where(member > 0.5, count, -1.0)
    rank[...] = slots
    exp = lax.axis_index("exp")
    slot = lax.broadcasted_iota(jnp.int32, (CAP, tokens), 0).astype(f32)
    tables = []
    for e in range(flight):
        tables.append(jnp.where(slots[e : e + 1, :] == slot, weight[e : e + 1, :], 0.0))
    per = local * CAP
    table = jnp.concatenate(tables, axis=0)
    upper = table.astype(bf16)
    lower = (table - upper.astype(f32)).astype(bf16)
    for d in range(n_exp):
        at = pl.ds(pl.multiple_of(jnp.bitwise_xor(exp, d) * per, per), per)
        high[at, :] = upper[d * per : (d + 1) * per, :]
        low[at, :] = lower[d * per : (d + 1) * per, :]


GROUP = 8


def attend(q, kv, bias, span, finish):
    scale = math.log2(math.e) / math.sqrt(HEAD)
    keys = kv.shape[0]
    group = min(GROUP, q.shape[0] // span)
    rows = group * span
    for g in range(q.shape[0] // rows):
        scores = dot_t(q[g * rows : (g + 1) * rows, :], kv[:, :HEAD])
        scores = (scores.reshape(group, span, keys) + bias[...][None]).reshape(rows, keys)
        top = jnp.max(scores, axis=1, keepdims=True)
        probs = jnp.exp2((scores - top) * scale)
        total = jnp.sum(probs, axis=1, keepdims=True)
        out = dot(probs.astype(bf16), kv[:, HEAD:])
        finish(g, rows, group, out, top, total)


def attend_first(span, q, kv, bias, o_out, m_out, l_out):
    def finish(g, rows, group, out, top, total):
        at = pl.ds(g * rows, rows)
        o_out[at, :] = out
        m_out[at, :] = jnp.broadcast_to(top, (rows, LANES))
        l_out[at, :] = jnp.broadcast_to(total, (rows, LANES))

    attend(q, kv, bias, span, finish)


def attend_second(span, q, kv, bias, o_in, m_in, l_in, *results):
    scale = math.log2(math.e) / math.sqrt(HEAD)
    half = results[0].shape[1] // HEAD

    def finish(g, rows, group, out, top, total):
        at = pl.ds(g * rows, rows)
        first = m_in[at, :]
        both = jnp.maximum(first, top)
        w_first = jnp.exp2((first - both) * scale)
        w_second = jnp.exp2((top - both) * scale)
        norm = l_in[at, :] * w_first + total * w_second
        merged = ((o_in[at, :] * w_first + out * w_second) / norm).astype(bf16)
        for h in range(group):
            head = g * group + h
            result = results[head // half]
            col = head % half * HEAD
            result[:, col : col + HEAD] = merged[h * span : (h + 1) * span, :]

    attend(q, kv, bias, span, finish)


def project_first(heads_out, weight, out):
    out[...] = dot(heads_out[...], weight[...])


def project_second(n_exp, span, heads_out, weight, first, residual, ranks, *refs):
    own_out, odd_out = refs[:2]
    even_outs = refs[2 : n_exp // 2 + 1]
    pick_outs, second = refs[n_exp // 2 + 1 : -1], refs[-1]
    second[...] = dot(heads_out[...], weight[...])
    ctx, exp = lax.axis_index("ctx"), lax.axis_index("exp")
    core, chip = ctx % 2, ctx // 2
    tokens, columns = residual.shape
    half = columns // 2
    flight = ranks.shape[0] // n_exp
    local = flight // n_exp
    slot = lax.broadcasted_iota(jnp.int32, (CAP, tokens), 0).astype(f32)
    held, step = [0], n_exp // 2
    while step:
        held, step = held + [k ^ step for k in held], step // 2
    for k in range(n_exp):
        block = jnp.bitwise_xor(exp, k)
        here = rows_at(jnp.bitwise_xor(chip, block) * span, span, span)
        same, other = first[here, :], second[here, :]
        part = jnp.concatenate(
            [jnp.where(core == 0, same, other), jnp.where(core == 0, other, same)], axis=0
        )
        if k == 0:
            part = part + residual[...].astype(f32)
            own_out[...] = part
        narrow = part.astype(bf16)
        if k % 2:
            odd_out[k // 2 * tokens : (k // 2 + 1) * tokens, :] = narrow
        elif k:
            even_outs[k // 2 - 1][...] = narrow
        table = []
        for d in range(n_exp):
            for j in range(local):
                row = held.index(k) * flight + jnp.bitwise_xor(exp, d) * local + j
                table.append(jnp.where(ranks[pl.ds(row, 1), :] == slot, 1.0, 0.0))
        rows = dot(jnp.concatenate(table, axis=0).astype(bf16), narrow).astype(bf16)
        for d in range(n_exp):
            for j in range(local):
                at = rows_at(j * n_exp * CAP + block * CAP, CAP, CAP)
                value = rows[(d * local + j) * CAP : (d * local + j + 1) * CAP, :]
                if d == 0:
                    pick_outs[d][at, :] = value
                else:
                    pick_outs[2 * d - 1][at, :] = value[:, :half]
                    pick_outs[2 * d][at, :] = value[:, half:]


def split_square(square):
    lane = lax.broadcasted_iota(jnp.int32, (square.shape[0], LANES), 1)
    high = square.astype(bf16).astype(f32)
    return jnp.where(lane == 0, high, jnp.where(lane == 1, square - high, 0.0))


def expert_in_kernel(n_arrived, direct, other, *refs):
    arrived = refs[:n_arrived]
    gain, weight, out = refs[n_arrived:]
    expert = jnp.bitwise_xor(lax.axis_index("ctx") % 2, other)
    rows = out.shape[0]
    width = weight.shape[2]
    at = rows_at(expert * rows, rows, rows)
    total = arrived[0][at, :].astype(f32)
    halves = [0.0, 0.0]
    for n, ref in enumerate(arrived[1:]):
        halves[n >= direct] = halves[n >= direct] + ref[at, :].astype(f32)
    mixed = (total + jnp.concatenate(halves, axis=1)).astype(bf16).astype(f32)
    out[:, width:] = split_square(jnp.sum(mixed * mixed, axis=1, keepdims=True)).astype(out.dtype)
    scaled = (mixed * gain[...]).astype(bf16)
    step = width // 6
    for n in range(0, width, step):
        out[:, n : n + step] = dot(scaled, weight[expert, :, n : n + step]).astype(out.dtype)


def chip_sum(mine, theirs, *outs):
    chip = lax.axis_index("ctx") // 2
    width = mine.shape[1] - LANES
    size = outs[0].shape[0]
    for k, out in enumerate(outs):
        at = rows_at(jnp.bitwise_xor(chip, k) * size, size, size)
        total = mine[at, :] + theirs[at, :].astype(f32)
        out[:, :width] = total[:, :width].astype(bf16)
        out[:, width:] = split_square(
            jnp.sum(total[:, width:], axis=1, keepdims=True)
        ).astype(bf16)


def activate(features, *refs):
    out = refs[-1]
    total = refs[0][...].astype(f32)
    for ref in refs[1:-1]:
        total = total + ref[...].astype(f32)
    hidden = out.shape[1]
    square = jnp.sum(total[:, 2 * hidden :], axis=1, keepdims=True)
    inverse = lax.rsqrt(square / features + eps_norm)
    gate = total[:, :hidden] * inverse
    up = total[:, hidden : 2 * hidden] * inverse
    out[...] = (gate / (1.0 + jnp.exp(-gate)) * up).astype(bf16)


def expert_out_first(active, weight, out):
    out[...] = dot(active[...], weight[lax.axis_index("ctx") % 2]).astype(bf16)


def expert_out_second(n_exp, active, weight, first, *refs):
    outs, whole = refs[:n_exp], refs[n_exp]
    ctx, exp = lax.axis_index("ctx"), lax.axis_index("exp")
    core, chip = ctx % 2, ctx // 2
    chips = lax.axis_size("ctx") // 2
    size = active.shape[0] // chips
    second = dot(active[...], weight[1 - core]).astype(bf16)
    for k in range(chips):
        at = rows_at(jnp.bitwise_xor(chip, turn(k, chips)) * size, size, size)
        here = slice(k * size, (k + 1) * size)
        whole[core, at, :] = first[here, :]
        whole[1 - core, at, :] = second[here, :]
    for k in range(n_exp):
        at = rows_at(jnp.bitwise_xor(exp, k) * CAP, CAP, CAP)
        for j in range(whole.shape[0]):
            outs[k][j * CAP : (j + 1) * CAP, :] = whole[j, at, :]


def combine(high, low, *refs):
    out = refs[-1]
    rows = jnp.concatenate([ref[...] for ref in (refs[0], *refs[2:-1], refs[1])], axis=0)
    dims = (((0,), (0,)), ((), ()))
    out[...] = (
        lax.dot_general(high[...], rows, dims, preferred_element_type=f32)
        + lax.dot_general(low[...], rows, dims, preferred_element_type=f32)
    ).astype(bf16)


def permute(x, axis, k):
    n = lax.axis_size(axis)
    return lax.ppermute(x, axis, [(i, i ^ k) for i in range(n)])


def gather_halves(halves, chips):
    low, high = halves
    if chips != 4:
        return [[low, high]] + [
            [permute(low, "ctx", 2 * k), permute(high, "ctx", 2 * k)] for k in range(1, chips)
        ]
    x_low, y_high = permute(low, "ctx", 2), permute(high, "ctx", 4)
    x_high, y_low = permute(high, "ctx", 2), permute(low, "ctx", 4)
    far_low, far_high = permute(x_low, "ctx", 4), permute(y_high, "ctx", 2)
    return [[low, high], [x_low, x_high], [y_low, y_high], [far_low, far_high]]


def body(
    queries,
    cache_keys,
    cache_values,
    block_keys,
    block_values,
    seg_starts,
    out_weight,
    residual,
    norm_gain,
    routes,
    gate_values,
    expert_in,
    expert_out,
):
    n_ctx, n_exp = lax.axis_size("ctx"), lax.axis_size("exp")
    chips = n_ctx // 2
    span = queries.shape[0]
    heads = queries.shape[1] // HEAD
    cache = cache_keys.shape[0]
    tokens = routes.shape[0]
    local, features, width = expert_in.shape
    hidden = width // 2
    columns = out_weight.shape[1]
    flight = n_exp * local

    def over_chips(x):
        return [permute(x, "ctx", 2 * k) for k in reversed(range(1, chips))]

    def over_exp(xs):
        return [permute(x, "exp", k) for k, x in zip(range(1, n_exp), xs)]

    local_kv = call(
        functools.partial(pick_kv, heads),
        shape((cache + span, 2 * HEAD), bf16),
        [HBM] * 4,
        [pltpu.SemaphoreType.DMA((4,))],
        vmem=ALL_VMEM,
    )(cache_keys, cache_values, block_keys, block_values)
    kv_moved = over_chips(local_kv)

    rows, keys = heads * span, chips * (cache + span)
    top, segments = routes.shape[1], seg_starts.shape[0]
    small = jnp.concatenate(
        [
            routes.T.astype(f32),
            gate_values.T,
            jnp.pad(seg_starts.astype(f32)[None], ((0, 0), (0, tokens - segments))),
        ],
        axis=0,
    )
    bias_same, bias_other, own_kv, rank, high, low = call(
        functools.partial(prepare, n_exp, top, segments, span, cache),
        [shape((span, keys), f32)] * 2
        + [shape(local_kv.shape, bf16)]
        + [shape((flight, tokens), f32)]
        + [shape((flight * CAP, tokens), bf16)] * 2,
        [VMEM] * 2,
        vmem=8,
        nbytes=2 * MIB,
    )(small, local_kv)
    stacked = queries.reshape(span, heads, HEAD).transpose(1, 0, 2).reshape(rows, HEAD)
    kv_moved, stacked, bias_same, bias_other, own_kv, rank = lax.optimization_barrier(
        (kv_moved, stacked, bias_same, bias_other, own_kv, rank)
    )
    kv_same = jnp.concatenate([own_kv] + kv_moved, axis=0)
    kv_other = permute(kv_same, "ctx", 1)

    cost = dict(flops=4 * rows * keys * HEAD, nbytes=4 * MIB)
    stats = call(
        functools.partial(attend_first, span),
        [shape((rows, HEAD), f32), shape((rows, LANES), f32), shape((rows, LANES), f32)],
        [VMEM] * 3,
        vmem=24,
        **cost,
    )(stacked, kv_same, bias_same)
    halves = call(
        functools.partial(attend_second, span),
        [shape((span, rows // span * HEAD // 2), bf16)] * 2,
        [VMEM] * 6,
        vmem=24,
        **cost,
    )(stacked, kv_other, bias_other, *stats)

    halves, ranks = lax.optimization_barrier((halves, rank))
    step = n_exp // 2
    while step:
        ranks = jnp.concatenate([ranks, permute(ranks, "exp", step)], axis=0)
        step //= 2
    pieces = gather_halves(halves, chips)
    pieces, ranks = lax.optimization_barrier((pieces, ranks))
    heads_same = jnp.concatenate([jnp.concatenate(pair, axis=1) for pair in pieces], axis=0)
    heads_other = permute(heads_same, "ctx", 1)
    cost = dict(
        flops=2 * heads_same.shape[0] * heads_same.shape[1] * columns, nbytes=4 * MIB
    )
    first = call(
        project_first,
        shape((heads_same.shape[0], columns), f32),
        [VMEM] * 2,
        vmem=16,
        **cost,
    )(heads_same, out_weight)
    per_exp = local * n_exp * CAP
    outs = call(
        functools.partial(project_second, n_exp, span),
        [shape((tokens, columns), f32)]
        + [shape((n_exp // 2 * tokens, columns), bf16)]
        + [shape((tokens, columns), bf16)] * (n_exp // 2 - 1)
        + [shape((per_exp, columns), bf16)]
        + [shape((per_exp, columns // 2), bf16)] * (2 * n_exp - 2),
        [VMEM] * 5,
        [pltpu.VMEM(first.shape, f32)],
        vmem=24,
        **cost,
    )(heads_other, out_weight, first, residual, ranks)
    own, odd, even, picks = outs[0], outs[1], outs[2 : n_exp // 2 + 1], outs[n_exp // 2 + 1 :]
    left, right = picks[3::2], picks[4::2]
    passed = [permute(right[2 * k - 1], "exp", 1) for k in range(1, n_exp // 2)]
    direct = [permute(x, "exp", k) for k, x in enumerate(left, 2)][::-1]
    direct.append(permute(picks[1], "exp", 1))
    arrived = [picks[0]] + direct + [permute(picks[2], "exp", 1)]
    for k, got in enumerate(passed, 1):
        pair = (right[2 * k - 2].astype(f32) + got.astype(f32)).astype(bf16)
        arrived.append(permute(pair, "exp", 2 * k))
    gain = norm_gain.reshape(1, features)
    expert_rows = n_exp * CAP

    def gate_up(other, dtype):
        return call(
            functools.partial(expert_in_kernel, len(arrived), len(direct), other),
            shape((expert_rows, width + LANES), dtype),
            [VMEM] * (len(arrived) + 2),
            vmem=16,
            flops=2 * expert_rows * features * width,
            nbytes=4 * MIB,
        )(*arrived, gain, expert_in)

    sent = gate_up(1, bf16)
    sent, odd = lax.optimization_barrier((sent, odd))
    odd = permute(odd, "exp", 1)
    theirs = permute(sent, "ctx", 1)
    mine = gate_up(0, f32)

    size = expert_rows // chips
    chunk = call(
        chip_sum,
        [shape((size, width + LANES), bf16)] * chips,
        [VMEM] * 2,
        vmem=8,
    )(mine, theirs)
    def beside(ready, sent, step, exchange):
        ready, sent = lax.optimization_barrier((ready, sent))
        return (ready, *lax.optimization_barrier((step(ready), exchange(sent))))

    gathered = [permute(chunk[k], "ctx", 2 * k) for k in range(1, chips)]
    gathered, odd = lax.optimization_barrier((gathered, odd))
    active = call(
        functools.partial(activate, n_ctx * features),
        shape((size, hidden), bf16),
        [VMEM] * chips,
        vmem=8,
    )(chunk[0], *gathered)
    even = [
        (x.astype(f32) + odd[k * tokens : (k + 1) * tokens].astype(f32)).astype(bf16)
        for k, x in enumerate(even, 1)
    ]
    even = [permute(x, "exp", 2 * k) for k, x in enumerate(even, 1)]
    gathered, even = lax.optimization_barrier((over_chips(active), even))
    active_same = jnp.concatenate([active] + gathered, axis=0)
    active_other = permute(active_same, "ctx", 1)
    cost = dict(flops=2 * expert_rows * hidden * columns, nbytes=2 * MIB)
    made = call(
        expert_out_first,
        shape((expert_rows, columns), bf16),
        [VMEM] * 2,
        vmem=8,
        **cost,
    )(active_same, expert_out)
    produced = call(
        functools.partial(expert_out_second, n_exp),
        [shape((local * CAP, columns), bf16)] * n_exp,
        [VMEM] * 3,
        [pltpu.VMEM((local, expert_rows, columns), bf16)],
        vmem=8,
        **cost,
    )(active_other, expert_out, made)
    returned = [permute(produced[k], "exp", k) for k in (n_exp - 1, *range(1, n_exp - 1))]
    mixed = own + odd[:tokens].astype(f32)
    for part in even:
        mixed = mixed + part.astype(f32)
    mixed = mixed.astype(bf16)
    expert_sum = call(
        combine,
        shape((tokens, columns), bf16),
        [VMEM] * (2 + n_exp),
        vmem=8,
    )(high, low, produced[0], *returned)
    return (mixed, expert_sum)


def solution(mesh):
    placed = (
        P("ctx", "exp"),
        P("ctx", None),
        P("ctx", None),
        P("ctx", None),
        P("ctx", None),
        P(),
        P("exp", "ctx"),
        P("exp", "ctx"),
        P("ctx"),
        P("exp", None),
        P("exp", None),
        P("exp", "ctx", None),
        P("exp", None, "ctx"),
    )
    return jax.shard_map(
        body,
        mesh=mesh,
        in_specs=placed,
        out_specs=(P("exp", "ctx"), P("exp", "ctx")),
        check_vma=False,
    )
```
